512 devices in a mesh: gz: 8 (over z_lo), xy: 64 (over y, z_hi, x, core).
Axes of the slice: x: 4, y: 4, z: 16 (z_hi: 2, z_lo: 8; z = z_hi * 8 + z_lo), core: 2. Of those that a mesh axis runs over, the one named last changes fastest.
Arguments:
- populations: float32 [19, 512, 64, 128], P(None, 'xy', 'gz'), may hold values from 0.02 to 0.08
- colour: float32 [512, 64, 128], P('xy', 'gz'), may hold values from -1 to 1
- conformation: float32 [6, 512, 64, 128], P(None, 'xy', 'gz'), may hold values from -1.5 to 1.5
- labels: int32 [512, 64, 128], P('xy', 'gz'), may hold values from 0 to 2
- pop_cotangent: float32 [19, 512, 64, 128], P(None, 'xy', 'gz'), may hold values from -6 to 6
- conf_cotangent: float32 [6, 512, 64, 128], P(None, 'xy', 'gz'), may hold values from -6 to 6
Outputs:
- adj_populations: float32 [19, 512, 64, 128], P(None, 'xy', 'gz')
- adj_colour: float32 [512, 64, 128], P('xy', 'gz')
- adj_conformation: float32 [6, 512, 64, 128], P(None, 'xy', 'gz')
The draws below stay inside these ranges and needn't reach their ends.
Inputs may be any that keep to these rules, and one draw needn't show every extreme that they name: `labels`: 0 marks a fluid cell, 1 a solid cell, 2 an inlet cell.
All inputs are finite; a program needn't handle non-finite values.
Results may differ from the reference program's by a relative error of at most 0.0003.
Values sent between devices are 32-bit elements; how exact they have to be, the bound alone decides.
A program may use at most 64 MiB of HBM per device.

```python
from functools import partial
import jax
import jax.numpy as jnp
from jax import lax

NY = 128
NX = 512
NZ = 64


def with_ends(values, rng, least, largest):
    longest = values.shape.index(max(values.shape))
    spots = []
    for shift in (0, 1):
        where = [jax.random.randint(jax.random.fold_in(rng, axis), (), 0, length) for axis, length in enumerate(values.shape)]
        where[longest] = (where[longest] + shift) % values.shape[longest]
        spots.append(tuple(where))
    return values.at[spots[0]].set(least).at[spots[1]].set(largest)


def shard_levels(rng, dims, shards, least, high):
    def one(position, parts):
        steps = jax.random.uniform(jax.random.fold_in(jax.random.fold_in(rng, 6), position), (parts,), jnp.float32, least / len(shards), high / len(shards))
        return jnp.repeat(jnp.exp(steps), dims[position] // parts).reshape((-1,) + (1,) * (len(dims) - position - 1))

    factor_of = one(*shards[0])
    for cut in shards[1:]:
        factor_of = factor_of * one(*cut)
    return factor_of


def normal_values(stream_key, shape, width, most, split=(), kind=jnp.bfloat16):
    values = width * jax.random.normal(stream_key, shape, jnp.float32)
    if split:
        values = values * shard_levels(stream_key, shape, split, -0.22, 0.18)
    return jnp.clip(values, -most, most).astype(kind)


def setup_inputs(seed: int = 0) -> dict:
    streams_of = jax.random.split(jax.random.key(seed), 7)
    populations = jnp.clip(0.02 + 0.06 * jax.random.uniform(streams_of[0], (19, NX, NZ, NY), jnp.float32) ** shard_levels(streams_of[0], (19, NX, NZ, NY), ((1, 64), (2, 8)), -0.2, 0.2), 0.02, 0.08)
    colour = jnp.clip(jax.random.uniform(streams_of[1], (NX, NZ, NY), jnp.float32, -1.0, 1.0) * shard_levels(streams_of[1], (NX, NZ, NY), ((0, 64), (1, 8)), -0.4, 0.0), -1.0, 1.0)
    conformation = normal_values(streams_of[2], (6, NX, NZ, NY), 0.3, 1.5, ((1, 64), (2, 8)), jnp.float32)
    labels = with_ends(jax.random.randint(streams_of[3], (NX, NZ, NY), 0, 3), jax.random.fold_in(streams_of[3], 1), 0, 2).astype(jnp.int32)
    pop_cotangent = normal_values(streams_of[4], (19, NX, NZ, NY), 1.0, 6.0, ((1, 64), (2, 8)), jnp.float32)
    conf_cotangent = normal_values(streams_of[5], (6, NX, NZ, NY), 1.0, 6.0, ((1, 64), (2, 8)), jnp.float32)
    return dict(populations=populations, colour=colour, conformation=conformation, labels=labels, pop_cotangent=pop_cotangent, conf_cotangent=conf_cotangent)


velocities = ((0, 0, 0), (1, 0, 0), (-1, 0, 0), (0, 1, 0), (0, -1, 0), (0, 0, 1), (0, 0, -1), (1, 1, 0), (-1, -1, 0), (1, -1, 0), (-1, 1, 0), (1, 0, 1), (-1, 0, -1), (1, 0, -1), (-1, 0, 1), (0, 1, 1), (0, -1, -1), (0, 1, -1), (0, -1, 1))
opposite = (0, 2, 1, 4, 3, 6, 5, 8, 7, 10, 9, 12, 11, 14, 13, 16, 15, 18, 17)
lattice_weights = (1.0 / 3.0,) + (1.0 / 18.0,) * 6 + (1.0 / 36.0,) * 12
component_slot = {(0, 0): 0, (1, 1): 1, (2, 2): 2, (0, 1): 3, (1, 0): 3, (0, 2): 4, (2, 0): 4, (1, 2): 5, (2, 1): 5}
relax_time = 0.8
time_step = 0.5
relax_rate = 0.1
smooth_speed = 0.02
inlet_speed = 0.05

def axis_derivative(padded, which):
    if which == 0:
        return 0.5 * (padded[:, 2:, 1:-1, :] - padded[:, :-2, 1:-1, :])
    if which == 2:
        return 0.5 * (padded[:, 1:-1, 2:, :] - padded[:, 1:-1, :-2, :])
    middle = padded[:, 1:-1, 1:-1, :]
    return 0.5 * (jnp.roll(middle, -1, axis=3) - jnp.roll(middle, 1, axis=3))

def axis_curvature(padded, which):
    middle = padded[:, 1:-1, 1:-1, :]
    if which == 0:
        return padded[:, 2:, 1:-1, :] + padded[:, :-2, 1:-1, :] - 2.0 * middle
    if which == 2:
        return padded[:, 1:-1, 2:, :] + padded[:, 1:-1, :-2, :] - 2.0 * middle
    return jnp.roll(middle, -1, axis=3) + jnp.roll(middle, 1, axis=3) - 2.0 * middle

def equilibrium(density, flow):
    square = flow[0] * flow[0] + flow[1] * flow[1] + flow[2] * flow[2]
    result = []
    for direction in range(19):
        vector = velocities[direction]
        along = vector[0] * flow[0] + vector[1] * flow[1] + vector[2] * flow[2]
        result.append(lattice_weights[direction] * density * (1.0 + 3.0 * along + 4.5 * along * along - 1.5 * square))
    return jnp.stack(result)

def local_step(populations, labels, colour_padded, conform_padded):
    density = lax.optimization_barrier(jnp.sum(populations, axis=0))
    velocity = []
    for which in range(3):
        moment = jnp.zeros_like(density)
        for direction in range(19):
            if velocities[direction][which] != 0:
                moment = moment + velocities[direction][which] * populations[direction]
        velocity.append(moment / density)
    phase = colour_padded[0, 1:-1, 1:-1, :]
    stress = []
    for slot_a in range(3):
        for slot_b in range(3):
            if slot_b >= slot_a:
                total = conform_padded[component_slot[slot_a, slot_b]]
                for middle in range(3):
                    total = total + 0.5 * conform_padded[component_slot[slot_a, middle]] * conform_padded[component_slot[middle, slot_b]]
                stress.append(total)
    stress = jnp.stack(stress)
    stress_slot = {(0, 0): 0, (0, 1): 1, (0, 2): 2, (1, 1): 3, (1, 2): 4, (2, 2): 5}
    force = []
    for slot_a in range(3):
        total = (1.0 - phase * phase) * axis_derivative(colour_padded, slot_a)[0]
        for slot_b in range(3):
            index = stress_slot[min(slot_a, slot_b), max(slot_a, slot_b)]
            total = total + axis_derivative(stress[index:index + 1], slot_b)[0]
        force.append(total)
    shifted = [velocity[k] + force[k] / (2.0 * density) for k in range(3)]
    balance = equilibrium(density, shifted)
    shift_force = shifted[0] * force[0] + shifted[1] * force[1] + shifted[2] * force[2]
    factor = 1.0 - 0.5 / relax_time
    sources = []
    for direction in range(19):
        vector = velocities[direction]
        along_force = vector[0] * force[0] + vector[1] * force[1] + vector[2] * force[2]
        along_flow = vector[0] * shifted[0] + vector[1] * shifted[1] + vector[2] * shifted[2]
        sources.append(factor * lattice_weights[direction] * (3.0 * (along_force - shift_force) + 9.0 * along_flow * along_force))
    collided = populations - (populations - balance) / relax_time + jnp.stack(sources)
    zeros_field = jnp.zeros_like(density)
    inlet = equilibrium(density, [zeros_field, zeros_field, zeros_field + inlet_speed])
    bounced = jnp.stack([populations[k] for k in opposite])
    marks = labels[None]
    post = jnp.where(marks == 1, bounced, jnp.where(marks == 2, inlet, collided))
    conform_centre = conform_padded[:, 1:-1, 1:-1, :]
    advection = jnp.zeros_like(conform_centre)
    for which in range(3):
        speed = jnp.sqrt(velocity[which] * velocity[which] + smooth_speed * smooth_speed)
        advection = advection + velocity[which][None] * axis_derivative(conform_padded, which) - 0.5 * speed[None] * axis_curvature(conform_padded, which)
    conform_next = conform_centre - time_step * advection - relax_rate * conform_centre
    return (post, conform_next)

def wrap_pad(field):
    return jnp.pad(field, ((0, 0), (1, 1), (1, 1), (0, 0)), mode='wrap')

def forward(populations, colour, conformation, labels):
    post, conform_next = local_step(populations, labels, wrap_pad(colour[None]), wrap_pad(conformation))
    moved = jnp.stack([jnp.roll(post[k], (velocities[k][0], velocities[k][2], velocities[k][1]), axis=(0, 1, 2)) for k in range(19)])
    return (moved, conform_next)

def reference(populations, colour, conformation, labels, pop_cotangent, conf_cotangent):
    outputs, pullback = jax.vjp(partial(forward, labels=labels), populations, colour, conformation)
    adj_populations, adj_colour, adj_conformation = pullback((pop_cotangent, conf_cotangent))
    return (adj_populations, adj_colour, adj_conformation)
```

```python
import functools

import jax
import jax.numpy as jnp
from jax import lax
from jax.experimental import pallas as pl
from jax.experimental.pallas import tpu as pltpu
from jax.sharding import PartitionSpec as P

MESH = pl.DeviceIdType.MESH
F32 = jnp.float32

velocities = (
    (0, 0, 0),
    (1, 0, 0),
    (-1, 0, 0),
    (0, 1, 0),
    (0, -1, 0),
    (0, 0, 1),
    (0, 0, -1),
    (1, 1, 0),
    (-1, -1, 0),
    (1, -1, 0),
    (-1, 1, 0),
    (1, 0, 1),
    (-1, 0, -1),
    (1, 0, -1),
    (-1, 0, 1),
    (0, 1, 1),
    (0, -1, -1),
    (0, 1, -1),
    (0, -1, 1),
)
opposite = (0, 2, 1, 4, 3, 6, 5, 8, 7, 10, 9, 12, 11, 14, 13, 16, 15, 18, 17)
slot = {(0, 0): 0, (1, 1): 1, (2, 2): 2, (0, 1): 3, (1, 0): 3, (0, 2): 4, (2, 0): 4, (1, 2): 5, (2, 1): 5}
pairs = ((0, 0), (1, 1), (2, 2), (0, 1), (0, 2), (1, 2))
inlet_speed = 0.05
smooth_square = 0.02 * 0.02
F_CONF, F_COL, F_COT, F_UPW, F_G, F_K, F_W, F_R, F_CHI, F_ALL = 0, 6, 7, 12, 18, 21, 27, 30, 31, 32
C_OWN, C_Z, C_ZIN, C_X, C_XIN, C_CONF, C_COL, C_ALL = 0, 1, 4, 5, 8, 9, 15, 16


def dirs_where(axis, sign):
    return tuple(i for i in range(19) if velocities[i][axis] == sign)


def corner_dir(sx, sz):
    return next(i for i in range(19) if velocities[i][0] == sx and velocities[i][2] == sz)


def edge_dirs(axis, sign, other):
    return tuple(i for i in range(19) if velocities[i][axis] == sign and velocities[i][other] == 0)


def stress_of(conf):
    out = []
    for a, b in pairs:
        dot = conf[slot[a, 0]] * conf[slot[0, b]]
        for m in (1, 2):
            dot = dot + conf[slot[a, m]] * conf[slot[m, b]]
        out.append(conf[slot[a, b]] + 0.5 * dot)
    return out


def total(terms):
    result = None
    for sign, value in terms:
        if result is None:
            result = value if sign > 0 else -value
        else:
            result = result + value if sign > 0 else result - value
    return result


def moments(values):
    def weighted(sign_of):
        axial = total([(sign_of(velocities[i]), v) for i, v in values if 0 < i < 7 and sign_of(velocities[i])])
        edge = total([(sign_of(velocities[i]), v) for i, v in values if i >= 7 and sign_of(velocities[i])])
        if axial is None and edge is None:
            return None
        if axial is None:
            return edge * (1.0 / 36.0)
        if edge is None:
            return axial * (1.0 / 18.0)
        return axial * (1.0 / 18.0) + edge * (1.0 / 36.0)

    zeroth = weighted(lambda c: 1)
    rest = [v for i, v in values if i == 0]
    if rest:
        zeroth = zeroth + rest[0] * (1.0 / 3.0)
    first = [weighted(lambda c, a=a: c[a]) for a in range(3)]
    second = [weighted(lambda c, a=a, b=b: c[a] * c[b]) for a, b in pairs]
    return zeroth, first, second


def tensor_of(zeroth, second):
    out = []
    for k in range(6):
        value = None if second[k] is None else 9.0 * second[k]
        if k < 3:
            value = -3.0 * zeroth if value is None else value - 3.0 * zeroth
        out.append(value)
    return out


def apply(tensor, vector):
    out = []
    for a in range(3):
        value = None
        for b in range(3):
            if tensor[slot[a, b]] is not None:
                term = tensor[slot[a, b]] * vector[b]
                value = term if value is None else value + term
        out.append(value)
    return out


def plus(a, b):
    return a if b is None else b if a is None else a + b


def in_y(value, by):
    return value if by == 0 else pltpu.roll(value, (-by) % 128, 1)


def rows_of(row):
    return jnp.broadcast_to(row, (8, 128))


def kernel(
    pop, col, conf, lab, cot, con,
    o_pop, o_col, o_conf,
    v_pop, v_col, v_conf, v_lab, v_cot, v_con,
    snd, rcv, csnd, crcv,
    x_cot, x_conf, x_col, x_str, x_h, x_up, x_down, z_cot, z_str, z_h, v_u, v_ri,
    in_sem, f_send, f_recv, c_send, c_recv,
):
    loads = [
        pltpu.make_async_copy(src, dst, in_sem.at[k])
        for k, (src, dst) in enumerate(
            [(conf, v_conf), (col, v_col), (cot, v_cot), (pop, v_pop), (lab, v_lab), (con, v_con)]
        )
    ]
    for copy in loads:
        copy.start()
    nz, nx = lax.axis_size("gz"), lax.axis_size("xy")
    z, x = lax.axis_index("gz"), lax.axis_index("xy")
    z_of = {-1: lax.rem(z + nz - 1, nz), 0: z, 1: lax.rem(z + 1, nz)}
    x_of = {-1: lax.rem(x + nx - 1, nx), 0: x, 1: lax.rem(x + 1, nx)}
    faces = ((0, -1), (0, 1), (2, -1), (2, 1))
    face_device = [(z_of[0], x_of[-1]), (z_of[0], x_of[1]), (z_of[-1], x_of[0]), (z_of[1], x_of[0])]
    corners = ((-1, -1), (-1, 1), (1, -1), (1, 1))
    corner_device = [(z_of[cz], x_of[cx]) for cx, cz in corners]
    barrier = pltpu.get_barrier_semaphore()
    for device in face_device + corner_device:
        pl.semaphore_signal(barrier, inc=1, device_id=device, device_id_type=MESH)
    for copy in loads:
        copy.wait()

    lane = lax.broadcasted_iota(jnp.int32, (8, 128), 0)
    first, last = lane == 0, lane == 7

    def shift(value, by, low=None, high=None):
        if by == 0:
            return value
        rolled = pltpu.roll(value, 7 if by > 0 else 1, 0)
        fill = high if by > 0 else low
        fill = 0.0 if fill is None else fill
        return jnp.where(last if by > 0 else first, fill, rolled)

    def plane(ref, axis, at, k=None):
        rows = pl.ds(8 * at, 8) if axis == 0 else pl.ds(at, 8, stride=8)
        return ref[rows, :] if k is None else ref[k, rows, :]

    def flow_of(load):
        f = [load(i) for i in range(19)]
        rho = f[0]
        for i in range(1, 19):
            rho = rho + f[i]
        inverse = 1.0 / rho
        u = [total([(velocities[i][a], f[i]) for i in range(19) if velocities[i][a]]) * inverse for a in range(3)]
        return rho, inverse, u

    def make_face(index):
        axis, side = faces[index]
        across = 2 - axis
        edge = 7 if side > 0 else 0
        inner = edge - side
        p_edge = [plane(v_conf, axis, edge, k) for k in range(6)]
        p_inner = [plane(v_conf, axis, inner, k) for k in range(6)]
        s_edge, s_inner = stress_of(p_edge), stress_of(p_inner)
        c_edge, c_inner = plane(v_col, axis, edge), plane(v_col, axis, inner)
        _, inverse, u = flow_of(lambda i: plane(v_pop, axis, edge, i))
        ratio = 0.6875 * inverse
        fluid = jnp.where(plane(v_lab, axis, edge) == 0, 1.0, 0.0)
        out = snd.at[index]
        for k in range(6):
            out[F_CONF + k] = p_edge[k]
        out[F_COL] = c_edge
        for j, i in enumerate(dirs_where(axis, -side)):
            out[F_COT + j] = plane(v_cot, axis, edge, i)
        speed = u[axis] * u[axis] + smooth_square
        speed = speed * lax.rsqrt(speed)
        upwind = 0.25 * (speed - side * u[axis])
        for k in range(6):
            out[F_UPW + k] = upwind * plane(v_con, axis, edge, k)
        values = []
        for i in range(19):
            c = velocities[i]
            if c[axis] == side:
                continue
            got = plane(v_cot, axis, edge if c[axis] == 0 else inner, i)
            values.append((i, in_y(shift(got, c[across]), c[1])))
        zeroth, one, two = moments(values)
        tensor = tensor_of(zeroth, two)
        mobility = 1.0 - c_edge * c_edge
        force = []
        for a in range(3):
            k = slot[a, 1]
            value = 0.5 * (in_y(s_edge[k], 1) - in_y(s_edge[k], -1))
            k = slot[a, across]
            value = value + 0.5 * (shift(s_edge[k], 1) - shift(s_edge[k], -1))
            value = value - (0.5 * side) * s_inner[slot[a, axis]]
            if a == 1:
                slope = 0.5 * (in_y(c_edge, 1) - in_y(c_edge, -1))
            elif a == across:
                slope = 0.5 * (shift(c_edge, 1) - shift(c_edge, -1))
            else:
                slope = (-0.5 * side) * c_inner
            force.append(value + mobility * slope)
        for a in range(3):
            out[F_G + a] = one[a]
            out[F_W + a] = u[a] + ratio * force[a]
        for k in range(6):
            out[F_K + k] = tensor[k]
        out[F_R] = ratio
        out[F_CHI] = fluid

    def make_corner(index):
        cx, cz = corners[index]
        ex, ez = (7 if cx > 0 else 0), (7 if cz > 0 else 0)
        here = pl.ds(8 * ex + ez, 1)
        in_x, in_z = pl.ds(8 * (ex - cx) + ez, 1), pl.ds(8 * ex + ez - cz, 1)
        diagonal = corner_dir(-cx, -cz)

        def put(row, value):
            csnd[index, pl.ds(row, 1), :] = value

        put(C_OWN, v_cot[diagonal, here, :])
        for j, i in enumerate(edge_dirs(2, -cz, 0)):
            put(C_Z + j, v_cot[i, here, :])
        put(C_ZIN, v_cot[diagonal, in_x, :])
        for j, i in enumerate(edge_dirs(0, -cx, 2)):
            put(C_X + j, v_cot[i, here, :])
        put(C_XIN, v_cot[diagonal, in_z, :])
        for k in range(6):
            put(C_CONF + k, v_conf[k, here, :])
        put(C_COL, v_col[here, :])

    for index in range(4):
        make_face(index)
    for index in range(4):
        make_corner(index)
    pl.semaphore_wait(barrier, 8)
    face_copies = [
        pltpu.make_async_remote_copy(
            src_ref=snd.at[k], dst_ref=rcv.at[k ^ 1], send_sem=f_send.at[k], recv_sem=f_recv.at[k ^ 1],
            device_id=face_device[k], device_id_type=MESH,
        )
        for k in range(4)
    ]
    corner_copies = [
        pltpu.make_async_remote_copy(
            src_ref=csnd.at[k], dst_ref=crcv.at[3 - k], send_sem=c_send.at[k], recv_sem=c_recv.at[3 - k],
            device_id=corner_device[k], device_id_type=MESH,
        )
        for k in range(4)
    ]
    for copy in face_copies + corner_copies:
        copy.start()

    def local(at, carry):
        rows, padded = pl.ds(pl.multiple_of(8 * at, 8), 8), pl.ds(pl.multiple_of(8 * at + 8, 8), 8)
        p = [v_conf[k, rows, :] for k in range(6)]
        s = stress_of(p)
        for k in range(6):
            x_conf[k, padded, :] = p[k]
            x_str[k, padded, :] = s[k]
        x_col[padded, :] = v_col[rows, :]
        for i in range(19):
            x_cot[i, padded, :] = v_cot[i, rows, :]
        _, inverse, u = flow_of(lambda i: v_pop[i, rows, :])
        for a in range(3):
            v_u[a, rows, :] = u[a]
        v_ri[rows, :] = inverse
        square = u[0] * u[0] + smooth_square
        speed = square * lax.rsqrt(square)
        up, down = 0.25 * (speed - u[0]), 0.25 * (speed + u[0])
        for k in range(6):
            q = v_con[k, rows, :]
            x_up[k, padded, :] = up * q
            x_down[k, padded, :] = down * q
        return carry

    lax.fori_loop(0, 8, local, 0)

    for copy in face_copies + corner_copies:
        copy.wait_recv()

    for side, index in ((-1, 0), (1, 1)):
        rows = pl.ds(0 if side < 0 else 72, 8)
        got = rcv.at[index]
        p = [got[F_CONF + k] for k in range(6)]
        s = stress_of(p)
        for k in range(6):
            x_conf[k, rows, :] = p[k]
            x_str[k, rows, :] = s[k]
        x_col[rows, :] = got[F_COL]
        for j, i in enumerate(dirs_where(0, side)):
            x_cot[i, rows, :] = got[F_COT + j]
        for k in range(6):
            (x_up if side < 0 else x_down)[k, rows, :] = got[F_UPW + k]
    for n, (side, index) in enumerate(((-1, 2), (1, 3))):
        got = rcv.at[index]
        for j, i in enumerate(dirs_where(2, side)):
            z_cot[n, j, pl.ds(8, 8), :] = got[F_COT + j]
            for cx in (-1, 1):
                if velocities[i][0] == cx:
                    z_cot[n, j, pl.ds(7 if cx < 0 else 16, 1), :] = crcv[corners.index((cx, side)), pl.ds(C_OWN, 1), :]
        s = stress_of([got[F_CONF + k] for k in range(6)])
        for a in range(3):
            z_str[n, a] = s[slot[a, 2]]

    def halo_force(index):
        axis, side = faces[index]
        across = 2 - axis
        edge = 0 if side < 0 else 7
        got = rcv.at[index]

        def corner_at(end):
            place = (side, end) if axis == 0 else (end, side)
            return corners.index(place)

        ends = {-1: first, 1: last}
        fills = {}
        for end in (-1, 1):
            c = corner_at(end)
            p = [crcv[c, pl.ds(C_CONF + k, 1), :] for k in range(6)]
            s = stress_of(p)
            fills[end] = ([s[slot[a, across]] for a in range(3)], crcv[c, pl.ds(C_COL, 1), :])
        c_halo = got[F_COL]
        mobility = 1.0 - c_halo * c_halo
        low, high = fills[-1], fills[1]

        def at_ends(lo, hi):
            return jnp.where(first, rows_of(-0.5 * lo), jnp.where(last, rows_of(0.5 * hi), 0.0))

        p = [plane(v_conf, axis, edge, k) for k in range(6)]
        s = stress_of(p)
        c_edge = plane(v_col, axis, edge)
        force = []
        for a in range(3):
            value = (-0.5 * side) * s[slot[a, axis]] + at_ends(low[0][a], high[0][a])
            if a == axis:
                value = value + mobility * ((-0.5 * side) * c_edge)
            elif a == across:
                value = value + mobility * at_ends(low[1], high[1])
            force.append(value)
        values = []
        for i in dirs_where(axis, -side):
            c = velocities[i]
            value = plane(v_cot, axis, edge, i)
            if c[across]:
                end = c[across]
                if axis == 0:
                    n = 0 if end < 0 else 1
                    j = dirs_where(2, end).index(i)
                    row = z_cot[n, j, pl.ds(8 + edge, 1), :]
                else:
                    row = x_cot[i, pl.ds((0 if end < 0 else 72) + edge, 1), :]
                value = shift(value, end, rows_of(row), rows_of(row))
            values.append((i, in_y(value, c[1])))
        for end in (-1, 1):
            c = corner_at(end)
            base = C_Z if axis == 0 else C_X
            for j, i in enumerate(edge_dirs(across, end, axis)):
                row = crcv[c, pl.ds(base + j, 1), :]
                values.append((i, in_y(jnp.where(ends[end], rows_of(row), 0.0), velocities[i][1])))
            i = corner_dir(side, end) if axis == 0 else corner_dir(end, side)
            row = crcv[c, pl.ds(C_ZIN if axis == 0 else C_XIN, 1), :]
            values.append((i, jnp.where(ends[end], rows_of(row), 0.0)))
        zeroth, one, two = moments(values)
        tensor = tensor_of(zeroth, two)
        one = [plus(one[a], got[F_G + a]) for a in range(3)]
        tensor = [plus(tensor[k], got[F_K + k]) for k in range(6)]
        ratio = got[F_R]
        w = [got[F_W + a] + ratio * force[a] for a in range(3)]
        turned = apply(tensor, w)
        return [got[F_CHI] * (3.0 * one[a] + turned[a]) for a in range(3)]

    for index in range(4):
        h = halo_force(index)
        for a in range(3):
            if index < 2:
                x_h[a, pl.ds(0 if index == 0 else 72, 8), :] = h[a]
            else:
                z_h[index - 2, a] = h[a]

    def main(at, carry):
        def rows(by=0):
            return pl.ds(pl.multiple_of(8 * (at + by), 8), 8)

        def padded(by=0):
            return pl.ds(pl.multiple_of(8 * (at + by) + 8, 8), 8)

        def z_row(ref, n, k):
            return rows_of(ref[n, k, pl.ds(at, 1), :])

        def face_row(index, k):
            return rows_of(rcv[index, k, pl.ds(at, 1), :])

        label = v_lab[rows(), :]
        fluid = jnp.where(label == 0, 1.0, 0.0)
        solid = label == 1
        inverse = v_ri[rows(), :]
        u = [v_u[a, rows(), :] for a in range(3)]
        colour = x_col[padded(), :]
        mobility = 1.0 - colour * colour
        force = []
        for a in range(3):
            k = slot[a, 0]
            value = x_str[k, padded(1), :] - x_str[k, padded(-1), :]
            k = slot[a, 1]
            here = x_str[k, padded(), :]
            value = value + (in_y(here, 1) - in_y(here, -1))
            here = x_str[slot[a, 2], padded(), :]
            value = value + (shift(here, 1, None, z_row(z_str, 1, a)) - shift(here, -1, z_row(z_str, 0, a), None))
            if a == 0:
                slope = x_col[padded(1), :] - x_col[padded(-1), :]
            elif a == 1:
                slope = in_y(colour, 1) - in_y(colour, -1)
            else:
                slope = shift(colour, 1, None, face_row(3, F_COL)) - shift(colour, -1, face_row(2, F_COL), None)
            force.append(0.5 * (value + mobility * slope))
        values = []
        for i in range(19):
            c = velocities[i]
            value = x_cot[i, padded(c[0]), :]
            if c[2]:
                n = 0 if c[2] < 0 else 1
                row = rows_of(z_cot[n, dirs_where(2, c[2]).index(i), pl.ds(8 + at + c[0], 1), :])
                value = shift(value, c[2], row, row)
            values.append((i, in_y(value, c[1])))
        zeroth, one, two = moments(values)
        tensor = tensor_of(zeroth, two)
        v = [u[a] + 0.5 * inverse * force[a] for a in range(3)]
        turned = apply(tensor, v)
        lean = [3.0 * one[a] + turned[a] for a in range(3)]
        energy = zeroth
        for a in range(3):
            energy = energy + v[a] * (3.0 * one[a] + 0.5 * turned[a])
        other = apply(tensor, force)
        h = [fluid * (lean[a] + (0.1875 * inverse) * other[a]) for a in range(3)]
        pull = [fluid * (1.25 * lean[a] + (0.375 * inverse) * other[a]) for a in range(3)]
        for a in range(3):
            x_h[a, padded(), :] = h[a]
        rho_bar = (1.25 * fluid) * energy
        for a in range(3):
            rho_bar = rho_bar - (0.5 * inverse) * (pull[a] * force[a])
        inlet = (
            (1.0 - 1.5 * inlet_speed * inlet_speed) * zeroth
            + (3.0 * inlet_speed) * one[2]
            + (4.5 * inlet_speed * inlet_speed) * two[2]
        )
        rho_bar = rho_bar + jnp.where(label == 2, inlet, 0.0)
        q = [v_con[k, rows(), :] for k in range(6)]
        m_bar = []
        for a in range(3):
            along = bend = None
            for k in range(6):
                here = x_conf[k, padded(), :]
                if a == 0:
                    up, down = x_conf[k, padded(1), :], x_conf[k, padded(-1), :]
                elif a == 1:
                    up, down = in_y(here, 1), in_y(here, -1)
                else:
                    up = shift(here, 1, None, face_row(3, F_CONF + k))
                    down = shift(here, -1, face_row(2, F_CONF + k), None)
                d, c = q[k] * (up - down), q[k] * (up + down - 2.0 * here)
                along, bend = plus(along, d), plus(bend, c)
            square = u[a] * u[a] + smooth_square
            u_bar = (0.25 * u[a] * lax.rsqrt(square)) * bend - 0.25 * along
            m_bar.append(pull[a] + inverse * u_bar)
        for a in range(3):
            rho_bar = rho_bar - m_bar[a] * u[a]
        keep = -0.25 * fluid
        by_dir = dict(values)
        for i in range(19):
            c = velocities[i]
            value = rho_bar + jnp.where(solid, by_dir[opposite[i]], keep * by_dir[i])
            for a in range(3):
                if c[a]:
                    value = value + m_bar[a] if c[a] > 0 else value - m_bar[a]
            o_pop[i, rows(), :] = value
        return carry

    lax.fori_loop(0, 8, main, 0)

    def finish(at, carry):
        def rows(by=0):
            return pl.ds(pl.multiple_of(8 * (at + by), 8), 8)

        def padded(by=0):
            return pl.ds(pl.multiple_of(8 * (at + by) + 8, 8), 8)

        h = [x_h[a, padded(), :] for a in range(3)]
        u = [v_u[a, rows(), :] for a in range(3)]
        colour = x_col[padded(), :]
        mobility = 1.0 - colour * colour
        t = []
        colour_bar = None
        for a in range(3):
            row_down = rows_of(z_h[0, a, pl.ds(at, 1), :])
            row_up = rows_of(z_h[1, a, pl.ds(at, 1), :])
            t.append(
                [
                    x_h[a, padded(-1), :] - x_h[a, padded(1), :],
                    in_y(h[a], -1) - in_y(h[a], 1),
                    shift(h[a], -1, row_down, None) - shift(h[a], 1, None, row_up),
                ]
            )
        def flux(by):
            near = x_col[padded(by), :]
            return (1.0 - near * near) * x_h[0, padded(by), :]

        up_c, down_c = x_col[padded(1), :], x_col[padded(-1), :]
        z_up_c, z_down_c = rows_of(rcv[3, F_COL, pl.ds(at, 1), :]), rows_of(rcv[2, F_COL, pl.ds(at, 1), :])
        slopes = [
            up_c - down_c,
            in_y(colour, 1) - in_y(colour, -1),
            shift(colour, 1, None, z_up_c) - shift(colour, -1, z_down_c, None),
        ]
        colour_bar = h[0] * slopes[0] + h[1] * slopes[1] + h[2] * slopes[2]
        colour_bar = -colour * colour_bar
        in_z = mobility * h[2]
        z_up_f = (1.0 - z_up_c * z_up_c) * rows_of(z_h[1, 2, pl.ds(at, 1), :])
        z_down_f = (1.0 - z_down_c * z_down_c) * rows_of(z_h[0, 2, pl.ds(at, 1), :])
        flow_y = mobility * h[1]
        spread = (
            (flux(-1) - flux(1))
            + (in_y(flow_y, -1) - in_y(flow_y, 1))
            + (shift(in_z, -1, z_down_f, None) - shift(in_z, 1, None, z_up_f))
        )
        o_col[rows(), :] = colour_bar + 0.5 * spread
        w = []
        for a, b in pairs:
            w.append(0.5 * t[a][a] if a == b else 0.25 * (t[a][b] + t[b][a]))
        p = [x_conf[k, padded(), :] for k in range(6)]
        result = []
        for a, b in pairs:
            dot = None
            for m in range(3):
                if a == b:
                    dot = plus(dot, w[slot[a, m]] * p[slot[m, b]])
                else:
                    dot = plus(dot, w[slot[a, m]] * p[slot[m, b]] + p[slot[a, m]] * w[slot[m, b]])
            result.append(w[slot[a, b]] + dot if a == b else 2.0 * w[slot[a, b]] + dot)
        speeds = []
        for a in range(3):
            square = u[a] * u[a] + smooth_square
            speeds.append(square * lax.rsqrt(square))
        stay = 0.9 - 0.5 * (speeds[0] + speeds[1] + speeds[2])
        go_up = [0.25 * (speeds[a] - u[a]) for a in range(3)]
        go_down = [0.25 * (speeds[a] + u[a]) for a in range(3)]
        for k in range(6):
            q = v_con[k, rows(), :]
            value = result[k] + stay * q
            value = value + in_y(go_up[1] * q, -1) + in_y(go_down[1] * q, 1)
            value = value + shift(go_up[2] * q, -1, rows_of(rcv[2, F_UPW + k, pl.ds(at, 1), :]), None)
            value = value + shift(go_down[2] * q, 1, None, rows_of(rcv[3, F_UPW + k, pl.ds(at, 1), :]))
            value = value + x_up[k, padded(-1), :] + x_down[k, padded(1), :]
            o_conf[k, rows(), :] = value
        return carry

    lax.fori_loop(0, 8, finish, 0)
    for copy in face_copies + corner_copies:
        copy.wait_send()


def deliver(a, b, c, out_a, out_b, out_c, sem):
    copies = [
        pltpu.make_async_copy(src, dst, sem.at[k]) for k, (src, dst) in enumerate(((a, out_a), (b, out_b), (c, out_c)))
    ]
    for copy in copies:
        copy.start()
    for copy in copies:
        copy.wait()


def body(populations, colour, conformation, labels, pop_cotangent, conf_cotangent):
    anywhere = pl.BlockSpec(memory_space=pl.ANY)
    near = pl.BlockSpec(memory_space=pltpu.VMEM)
    args = [
        v.reshape(v.shape[:-3] + (64, 128))
        for v in (populations, colour, conformation, labels, pop_cotangent, conf_cotangent)
    ]
    shapes = [(19, 64, 128), (64, 128), (6, 64, 128)]
    scratch = [pltpu.VMEM(v.shape, v.dtype) for v in args]
    scratch += [pltpu.VMEM((4, F_ALL, 8, 128), F32)] * 2
    scratch += [pltpu.VMEM((4, C_ALL, 128), F32)] * 2
    padded = [(19, 80, 128), (6, 80, 128), (80, 128), (6, 80, 128), (3, 80, 128), (6, 80, 128), (6, 80, 128)]
    scratch += [pltpu.VMEM(s, F32) for s in padded]
    scratch += [pltpu.VMEM(s, F32) for s in [(2, 5, 24, 128), (2, 3, 8, 128), (2, 3, 8, 128), (3, 64, 128), (64, 128)]]
    scratch += [pltpu.SemaphoreType.DMA((6,))] + [pltpu.SemaphoreType.DMA((4,))] * 4
    parts = pl.pallas_call(
        kernel,
        out_shape=tuple(pltpu.VMEM(s, F32) for s in shapes),
        in_specs=[anywhere] * 6,
        out_specs=[near] * 3,
        scratch_shapes=scratch,
        compiler_params=pltpu.CompilerParams(
            collective_id=0, has_side_effects=True, vmem_limit_bytes=32 * 1024 * 1024
        ),
    )(*[pltpu.with_memory_space_constraint(v, pltpu.HBM) for v in args])
    parts = [pltpu.with_memory_space_constraint(v, pltpu.VMEM) for v in parts]
    out = pl.pallas_call(
        deliver,
        out_shape=tuple(jax.ShapeDtypeStruct(s, F32) for s in shapes),
        in_specs=[near] * 3,
        out_specs=[anywhere] * 3,
        scratch_shapes=[pltpu.SemaphoreType.DMA((3,))],
    )(*parts)
    return tuple(v.reshape(v.shape[:-2] + (8, 8, 128)) for v in out)


def solution(mesh):
    placed = (
        P(None, "xy", "gz", None),
        P("xy", "gz", None),
        P(None, "xy", "gz", None),
        P("xy", "gz", None),
        P(None, "xy", "gz", None),
        P(None, "xy", "gz", None),
    )
    return jax.shard_map(
        body,
        mesh=mesh,
        in_specs=placed,
        out_specs=(P(None, "xy", "gz", None), P("xy", "gz", None), P(None, "xy", "gz", None)),
        check_vma=False,
    )
```

```python
import functools

import jax
import jax.numpy as jnp
from jax import lax
from jax.experimental import pallas as pl
from jax.experimental.pallas import tpu as pltpu
from jax.sharding import PartitionSpec as P

MESH = pl.DeviceIdType.MESH
F32 = jnp.float32

velocities = (
    (0, 0, 0),
    (1, 0, 0),
    (-1, 0, 0),
    (0, 1, 0),
    (0, -1, 0),
    (0, 0, 1),
    (0, 0, -1),
    (1, 1, 0),
    (-1, -1, 0),
    (1, -1, 0),
    (-1, 1, 0),
    (1, 0, 1),
    (-1, 0, -1),
    (1, 0, -1),
    (-1, 0, 1),
    (0, 1, 1),
    (0, -1, -1),
    (0, 1, -1),
    (0, -1, 1),
)
opposite = (0, 2, 1, 4, 3, 6, 5, 8, 7, 10, 9, 12, 11, 14, 13, 16, 15, 18, 17)
slot = {(0, 0): 0, (1, 1): 1, (2, 2): 2, (0, 1): 3, (1, 0): 3, (0, 2): 4, (2, 0): 4, (1, 2): 5, (2, 1): 5}
pairs = ((0, 0), (1, 1), (2, 2), (0, 1), (0, 2), (1, 2))
inlet_speed = 0.05
smooth_square = 0.02 * 0.02
F_CONF, F_COL, F_COT, F_UPW, F_G, F_K, F_W, F_R, F_CHI, F_ALL = 0, 6, 7, 12, 18, 21, 27, 30, 31, 32
C_OWN, C_Z, C_ZIN, C_X, C_XIN, C_CONF, C_COL, C_ALL = 0, 1, 4, 5, 8, 9, 15, 16


def dirs_where(axis, sign):
    return tuple(i for i in range(19) if velocities[i][axis] == sign)


def corner_dir(sx, sz):
    return next(i for i in range(19) if velocities[i][0] == sx and velocities[i][2] == sz)


def edge_dirs(axis, sign, other):
    return tuple(i for i in range(19) if velocities[i][axis] == sign and velocities[i][other] == 0)


def stress_of(conf):
    out = []
    for a, b in pairs:
        dot = conf[slot[a, 0]] * conf[slot[0, b]]
        for m in (1, 2):
            dot = dot + conf[slot[a, m]] * conf[slot[m, b]]
        out.append(conf[slot[a, b]] + 0.5 * dot)
    return out


def total(terms):
    result = None
    for sign, value in terms:
        if result is None:
            result = value if sign > 0 else -value
        else:
            result = result + value if sign > 0 else result - value
    return result


def moments(values):
    def weighted(sign_of):
        axial = total([(sign_of(velocities[i]), v) for i, v in values if 0 < i < 7 and sign_of(velocities[i])])
        edge = total([(sign_of(velocities[i]), v) for i, v in values if i >= 7 and sign_of(velocities[i])])
        if axial is None and edge is None:
            return None
        if axial is None:
            return edge * (1.0 / 36.0)
        if edge is None:
            return axial * (1.0 / 18.0)
        return axial * (1.0 / 18.0) + edge * (1.0 / 36.0)

    zeroth = weighted(lambda c: 1)
    rest = [v for i, v in values if i == 0]
    if rest:
        zeroth = zeroth + rest[0] * (1.0 / 3.0)
    first = [weighted(lambda c, a=a: c[a]) for a in range(3)]
    second = [weighted(lambda c, a=a, b=b: c[a] * c[b]) for a, b in pairs]
    return zeroth, first, second


def tensor_of(zeroth, second):
    out = []
    for k in range(6):
        value = None if second[k] is None else 9.0 * second[k]
        if k < 3:
            value = -3.0 * zeroth if value is None else value - 3.0 * zeroth
        out.append(value)
    return out


def apply(tensor, vector):
    out = []
    for a in range(3):
        value = None
        for b in range(3):
            if tensor[slot[a, b]] is not None:
                term = tensor[slot[a, b]] * vector[b]
                value = term if value is None else value + term
        out.append(value)
    return out


def plus(a, b):
    return a if b is None else b if a is None else a + b


def in_y(value, by):
    return value if by == 0 else pltpu.roll(value, (-by) % 128, 1)


def rows_of(row):
    return jnp.broadcast_to(row, (8, 128))


def kernel(
    pop, col, conf, lab, cot, con,
    o_pop, o_col, o_conf,
    v_pop, v_col, v_conf, v_lab, v_cot, v_con,
    snd, rcv, csnd, crcv,
    x_cot, x_conf, x_col, x_str, x_h, x_up, x_down, z_cot, z_str, z_h, v_u, v_ri,
    in_sem, f_send, f_recv, c_send, c_recv, go_sem,
):
    loads = [
        pltpu.make_async_copy(src, dst, in_sem.at[k])
        for k, (src, dst) in enumerate(
            [(conf, v_conf), (col, v_col), (cot, v_cot), (pop, v_pop), (lab, v_lab), (con, v_con)]
        )
    ]
    for copy in loads:
        copy.start()
    nz, nx = lax.axis_size("gz"), lax.axis_size("xy")
    z, x = lax.axis_index("gz"), lax.axis_index("xy")
    z_of = {-1: lax.rem(z + nz - 1, nz), 0: z, 1: lax.rem(z + 1, nz)}
    x_of = {-1: lax.rem(x + nx - 1, nx), 0: x, 1: lax.rem(x + 1, nx)}
    faces = ((0, -1), (0, 1), (2, -1), (2, 1))
    face_device = [(z_of[0], x_of[-1]), (z_of[0], x_of[1]), (z_of[-1], x_of[0]), (z_of[1], x_of[0])]
    corners = ((-1, -1), (-1, 1), (1, -1), (1, 1))
    corner_device = [(z_of[cz], x_of[cx]) for cx, cz in corners]
    place = lax.rem(x, 8)
    upper = lax.rem(lax.div(x, 8), 2)
    edge_x = {-1: place == 0, 0: False, 1: place == 7}
    edge_z = {-1: z == 0, 0: False, 1: z == nz - 1}
    offsets = [((side, 0) if axis == 0 else (0, side)) for axis, side in faces] + list(corners)
    devices = face_device + corner_device
    flip = (1, 0, 3, 2, 7, 6, 5, 4)
    follows, leads = [], []
    for dx, dz in offsets:
        far_x, far_z = edge_x[dx], edge_z[dz]
        far = jnp.logical_or(far_x, far_z)
        follow = jnp.logical_or(
            jnp.logical_and(far_x, upper == 0),
            jnp.logical_and(jnp.logical_and(far_z, jnp.logical_not(far_x)), z == 0),
        )
        follows.append(follow)
        leads.append(jnp.logical_and(far, jnp.logical_not(follow)))
    barrier = pltpu.get_barrier_semaphore()
    expected = jnp.int32(0)
    for device, follow, lead in zip(devices, follows, leads):
        expected = expected + jnp.where(follow, 0, 1)

        @pl.when(jnp.logical_not(lead))
        def _(device=device):
            pl.semaphore_signal(barrier, inc=1, device_id=device, device_id_type=MESH)

    for copy in loads:
        copy.wait()

    lane = lax.broadcasted_iota(jnp.int32, (8, 128), 0)
    first, last = lane == 0, lane == 7

    def shift(value, by, low=None, high=None):
        if by == 0:
            return value
        rolled = pltpu.roll(value, 7 if by > 0 else 1, 0)
        fill = high if by > 0 else low
        fill = 0.0 if fill is None else fill
        return jnp.where(last if by > 0 else first, fill, rolled)

    def plane(ref, axis, at, k=None):
        rows = pl.ds(8 * at, 8) if axis == 0 else pl.ds(at, 8, stride=8)
        return ref[rows, :] if k is None else ref[k, rows, :]

    def flow_of(load):
        f = [load(i) for i in range(19)]
        rho = f[0]
        for i in range(1, 19):
            rho = rho + f[i]
        inverse = 1.0 / rho
        u = [total([(velocities[i][a], f[i]) for i in range(19) if velocities[i][a]]) * inverse for a in range(3)]
        return rho, inverse, u

    def make_face(index):
        axis, side = faces[index]
        across = 2 - axis
        edge = 7 if side > 0 else 0
        inner = edge - side
        p_edge = [plane(v_conf, axis, edge, k) for k in range(6)]
        p_inner = [plane(v_conf, axis, inner, k) for k in range(6)]
        s_edge, s_inner = stress_of(p_edge), stress_of(p_inner)
        c_edge, c_inner = plane(v_col, axis, edge), plane(v_col, axis, inner)
        _, inverse, u = flow_of(lambda i: plane(v_pop, axis, edge, i))
        ratio = 0.6875 * inverse
        fluid = jnp.where(plane(v_lab, axis, edge) == 0, 1.0, 0.0)
        out = snd.at[index]
        for k in range(6):
            out[F_CONF + k] = p_edge[k]
        out[F_COL] = c_edge
        for j, i in enumerate(dirs_where(axis, -side)):
            out[F_COT + j] = plane(v_cot, axis, edge, i)
        speed = u[axis] * u[axis] + smooth_square
        speed = speed * lax.rsqrt(speed)
        upwind = 0.25 * (speed - side * u[axis])
        for k in range(6):
            out[F_UPW + k] = upwind * plane(v_con, axis, edge, k)
        values = []
        for i in range(19):
            c = velocities[i]
            if c[axis] == side:
                continue
            got = plane(v_cot, axis, edge if c[axis] == 0 else inner, i)
            values.append((i, in_y(shift(got, c[across]), c[1])))
        zeroth, one, two = moments(values)
        tensor = tensor_of(zeroth, two)
        mobility = 1.0 - c_edge * c_edge
        force = []
        for a in range(3):
            k = slot[a, 1]
            value = 0.5 * (in_y(s_edge[k], 1) - in_y(s_edge[k], -1))
            k = slot[a, across]
            value = value + 0.5 * (shift(s_edge[k], 1) - shift(s_edge[k], -1))
            value = value - (0.5 * side) * s_inner[slot[a, axis]]
            if a == 1:
                slope = 0.5 * (in_y(c_edge, 1) - in_y(c_edge, -1))
            elif a == across:
                slope = 0.5 * (shift(c_edge, 1) - shift(c_edge, -1))
            else:
                slope = (-0.5 * side) * c_inner
            force.append(value + mobility * slope)
        for a in range(3):
            out[F_G + a] = one[a]
            out[F_W + a] = u[a] + ratio * force[a]
        for k in range(6):
            out[F_K + k] = tensor[k]
        out[F_R] = ratio
        out[F_CHI] = fluid

    def make_corner(index):
        cx, cz = corners[index]
        ex, ez = (7 if cx > 0 else 0), (7 if cz > 0 else 0)
        here = pl.ds(8 * ex + ez, 1)
        in_x, in_z = pl.ds(8 * (ex - cx) + ez, 1), pl.ds(8 * ex + ez - cz, 1)
        diagonal = corner_dir(-cx, -cz)

        def put(row, value):
            csnd[index, pl.ds(row, 1), :] = value

        put(C_OWN, v_cot[diagonal, here, :])
        for j, i in enumerate(edge_dirs(2, -cz, 0)):
            put(C_Z + j, v_cot[i, here, :])
        put(C_ZIN, v_cot[diagonal, in_x, :])
        for j, i in enumerate(edge_dirs(0, -cx, 2)):
            put(C_X + j, v_cot[i, here, :])
        put(C_XIN, v_cot[diagonal, in_z, :])
        for k in range(6):
            put(C_CONF + k, v_conf[k, here, :])
        put(C_COL, v_col[here, :])

    for index in range(4):
        make_face(index)
    for index in range(4):
        make_corner(index)
    pl.semaphore_wait(barrier, expected)
    face_copies = [
        pltpu.make_async_remote_copy(
            src_ref=snd.at[k], dst_ref=rcv.at[k ^ 1], send_sem=f_send.at[k], recv_sem=f_recv.at[k ^ 1],
            device_id=face_device[k], device_id_type=MESH,
        )
        for k in range(4)
    ]
    corner_copies = [
        pltpu.make_async_remote_copy(
            src_ref=csnd.at[k], dst_ref=crcv.at[3 - k], send_sem=c_send.at[k], recv_sem=c_recv.at[3 - k],
            device_id=corner_device[k], device_id_type=MESH,
        )
        for k in range(4)
    ]
    copies = face_copies + corner_copies
    for k in range(8):

        @pl.when(leads[k])
        def _(k=k):
            pl.semaphore_signal(go_sem.at[flip[k]], inc=1, device_id=devices[k], device_id_type=MESH)

    for copy, follow in zip(copies, follows):

        @pl.when(jnp.logical_not(follow))
        def _(copy=copy):
            copy.start()

    def send_later(ks):
        for k in ks:

            @pl.when(follows[k])
            def _(k=k):
                pl.semaphore_wait(go_sem.at[k], 1)
                copies[k].start()

    def local(at, carry):
        rows, padded = pl.ds(pl.multiple_of(8 * at, 8), 8), pl.ds(pl.multiple_of(8 * at + 8, 8), 8)
        p = [v_conf[k, rows, :] for k in range(6)]
        s = stress_of(p)
        for k in range(6):
            x_conf[k, padded, :] = p[k]
            x_str[k, padded, :] = s[k]
        x_col[padded, :] = v_col[rows, :]
        for i in range(19):
            x_cot[i, padded, :] = v_cot[i, rows, :]
        _, inverse, u = flow_of(lambda i: v_pop[i, rows, :])
        for a in range(3):
            v_u[a, rows, :] = u[a]
        v_ri[rows, :] = inverse
        square = u[0] * u[0] + smooth_square
        speed = square * lax.rsqrt(square)
        up, down = 0.25 * (speed - u[0]), 0.25 * (speed + u[0])
        for k in range(6):
            q = v_con[k, rows, :]
            x_up[k, padded, :] = up * q
            x_down[k, padded, :] = down * q
        return carry

    lax.fori_loop(0, 8, local, 0)

    arrival = [copies[k] for k in flip]
    send_later((2, 3, 4, 5, 6, 7, 0, 1))
    for k in range(8):
        arrival[k].wait_recv()

    for side, index in ((-1, 0), (1, 1)):
        rows = pl.ds(0 if side < 0 else 72, 8)
        got = rcv.at[index]
        p = [got[F_CONF + k] for k in range(6)]
        s = stress_of(p)
        for k in range(6):
            x_conf[k, rows, :] = p[k]
            x_str[k, rows, :] = s[k]
        x_col[rows, :] = got[F_COL]
        for j, i in enumerate(dirs_where(0, side)):
            x_cot[i, rows, :] = got[F_COT + j]
        for k in range(6):
            (x_up if side < 0 else x_down)[k, rows, :] = got[F_UPW + k]
    for n, (side, index) in enumerate(((-1, 2), (1, 3))):
        got = rcv.at[index]
        for j, i in enumerate(dirs_where(2, side)):
            z_cot[n, j, pl.ds(8, 8), :] = got[F_COT + j]
            for cx in (-1, 1):
                if velocities[i][0] == cx:
                    z_cot[n, j, pl.ds(7 if cx < 0 else 16, 1), :] = crcv[corners.index((cx, side)), pl.ds(C_OWN, 1), :]
        s = stress_of([got[F_CONF + k] for k in range(6)])
        for a in range(3):
            z_str[n, a] = s[slot[a, 2]]

    def halo_force(index):
        axis, side = faces[index]
        across = 2 - axis
        edge = 0 if side < 0 else 7
        got = rcv.at[index]

        def corner_at(end):
            place = (side, end) if axis == 0 else (end, side)
            return corners.index(place)

        ends = {-1: first, 1: last}
        fills = {}
        for end in (-1, 1):
            c = corner_at(end)
            p = [crcv[c, pl.ds(C_CONF + k, 1), :] for k in range(6)]
            s = stress_of(p)
            fills[end] = ([s[slot[a, across]] for a in range(3)], crcv[c, pl.ds(C_COL, 1), :])
        c_halo = got[F_COL]
        mobility = 1.0 - c_halo * c_halo
        low, high = fills[-1], fills[1]

        def at_ends(lo, hi):
            return jnp.where(first, rows_of(-0.5 * lo), jnp.where(last, rows_of(0.5 * hi), 0.0))

        p = [plane(v_conf, axis, edge, k) for k in range(6)]
        s = stress_of(p)
        c_edge = plane(v_col, axis, edge)
        force = []
        for a in range(3):
            value = (-0.5 * side) * s[slot[a, axis]] + at_ends(low[0][a], high[0][a])
            if a == axis:
                value = value + mobility * ((-0.5 * side) * c_edge)
            elif a == across:
                value = value + mobility * at_ends(low[1], high[1])
            force.append(value)
        values = []
        for i in dirs_where(axis, -side):
            c = velocities[i]
            value = plane(v_cot, axis, edge, i)
            if c[across]:
                end = c[across]
                if axis == 0:
                    n = 0 if end < 0 else 1
                    j = dirs_where(2, end).index(i)
                    row = z_cot[n, j, pl.ds(8 + edge, 1), :]
                else:
                    row = x_cot[i, pl.ds((0 if end < 0 else 72) + edge, 1), :]
                value = shift(value, end, rows_of(row), rows_of(row))
            values.append((i, in_y(value, c[1])))
        for end in (-1, 1):
            c = corner_at(end)
            base = C_Z if axis == 0 else C_X
            for j, i in enumerate(edge_dirs(across, end, axis)):
                row = crcv[c, pl.ds(base + j, 1), :]
                values.append((i, in_y(jnp.where(ends[end], rows_of(row), 0.0), velocities[i][1])))
            i = corner_dir(side, end) if axis == 0 else corner_dir(end, side)
            row = crcv[c, pl.ds(C_ZIN if axis == 0 else C_XIN, 1), :]
            values.append((i, jnp.where(ends[end], rows_of(row), 0.0)))
        zeroth, one, two = moments(values)
        tensor = tensor_of(zeroth, two)
        one = [plus(one[a], got[F_G + a]) for a in range(3)]
        tensor = [plus(tensor[k], got[F_K + k]) for k in range(6)]
        ratio = got[F_R]
        w = [got[F_W + a] + ratio * force[a] for a in range(3)]
        turned = apply(tensor, w)
        return [got[F_CHI] * (3.0 * one[a] + turned[a]) for a in range(3)]

    for index in range(4):
        h = halo_force(index)
        for a in range(3):
            if index < 2:
                x_h[a, pl.ds(0 if index == 0 else 72, 8), :] = h[a]
            else:
                z_h[index - 2, a] = h[a]

    def main(at, carry):
        def rows(by=0):
            return pl.ds(pl.multiple_of(8 * (at + by), 8), 8)

        def padded(by=0):
            return pl.ds(pl.multiple_of(8 * (at + by) + 8, 8), 8)

        def z_row(ref, n, k):
            return rows_of(ref[n, k, pl.ds(at, 1), :])

        def face_row(index, k):
            return rows_of(rcv[index, k, pl.ds(at, 1), :])

        label = v_lab[rows(), :]
        fluid = jnp.where(label == 0, 1.0, 0.0)
        solid = label == 1
        inverse = v_ri[rows(), :]
        u = [v_u[a, rows(), :] for a in range(3)]
        colour = x_col[padded(), :]
        mobility = 1.0 - colour * colour
        force = []
        for a in range(3):
            k = slot[a, 0]
            value = x_str[k, padded(1), :] - x_str[k, padded(-1), :]
            k = slot[a, 1]
            here = x_str[k, padded(), :]
            value = value + (in_y(here, 1) - in_y(here, -1))
            here = x_str[slot[a, 2], padded(), :]
            value = value + (shift(here, 1, None, z_row(z_str, 1, a)) - shift(here, -1, z_row(z_str, 0, a), None))
            if a == 0:
                slope = x_col[padded(1), :] - x_col[padded(-1), :]
            elif a == 1:
                slope = in_y(colour, 1) - in_y(colour, -1)
            else:
                slope = shift(colour, 1, None, face_row(3, F_COL)) - shift(colour, -1, face_row(2, F_COL), None)
            force.append(0.5 * (value + mobility * slope))
        values = []
        for i in range(19):
            c = velocities[i]
            value = x_cot[i, padded(c[0]), :]
            if c[2]:
                n = 0 if c[2] < 0 else 1
                row = rows_of(z_cot[n, dirs_where(2, c[2]).index(i), pl.ds(8 + at + c[0], 1), :])
                value = shift(value, c[2], row, row)
            values.append((i, in_y(value, c[1])))
        zeroth, one, two = moments(values)
        tensor = tensor_of(zeroth, two)
        v = [u[a] + 0.5 * inverse * force[a] for a in range(3)]
        turned = apply(tensor, v)
        lean = [3.0 * one[a] + turned[a] for a in range(3)]
        energy = zeroth
        for a in range(3):
            energy = energy + v[a] * (3.0 * one[a] + 0.5 * turned[a])
        other = apply(tensor, force)
        h = [fluid * (lean[a] + (0.1875 * inverse) * other[a]) for a in range(3)]
        pull = [fluid * (1.25 * lean[a] + (0.375 * inverse) * other[a]) for a in range(3)]
        for a in range(3):
            x_h[a, padded(), :] = h[a]
        rho_bar = (1.25 * fluid) * energy
        for a in range(3):
            rho_bar = rho_bar - (0.5 * inverse) * (pull[a] * force[a])
        inlet = (
            (1.0 - 1.5 * inlet_speed * inlet_speed) * zeroth
            + (3.0 * inlet_speed) * one[2]
            + (4.5 * inlet_speed * inlet_speed) * two[2]
        )
        rho_bar = rho_bar + jnp.where(label == 2, inlet, 0.0)
        q = [v_con[k, rows(), :] for k in range(6)]
        m_bar = []
        for a in range(3):
            along = bend = None
            for k in range(6):
                here = x_conf[k, padded(), :]
                if a == 0:
                    up, down = x_conf[k, padded(1), :], x_conf[k, padded(-1), :]
                elif a == 1:
                    up, down = in_y(here, 1), in_y(here, -1)
                else:
                    up = shift(here, 1, None, face_row(3, F_CONF + k))
                    down = shift(here, -1, face_row(2, F_CONF + k), None)
                d, c = q[k] * (up - down), q[k] * (up + down - 2.0 * here)
                along, bend = plus(along, d), plus(bend, c)
            square = u[a] * u[a] + smooth_square
            u_bar = (0.25 * u[a] * lax.rsqrt(square)) * bend - 0.25 * along
            m_bar.append(pull[a] + inverse * u_bar)
        for a in range(3):
            rho_bar = rho_bar - m_bar[a] * u[a]
        keep = -0.25 * fluid
        by_dir = dict(values)
        for i in range(19):
            c = velocities[i]
            value = rho_bar + jnp.where(solid, by_dir[opposite[i]], keep * by_dir[i])
            for a in range(3):
                if c[a]:
                    value = value + m_bar[a] if c[a] > 0 else value - m_bar[a]
            o_pop[i, rows(), :] = value
        return carry

    lax.fori_loop(0, 8, main, 0)

    def finish(at, carry):
        def rows(by=0):
            return pl.ds(pl.multiple_of(8 * (at + by), 8), 8)

        def padded(by=0):
            return pl.ds(pl.multiple_of(8 * (at + by) + 8, 8), 8)

        h = [x_h[a, padded(), :] for a in range(3)]
        u = [v_u[a, rows(), :] for a in range(3)]
        colour = x_col[padded(), :]
        mobility = 1.0 - colour * colour
        t = []
        colour_bar = None
        for a in range(3):
            row_down = rows_of(z_h[0, a, pl.ds(at, 1), :])
            row_up = rows_of(z_h[1, a, pl.ds(at, 1), :])
            t.append(
                [
                    x_h[a, padded(-1), :] - x_h[a, padded(1), :],
                    in_y(h[a], -1) - in_y(h[a], 1),
                    shift(h[a], -1, row_down, None) - shift(h[a], 1, None, row_up),
                ]
            )
        def flux(by):
            near = x_col[padded(by), :]
            return (1.0 - near * near) * x_h[0, padded(by), :]

        up_c, down_c = x_col[padded(1), :], x_col[padded(-1), :]
        z_up_c, z_down_c = rows_of(rcv[3, F_COL, pl.ds(at, 1), :]), rows_of(rcv[2, F_COL, pl.ds(at, 1), :])
        slopes = [
            up_c - down_c,
            in_y(colour, 1) - in_y(colour, -1),
            shift(colour, 1, None, z_up_c) - shift(colour, -1, z_down_c, None),
        ]
        colour_bar = h[0] * slopes[0] + h[1] * slopes[1] + h[2] * slopes[2]
        colour_bar = -colour * colour_bar
        in_z = mobility * h[2]
        z_up_f = (1.0 - z_up_c * z_up_c) * rows_of(z_h[1, 2, pl.ds(at, 1), :])
        z_down_f = (1.0 - z_down_c * z_down_c) * rows_of(z_h[0, 2, pl.ds(at, 1), :])
        flow_y = mobility * h[1]
        spread = (
            (flux(-1) - flux(1))
            + (in_y(flow_y, -1) - in_y(flow_y, 1))
            + (shift(in_z, -1, z_down_f, None) - shift(in_z, 1, None, z_up_f))
        )
        o_col[rows(), :] = colour_bar + 0.5 * spread
        w = []
        for a, b in pairs:
            w.append(0.5 * t[a][a] if a == b else 0.25 * (t[a][b] + t[b][a]))
        p = [x_conf[k, padded(), :] for k in range(6)]
        result = []
        for a, b in pairs:
            dot = None
            for m in range(3):
                if a == b:
                    dot = plus(dot, w[slot[a, m]] * p[slot[m, b]])
                else:
                    dot = plus(dot, w[slot[a, m]] * p[slot[m, b]] + p[slot[a, m]] * w[slot[m, b]])
            result.append(w[slot[a, b]] + dot if a == b else 2.0 * w[slot[a, b]] + dot)
        speeds = []
        for a in range(3):
            square = u[a] * u[a] + smooth_square
            speeds.append(square * lax.rsqrt(square))
        stay = 0.9 - 0.5 * (speeds[0] + speeds[1] + speeds[2])
        go_up = [0.25 * (speeds[a] - u[a]) for a in range(3)]
        go_down = [0.25 * (speeds[a] + u[a]) for a in range(3)]
        for k in range(6):
            q = v_con[k, rows(), :]
            value = result[k] + stay * q
            value = value + in_y(go_up[1] * q, -1) + in_y(go_down[1] * q, 1)
            value = value + shift(go_up[2] * q, -1, rows_of(rcv[2, F_UPW + k, pl.ds(at, 1), :]), None)
            value = value + shift(go_down[2] * q, 1, None, rows_of(rcv[3, F_UPW + k, pl.ds(at, 1), :]))
            value = value + x_up[k, padded(-1), :] + x_down[k, padded(1), :]
            o_conf[k, rows(), :] = value
        return carry

    lax.fori_loop(0, 8, finish, 0)
    for copy in copies:
        copy.wait_send()


def deliver(a, b, c, out_a, out_b, out_c, sem):
    copies = [
        pltpu.make_async_copy(src, dst, sem.at[k]) for k, (src, dst) in enumerate(((a, out_a), (b, out_b), (c, out_c)))
    ]
    for copy in copies:
        copy.start()
    for copy in copies:
        copy.wait()


def body(populations, colour, conformation, labels, pop_cotangent, conf_cotangent):
    anywhere = pl.BlockSpec(memory_space=pl.ANY)
    near = pl.BlockSpec(memory_space=pltpu.VMEM)
    args = [
        v.reshape(v.shape[:-3] + (64, 128))
        for v in (populations, colour, conformation, labels, pop_cotangent, conf_cotangent)
    ]
    shapes = [(19, 64, 128), (64, 128), (6, 64, 128)]
    scratch = [pltpu.VMEM(v.shape, v.dtype) for v in args]
    scratch += [pltpu.VMEM((4, F_ALL, 8, 128), F32)] * 2
    scratch += [pltpu.VMEM((4, C_ALL, 128), F32)] * 2
    padded = [(19, 80, 128), (6, 80, 128), (80, 128), (6, 80, 128), (3, 80, 128), (6, 80, 128), (6, 80, 128)]
    scratch += [pltpu.VMEM(s, F32) for s in padded]
    scratch += [pltpu.VMEM(s, F32) for s in [(2, 5, 24, 128), (2, 3, 8, 128), (2, 3, 8, 128), (3, 64, 128), (64, 128)]]
    scratch += [pltpu.SemaphoreType.DMA((6,))] + [pltpu.SemaphoreType.DMA((4,))] * 4
    scratch += [pltpu.SemaphoreType.REGULAR((8,))]
    parts = pl.pallas_call(
        kernel,
        out_shape=tuple(pltpu.VMEM(s, F32) for s in shapes),
        in_specs=[anywhere] * 6,
        out_specs=[near] * 3,
        scratch_shapes=scratch,
        compiler_params=pltpu.CompilerParams(
            collective_id=0, has_side_effects=True, vmem_limit_bytes=32 * 1024 * 1024
        ),
    )(*[pltpu.with_memory_space_constraint(v, pltpu.HBM) for v in args])
    parts = [pltpu.with_memory_space_constraint(v, pltpu.VMEM) for v in parts]
    out = pl.pallas_call(
        deliver,
        out_shape=tuple(jax.ShapeDtypeStruct(s, F32) for s in shapes),
        in_specs=[near] * 3,
        out_specs=[anywhere] * 3,
        scratch_shapes=[pltpu.SemaphoreType.DMA((3,))],
    )(*parts)
    return tuple(v.reshape(v.shape[:-2] + (8, 8, 128)) for v in out)


def solution(mesh):
    placed = (
        P(None, "xy", "gz", None),
        P("xy", "gz", None),
        P(None, "xy", "gz", None),
        P("xy", "gz", None),
        P(None, "xy", "gz", None),
        P(None, "xy", "gz", None),
    )
    return jax.shard_map(
        body,
        mesh=mesh,
        in_specs=placed,
        out_specs=(P(None, "xy", "gz", None), P("xy", "gz", None), P(None, "xy", "gz", None)),
        check_vma=False,
    )
```

```python
import functools

import jax
import jax.numpy as jnp
from jax import lax
from jax.experimental import pallas as pl
from jax.experimental.pallas import tpu as pltpu
from jax.sharding import PartitionSpec as P

MESH = pl.DeviceIdType.MESH
F32 = jnp.float32
LEVEL = (3, 6)

velocities = (
    (0, 0, 0),
    (1, 0, 0),
    (-1, 0, 0),
    (0, 1, 0),
    (0, -1, 0),
    (0, 0, 1),
    (0, 0, -1),
    (1, 1, 0),
    (-1, -1, 0),
    (1, -1, 0),
    (-1, 1, 0),
    (1, 0, 1),
    (-1, 0, -1),
    (1, 0, -1),
    (-1, 0, 1),
    (0, 1, 1),
    (0, -1, -1),
    (0, 1, -1),
    (0, -1, 1),
)
opposite = (0, 2, 1, 4, 3, 6, 5, 8, 7, 10, 9, 12, 11, 14, 13, 16, 15, 18, 17)
slot = {(0, 0): 0, (1, 1): 1, (2, 2): 2, (0, 1): 3, (1, 0): 3, (0, 2): 4, (2, 0): 4, (1, 2): 5, (2, 1): 5}
pairs = ((0, 0), (1, 1), (2, 2), (0, 1), (0, 2), (1, 2))
inlet_speed = 0.05
smooth_square = 0.02 * 0.02
F_CONF, F_COL, F_COT, F_UPW, F_G, F_K, F_W, F_R, F_CHI, F_ALL = 0, 6, 7, 12, 18, 21, 27, 30, 31, 32
C_OWN, C_Z, C_ZIN, C_X, C_XIN, C_CONF, C_COL, C_ALL = 0, 1, 4, 5, 8, 9, 15, 16


def dirs_where(axis, sign):
    return tuple(i for i in range(19) if velocities[i][axis] == sign)


def corner_dir(sx, sz):
    return next(i for i in range(19) if velocities[i][0] == sx and velocities[i][2] == sz)


def edge_dirs(axis, sign, other):
    return tuple(i for i in range(19) if velocities[i][axis] == sign and velocities[i][other] == 0)


def stress_of(conf):
    out = []
    for a, b in pairs:
        dot = conf[slot[a, 0]] * conf[slot[0, b]]
        for m in (1, 2):
            dot = dot + conf[slot[a, m]] * conf[slot[m, b]]
        out.append(conf[slot[a, b]] + 0.5 * dot)
    return out


def total(terms):
    result = None
    for sign, value in terms:
        if result is None:
            result = value if sign > 0 else -value
        else:
            result = result + value if sign > 0 else result - value
    return result


def moments(values):
    def weighted(sign_of):
        axial = total([(sign_of(velocities[i]), v) for i, v in values if 0 < i < 7 and sign_of(velocities[i])])
        edge = total([(sign_of(velocities[i]), v) for i, v in values if i >= 7 and sign_of(velocities[i])])
        if axial is None and edge is None:
            return None
        if axial is None:
            return edge * (1.0 / 36.0)
        if edge is None:
            return axial * (1.0 / 18.0)
        return axial * (1.0 / 18.0) + edge * (1.0 / 36.0)

    zeroth = weighted(lambda c: 1)
    rest = [v for i, v in values if i == 0]
    if rest:
        zeroth = zeroth + rest[0] * (1.0 / 3.0)
    first = [weighted(lambda c, a=a: c[a]) for a in range(3)]
    second = [weighted(lambda c, a=a, b=b: c[a] * c[b]) for a, b in pairs]
    return zeroth, first, second


def tensor_of(zeroth, second):
    out = []
    for k in range(6):
        value = None if second[k] is None else 9.0 * second[k]
        if k < 3:
            value = -3.0 * zeroth if value is None else value - 3.0 * zeroth
        out.append(value)
    return out


def apply(tensor, vector):
    out = []
    for a in range(3):
        value = None
        for b in range(3):
            if tensor[slot[a, b]] is not None:
                term = tensor[slot[a, b]] * vector[b]
                value = term if value is None else value + term
        out.append(value)
    return out


def plus(a, b):
    return a if b is None else b if a is None else a + b


def in_y(value, by):
    return value if by == 0 else pltpu.roll(value, (-by) % 128, 1)


def eights(n):
    return 8 * n if isinstance(n, int) else pl.multiple_of(8 * n, 8)


def rows_of(row):
    return jnp.broadcast_to(row, (8, 128))


def kernel(
    pop, col, conf, lab, cot, con,
    o_pop, o_col, o_conf,
    v_pop, v_col, v_conf, v_lab, v_cot, v_con,
    snd, rcv, csnd, crcv,
    x_cot, x_conf, x_col, x_str, x_h, x_up, x_down, z_cot, z_str, z_h, v_u, v_ri,
    in_sem, f_send, f_recv, c_send, c_recv, go_sem,
):
    fields = [(conf, v_conf), (col, v_col), (cot, v_cot), (pop, v_pop), (lab, v_lab), (con, v_con)]

    def load(group, begin, count):
        rows = pl.ds(begin, count)
        return [
            pltpu.make_async_copy(
                src.at[rows] if len(src.shape) == 2 else src.at[:, rows],
                dst.at[rows] if len(dst.shape) == 2 else dst.at[:, rows],
                in_sem.at[group, k],
            )
            for k, (src, dst) in enumerate(fields)
        ]

    outer = load(0, 0, 16) + load(1, 48, 16)
    middle = load(2, 16, 32)
    for copy in outer + middle:
        copy.start()
    nz, nx = lax.axis_size("gz"), lax.axis_size("xy")
    z, x = lax.axis_index("gz"), lax.axis_index("xy")
    z_of = {-1: lax.rem(z + nz - 1, nz), 0: z, 1: lax.rem(z + 1, nz)}
    x_of = {-1: lax.rem(x + nx - 1, nx), 0: x, 1: lax.rem(x + 1, nx)}
    faces = ((0, -1), (0, 1), (2, -1), (2, 1))
    face_device = [(z_of[0], x_of[-1]), (z_of[0], x_of[1]), (z_of[-1], x_of[0]), (z_of[1], x_of[0])]
    corners = ((-1, -1), (-1, 1), (1, -1), (1, 1))
    corner_device = [(z_of[cz], x_of[cx]) for cx, cz in corners]
    place = lax.rem(x, 8)
    upper = lax.rem(lax.div(x, 8), 2)
    edge_x = {-1: place == 0, 0: False, 1: place == 7}
    edge_z = {-1: z == 0, 0: False, 1: z == nz - 1}
    offsets = [((side, 0) if axis == 0 else (0, side)) for axis, side in faces] + list(corners)
    devices = face_device + corner_device
    flip = (1, 0, 3, 2, 7, 6, 5, 4)
    follows, leads, across_x = [], [], []
    for dx, dz in offsets:
        far_x, far_z = edge_x[dx], edge_z[dz]
        level = jnp.logical_and(jnp.minimum(z, z + dz) >= LEVEL[0], jnp.maximum(z, z + dz) <= LEVEL[1])
        far_x_led = jnp.logical_and(far_x, jnp.logical_not(level))
        far = jnp.logical_or(far_x_led, far_z)
        follow = jnp.logical_or(
            jnp.logical_and(far_x_led, upper == 0),
            jnp.logical_and(jnp.logical_and(far_z, jnp.logical_not(far_x)), z == 0),
        )
        follows.append(follow)
        across_x.append(far_x)
        leads.append(jnp.logical_and(far, jnp.logical_not(follow)))
    barrier = pltpu.get_barrier_semaphore()
    expected = jnp.int32(0)
    for device, follow, lead in zip(devices, follows, leads):
        expected = expected + jnp.where(follow, 0, 1)

        @pl.when(jnp.logical_not(lead))
        def _(device=device):
            pl.semaphore_signal(barrier, inc=1, device_id=device, device_id_type=MESH)


    lane = lax.broadcasted_iota(jnp.int32, (8, 128), 0)
    first, last = lane == 0, lane == 7

    def shift(value, by, low=None, high=None):
        if by == 0:
            return value
        rolled = pltpu.roll(value, 7 if by > 0 else 1, 0)
        fill = high if by > 0 else low
        fill = 0.0 if fill is None else fill
        return jnp.where(last if by > 0 else first, fill, rolled)

    def plane(ref, axis, at, k=None):
        rows = pl.ds(8 * at, 8) if axis == 0 else pl.ds(at, 8, stride=8)
        return ref[rows, :] if k is None else ref[k, rows, :]

    def flow_of(load):
        f = [load(i) for i in range(19)]
        rho = f[0]
        for i in range(1, 19):
            rho = rho + f[i]
        inverse = 1.0 / rho
        u = [total([(velocities[i][a], f[i]) for i in range(19) if velocities[i][a]]) * inverse for a in range(3)]
        return rho, inverse, u

    def make_face(index):
        axis, side = faces[index]
        across = 2 - axis
        edge = 7 if side > 0 else 0
        inner = edge - side
        p_edge = [plane(v_conf, axis, edge, k) for k in range(6)]
        p_inner = [plane(v_conf, axis, inner, k) for k in range(6)]
        s_edge, s_inner = stress_of(p_edge), stress_of(p_inner)
        c_edge, c_inner = plane(v_col, axis, edge), plane(v_col, axis, inner)
        _, inverse, u = flow_of(lambda i: plane(v_pop, axis, edge, i))
        ratio = 0.6875 * inverse
        fluid = jnp.where(plane(v_lab, axis, edge) == 0, 1.0, 0.0)
        out = snd.at[index]
        for k in range(6):
            out[F_CONF + k] = p_edge[k]
        out[F_COL] = c_edge
        for j, i in enumerate(dirs_where(axis, -side)):
            out[F_COT + j] = plane(v_cot, axis, edge, i)
        speed = u[axis] * u[axis] + smooth_square
        speed = speed * lax.rsqrt(speed)
        upwind = 0.25 * (speed - side * u[axis])
        for k in range(6):
            out[F_UPW + k] = upwind * plane(v_con, axis, edge, k)
        values = []
        for i in range(19):
            c = velocities[i]
            if c[axis] == side:
                continue
            got = plane(v_cot, axis, edge if c[axis] == 0 else inner, i)
            values.append((i, in_y(shift(got, c[across]), c[1])))
        zeroth, one, two = moments(values)
        tensor = tensor_of(zeroth, two)
        mobility = 1.0 - c_edge * c_edge
        force = []
        for a in range(3):
            k = slot[a, 1]
            value = 0.5 * (in_y(s_edge[k], 1) - in_y(s_edge[k], -1))
            k = slot[a, across]
            value = value + 0.5 * (shift(s_edge[k], 1) - shift(s_edge[k], -1))
            value = value - (0.5 * side) * s_inner[slot[a, axis]]
            if a == 1:
                slope = 0.5 * (in_y(c_edge, 1) - in_y(c_edge, -1))
            elif a == across:
                slope = 0.5 * (shift(c_edge, 1) - shift(c_edge, -1))
            else:
                slope = (-0.5 * side) * c_inner
            force.append(value + mobility * slope)
        for a in range(3):
            out[F_G + a] = one[a]
            out[F_W + a] = u[a] + ratio * force[a]
        for k in range(6):
            out[F_K + k] = tensor[k]
        out[F_R] = ratio
        out[F_CHI] = fluid

    def make_corner(index):
        cx, cz = corners[index]
        ex, ez = (7 if cx > 0 else 0), (7 if cz > 0 else 0)
        here = pl.ds(8 * ex + ez, 1)
        in_x, in_z = pl.ds(8 * (ex - cx) + ez, 1), pl.ds(8 * ex + ez - cz, 1)
        diagonal = corner_dir(-cx, -cz)

        def put(row, value):
            csnd[index, pl.ds(row, 1), :] = value

        put(C_OWN, v_cot[diagonal, here, :])
        for j, i in enumerate(edge_dirs(2, -cz, 0)):
            put(C_Z + j, v_cot[i, here, :])
        put(C_ZIN, v_cot[diagonal, in_x, :])
        for j, i in enumerate(edge_dirs(0, -cx, 2)):
            put(C_X + j, v_cot[i, here, :])
        put(C_XIN, v_cot[diagonal, in_z, :])
        for k in range(6):
            put(C_CONF + k, v_conf[k, here, :])
        put(C_COL, v_col[here, :])

    face_copies = [
        pltpu.make_async_remote_copy(
            src_ref=snd.at[k], dst_ref=rcv.at[k ^ 1], send_sem=f_send.at[k], recv_sem=f_recv.at[k ^ 1],
            device_id=face_device[k], device_id_type=MESH,
        )
        for k in range(4)
    ]
    corner_copies = [
        pltpu.make_async_remote_copy(
            src_ref=csnd.at[k], dst_ref=crcv.at[3 - k], send_sem=c_send.at[k], recv_sem=c_recv.at[3 - k],
            device_id=corner_device[k], device_id_type=MESH,
        )
        for k in range(4)
    ]
    copies = face_copies + corner_copies
    arrival = [copies[k] for k in flip]

    def send(ks):
        for k in ks:

            @pl.when(jnp.logical_not(follows[k]))
            def _(k=k):
                copies[k].start()

    def send_later(ks, over_x):
        for k in ks:

            @pl.when(jnp.logical_and(follows[k], jnp.equal(across_x[k], over_x)))
            def _(k=k):
                pl.semaphore_wait(go_sem.at[k], 1)
                copies[k].start()

    for copy in outer:
        copy.wait()
    make_face(0)
    make_face(1)
    pl.semaphore_wait(barrier, expected)
    for k in range(8):

        @pl.when(leads[k])
        def _(k=k):
            pl.semaphore_signal(go_sem.at[flip[k]], inc=1, device_id=devices[k], device_id_type=MESH)

    send((0, 1))
    for copy in middle:
        copy.wait()
    for index in range(4):
        make_corner(index)
    make_face(2)
    make_face(3)
    send((4, 5, 6, 7, 3, 2))

    def local(at, carry):
        rows, padded = pl.ds(pl.multiple_of(8 * at, 8), 8), pl.ds(pl.multiple_of(8 * at + 8, 8), 8)
        p = [v_conf[k, rows, :] for k in range(6)]
        s = stress_of(p)
        for k in range(6):
            x_conf[k, padded, :] = p[k]
            x_str[k, padded, :] = s[k]
        x_col[padded, :] = v_col[rows, :]
        for i in range(19):
            x_cot[i, padded, :] = v_cot[i, rows, :]
        _, inverse, u = flow_of(lambda i: v_pop[i, rows, :])
        for a in range(3):
            v_u[a, rows, :] = u[a]
        v_ri[rows, :] = inverse
        square = u[0] * u[0] + smooth_square
        speed = square * lax.rsqrt(square)
        up, down = 0.25 * (speed - u[0]), 0.25 * (speed + u[0])
        for k in range(6):
            q = v_con[k, rows, :]
            x_up[k, padded, :] = up * q
            x_down[k, padded, :] = down * q
        return carry

    lax.fori_loop(0, 8, local, 0)

    def z_halo():
        for n, (side, index) in enumerate(((-1, 2), (1, 3))):
            got = rcv.at[index]
            for j, i in enumerate(dirs_where(2, side)):
                z_cot[n, j, pl.ds(8, 8), :] = got[F_COT + j]
            s = stress_of([got[F_CONF + k] for k in range(6)])
            for a in range(3):
                z_str[n, a] = s[slot[a, 2]]

    def x_halo():
        for side, index in ((-1, 0), (1, 1)):
            rows = pl.ds(0 if side < 0 else 72, 8)
            got = rcv.at[index]
            p = [got[F_CONF + k] for k in range(6)]
            s = stress_of(p)
            for k in range(6):
                x_conf[k, rows, :] = p[k]
                x_str[k, rows, :] = s[k]
            x_col[rows, :] = got[F_COL]
            for j, i in enumerate(dirs_where(0, side)):
                x_cot[i, rows, :] = got[F_COT + j]
            for k in range(6):
                (x_up if side < 0 else x_down)[k, rows, :] = got[F_UPW + k]
        for n, side in enumerate((-1, 1)):
            for cx in (-1, 1):
                j = dirs_where(2, side).index(corner_dir(cx, side))
                row = crcv[corners.index((cx, side)), pl.ds(C_OWN, 1), :]
                z_cot[n, j, pl.ds(7 if cx < 0 else 16, 1), :] = row

    def halo_force(index, with_ends):
        axis, side = faces[index]
        across = 2 - axis
        edge = 0 if side < 0 else 7
        got = rcv.at[index]

        def corner_at(end):
            place = (side, end) if axis == 0 else (end, side)
            return corners.index(place)

        ends = {-1: first, 1: last}
        fills = {}
        for end in (-1, 1) if with_ends else ():
            c = corner_at(end)
            p = [crcv[c, pl.ds(C_CONF + k, 1), :] for k in range(6)]
            s = stress_of(p)
            fills[end] = ([s[slot[a, across]] for a in range(3)], crcv[c, pl.ds(C_COL, 1), :])
        c_halo = got[F_COL]
        mobility = 1.0 - c_halo * c_halo

        def at_ends(lo, hi):
            return jnp.where(first, rows_of(-0.5 * lo), jnp.where(last, rows_of(0.5 * hi), 0.0))

        p = [plane(v_conf, axis, edge, k) for k in range(6)]
        s = stress_of(p)
        c_edge = plane(v_col, axis, edge)
        force = []
        for a in range(3):
            value = (-0.5 * side) * s[slot[a, axis]]
            if with_ends:
                value = value + at_ends(fills[-1][0][a], fills[1][0][a])
            if a == axis:
                value = value + mobility * ((-0.5 * side) * c_edge)
            elif a == across and with_ends:
                value = value + mobility * at_ends(fills[-1][1], fills[1][1])
            force.append(value)
        values = []
        for i in dirs_where(axis, -side):
            c = velocities[i]
            value = plane(v_cot, axis, edge, i)
            if c[across]:
                end = c[across]
                if axis == 0:
                    n = 0 if end < 0 else 1
                    j = dirs_where(2, end).index(i)
                    row = z_cot[n, j, pl.ds(8 + edge, 1), :]
                elif with_ends:
                    row = x_cot[i, pl.ds((0 if end < 0 else 72) + edge, 1), :]
                else:
                    row = None
                fill = None if row is None else rows_of(row)
                value = shift(value, end, fill, fill)
            values.append((i, in_y(value, c[1])))
        for end in (-1, 1) if with_ends else ():
            c = corner_at(end)
            base = C_Z if axis == 0 else C_X
            for j, i in enumerate(edge_dirs(across, end, axis)):
                row = crcv[c, pl.ds(base + j, 1), :]
                values.append((i, in_y(jnp.where(ends[end], rows_of(row), 0.0), velocities[i][1])))
            i = corner_dir(side, end) if axis == 0 else corner_dir(end, side)
            row = crcv[c, pl.ds(C_ZIN if axis == 0 else C_XIN, 1), :]
            values.append((i, jnp.where(ends[end], rows_of(row), 0.0)))
        zeroth, one, two = moments(values)
        tensor = tensor_of(zeroth, two)
        one = [plus(one[a], got[F_G + a]) for a in range(3)]
        tensor = [plus(tensor[k], got[F_K + k]) for k in range(6)]
        ratio = got[F_R]
        w = [got[F_W + a] + ratio * force[a] for a in range(3)]
        turned = apply(tensor, w)
        return [got[F_CHI] * (3.0 * one[a] + turned[a]) for a in range(3)]

    def put_halo_force(index, with_ends):
        h = halo_force(index, with_ends)
        for a in range(3):
            if index < 2:
                x_h[a, pl.ds(0 if index == 0 else 72, 8), :] = h[a]
            else:
                z_h[index - 2, a] = h[a]

    def main(at, carry):
        def rows(by=0):
            return pl.ds(eights(at + by), 8)

        def padded(by=0):
            return pl.ds(eights(at + by + 1), 8)

        def z_row(ref, n, k):
            return rows_of(ref[n, k, pl.ds(at, 1), :])

        def face_row(index, k):
            return rows_of(rcv[index, k, pl.ds(at, 1), :])

        label = v_lab[rows(), :]
        fluid = jnp.where(label == 0, 1.0, 0.0)
        solid = label == 1
        inverse = v_ri[rows(), :]
        u = [v_u[a, rows(), :] for a in range(3)]
        colour = x_col[padded(), :]
        mobility = 1.0 - colour * colour
        force = []
        for a in range(3):
            k = slot[a, 0]
            value = x_str[k, padded(1), :] - x_str[k, padded(-1), :]
            k = slot[a, 1]
            here = x_str[k, padded(), :]
            value = value + (in_y(here, 1) - in_y(here, -1))
            here = x_str[slot[a, 2], padded(), :]
            value = value + (shift(here, 1, None, z_row(z_str, 1, a)) - shift(here, -1, z_row(z_str, 0, a), None))
            if a == 0:
                slope = x_col[padded(1), :] - x_col[padded(-1), :]
            elif a == 1:
                slope = in_y(colour, 1) - in_y(colour, -1)
            else:
                slope = shift(colour, 1, None, face_row(3, F_COL)) - shift(colour, -1, face_row(2, F_COL), None)
            force.append(0.5 * (value + mobility * slope))
        values = []
        for i in range(19):
            c = velocities[i]
            value = x_cot[i, padded(c[0]), :]
            if c[2]:
                n = 0 if c[2] < 0 else 1
                row = rows_of(z_cot[n, dirs_where(2, c[2]).index(i), pl.ds(8 + at + c[0], 1), :])
                value = shift(value, c[2], row, row)
            values.append((i, in_y(value, c[1])))
        zeroth, one, two = moments(values)
        tensor = tensor_of(zeroth, two)
        v = [u[a] + 0.5 * inverse * force[a] for a in range(3)]
        turned = apply(tensor, v)
        lean = [3.0 * one[a] + turned[a] for a in range(3)]
        energy = zeroth
        for a in range(3):
            energy = energy + v[a] * (3.0 * one[a] + 0.5 * turned[a])
        other = apply(tensor, force)
        h = [fluid * (lean[a] + (0.1875 * inverse) * other[a]) for a in range(3)]
        pull = [fluid * (1.25 * lean[a] + (0.375 * inverse) * other[a]) for a in range(3)]
        for a in range(3):
            x_h[a, padded(), :] = h[a]
        rho_bar = (1.25 * fluid) * energy
        for a in range(3):
            rho_bar = rho_bar - (0.5 * inverse) * (pull[a] * force[a])
        inlet = (
            (1.0 - 1.5 * inlet_speed * inlet_speed) * zeroth
            + (3.0 * inlet_speed) * one[2]
            + (4.5 * inlet_speed * inlet_speed) * two[2]
        )
        rho_bar = rho_bar + jnp.where(label == 2, inlet, 0.0)
        q = [v_con[k, rows(), :] for k in range(6)]
        m_bar = []
        for a in range(3):
            along = bend = None
            for k in range(6):
                here = x_conf[k, padded(), :]
                if a == 0:
                    up, down = x_conf[k, padded(1), :], x_conf[k, padded(-1), :]
                elif a == 1:
                    up, down = in_y(here, 1), in_y(here, -1)
                else:
                    up = shift(here, 1, None, face_row(3, F_CONF + k))
                    down = shift(here, -1, face_row(2, F_CONF + k), None)
                d, c = q[k] * (up - down), q[k] * (up + down - 2.0 * here)
                along, bend = plus(along, d), plus(bend, c)
            square = u[a] * u[a] + smooth_square
            u_bar = (0.25 * u[a] * lax.rsqrt(square)) * bend - 0.25 * along
            m_bar.append(pull[a] + inverse * u_bar)
        for a in range(3):
            rho_bar = rho_bar - m_bar[a] * u[a]
        keep = -0.25 * fluid
        by_dir = dict(values)
        for i in range(19):
            c = velocities[i]
            value = rho_bar + jnp.where(solid, by_dir[opposite[i]], keep * by_dir[i])
            for a in range(3):
                if c[a]:
                    value = value + m_bar[a] if c[a] > 0 else value - m_bar[a]
            o_pop[i, rows(), :] = value
        return carry


    def finish(at, carry):
        def rows(by=0):
            return pl.ds(eights(at + by), 8)

        def padded(by=0):
            return pl.ds(eights(at + by + 1), 8)

        h = [x_h[a, padded(), :] for a in range(3)]
        u = [v_u[a, rows(), :] for a in range(3)]
        colour = x_col[padded(), :]
        mobility = 1.0 - colour * colour
        t = []
        colour_bar = None
        for a in range(3):
            row_down = rows_of(z_h[0, a, pl.ds(at, 1), :])
            row_up = rows_of(z_h[1, a, pl.ds(at, 1), :])
            t.append(
                [
                    x_h[a, padded(-1), :] - x_h[a, padded(1), :],
                    in_y(h[a], -1) - in_y(h[a], 1),
                    shift(h[a], -1, row_down, None) - shift(h[a], 1, None, row_up),
                ]
            )
        def flux(by):
            near = x_col[padded(by), :]
            return (1.0 - near * near) * x_h[0, padded(by), :]

        up_c, down_c = x_col[padded(1), :], x_col[padded(-1), :]
        z_up_c, z_down_c = rows_of(rcv[3, F_COL, pl.ds(at, 1), :]), rows_of(rcv[2, F_COL, pl.ds(at, 1), :])
        slopes = [
            up_c - down_c,
            in_y(colour, 1) - in_y(colour, -1),
            shift(colour, 1, None, z_up_c) - shift(colour, -1, z_down_c, None),
        ]
        colour_bar = h[0] * slopes[0] + h[1] * slopes[1] + h[2] * slopes[2]
        colour_bar = -colour * colour_bar
        in_z = mobility * h[2]
        z_up_f = (1.0 - z_up_c * z_up_c) * rows_of(z_h[1, 2, pl.ds(at, 1), :])
        z_down_f = (1.0 - z_down_c * z_down_c) * rows_of(z_h[0, 2, pl.ds(at, 1), :])
        flow_y = mobility * h[1]
        spread = (
            (flux(-1) - flux(1))
            + (in_y(flow_y, -1) - in_y(flow_y, 1))
            + (shift(in_z, -1, z_down_f, None) - shift(in_z, 1, None, z_up_f))
        )
        o_col[rows(), :] = colour_bar + 0.5 * spread
        w = []
        for a, b in pairs:
            w.append(0.5 * t[a][a] if a == b else 0.25 * (t[a][b] + t[b][a]))
        p = [x_conf[k, padded(), :] for k in range(6)]
        result = []
        for a, b in pairs:
            dot = None
            for m in range(3):
                if a == b:
                    dot = plus(dot, w[slot[a, m]] * p[slot[m, b]])
                else:
                    dot = plus(dot, w[slot[a, m]] * p[slot[m, b]] + p[slot[a, m]] * w[slot[m, b]])
            result.append(w[slot[a, b]] + dot if a == b else 2.0 * w[slot[a, b]] + dot)
        speeds = []
        for a in range(3):
            square = u[a] * u[a] + smooth_square
            speeds.append(square * lax.rsqrt(square))
        stay = 0.9 - 0.5 * (speeds[0] + speeds[1] + speeds[2])
        go_up = [0.25 * (speeds[a] - u[a]) for a in range(3)]
        go_down = [0.25 * (speeds[a] + u[a]) for a in range(3)]
        for k in range(6):
            q = v_con[k, rows(), :]
            value = result[k] + stay * q
            value = value + in_y(go_up[1] * q, -1) + in_y(go_down[1] * q, 1)
            value = value + shift(go_up[2] * q, -1, rows_of(rcv[2, F_UPW + k, pl.ds(at, 1), :]), None)
            value = value + shift(go_down[2] * q, 1, None, rows_of(rcv[3, F_UPW + k, pl.ds(at, 1), :]))
            value = value + x_up[k, padded(-1), :] + x_down[k, padded(1), :]
            o_conf[k, rows(), :] = value
        return carry

    send_later((2, 3, 4, 5, 6, 7), False)
    send_later((0, 1, 4, 5, 6, 7), True)
    for k in (2, 3):
        arrival[k].wait_recv()
    z_halo()
    put_halo_force(2, False)
    put_halo_force(3, False)
    lax.fori_loop(1, 7, main, 0)
    lax.fori_loop(2, 6, finish, 0)
    for k in (0, 1, 4, 5, 6, 7):
        arrival[k].wait_recv()
    x_halo()
    for index in range(4):
        put_halo_force(index, True)
    for at in (0, 7):
        main(at, 0)
    for at in (0, 1, 6, 7):
        finish(at, 0)
    for copy in copies:
        copy.wait_send()


def deliver(a, b, c, out_a, out_b, out_c, sem):
    copies = [
        pltpu.make_async_copy(src, dst, sem.at[k]) for k, (src, dst) in enumerate(((a, out_a), (b, out_b), (c, out_c)))
    ]
    for copy in copies:
        copy.start()
    for copy in copies:
        copy.wait()


def body(populations, colour, conformation, labels, pop_cotangent, conf_cotangent):
    anywhere = pl.BlockSpec(memory_space=pl.ANY)
    near = pl.BlockSpec(memory_space=pltpu.VMEM)
    args = [
        v.reshape(v.shape[:-3] + (64, 128))
        for v in (populations, colour, conformation, labels, pop_cotangent, conf_cotangent)
    ]
    shapes = [(19, 64, 128), (64, 128), (6, 64, 128)]
    scratch = [pltpu.VMEM(v.shape, v.dtype) for v in args]
    scratch += [pltpu.VMEM((4, F_ALL, 8, 128), F32)] * 2
    scratch += [pltpu.VMEM((4, C_ALL, 128), F32)] * 2
    padded = [(19, 80, 128), (6, 80, 128), (80, 128), (6, 80, 128), (3, 80, 128), (6, 80, 128), (6, 80, 128)]
    scratch += [pltpu.VMEM(s, F32) for s in padded]
    scratch += [pltpu.VMEM(s, F32) for s in [(2, 5, 24, 128), (2, 3, 8, 128), (2, 3, 8, 128), (3, 64, 128), (64, 128)]]
    scratch += [pltpu.SemaphoreType.DMA((3, 6))] + [pltpu.SemaphoreType.DMA((4,))] * 4
    scratch += [pltpu.SemaphoreType.REGULAR((8,))]
    parts = pl.pallas_call(
        kernel,
        out_shape=tuple(pltpu.VMEM(s, F32) for s in shapes),
        in_specs=[anywhere] * 6,
        out_specs=[near] * 3,
        scratch_shapes=scratch,
        compiler_params=pltpu.CompilerParams(
            collective_id=0, has_side_effects=True, vmem_limit_bytes=32 * 1024 * 1024
        ),
    )(*[pltpu.with_memory_space_constraint(v, pltpu.HBM) for v in args])
    parts = [pltpu.with_memory_space_constraint(v, pltpu.VMEM) for v in parts]
    out = pl.pallas_call(
        deliver,
        out_shape=tuple(jax.ShapeDtypeStruct(s, F32) for s in shapes),
        in_specs=[near] * 3,
        out_specs=[anywhere] * 3,
        scratch_shapes=[pltpu.SemaphoreType.DMA((3,))],
    )(*parts)
    return tuple(v.reshape(v.shape[:-2] + (8, 8, 128)) for v in out)


def solution(mesh):
    placed = (
        P(None, "xy", "gz", None),
        P("xy", "gz", None),
        P(None, "xy", "gz", None),
        P("xy", "gz", None),
        P(None, "xy", "gz", None),
        P(None, "xy", "gz", None),
    )
    return jax.shard_map(
        body,
        mesh=mesh,
        in_specs=placed,
        out_specs=(P(None, "xy", "gz", None), P("xy", "gz", None), P(None, "xy", "gz", None)),
        check_vma=False,
    )
```

```python
import functools

import jax
import jax.numpy as jnp
from jax import lax
from jax.experimental import pallas as pl
from jax.experimental.pallas import tpu as pltpu
from jax.sharding import PartitionSpec as P

MESH = pl.DeviceIdType.MESH
F32 = jnp.float32
LEVEL = (5, 6)

velocities = (
    (0, 0, 0),
    (1, 0, 0),
    (-1, 0, 0),
    (0, 1, 0),
    (0, -1, 0),
    (0, 0, 1),
    (0, 0, -1),
    (1, 1, 0),
    (-1, -1, 0),
    (1, -1, 0),
    (-1, 1, 0),
    (1, 0, 1),
    (-1, 0, -1),
    (1, 0, -1),
    (-1, 0, 1),
    (0, 1, 1),
    (0, -1, -1),
    (0, 1, -1),
    (0, -1, 1),
)
opposite = (0, 2, 1, 4, 3, 6, 5, 8, 7, 10, 9, 12, 11, 14, 13, 16, 15, 18, 17)
slot = {(0, 0): 0, (1, 1): 1, (2, 2): 2, (0, 1): 3, (1, 0): 3, (0, 2): 4, (2, 0): 4, (1, 2): 5, (2, 1): 5}
pairs = ((0, 0), (1, 1), (2, 2), (0, 1), (0, 2), (1, 2))
inlet_speed = 0.05
smooth_square = 0.02 * 0.02
F_CONF, F_COL, F_COT, F_UPW, F_G, F_K, F_W, F_R, F_CHI, F_ALL = 0, 6, 7, 12, 18, 21, 27, 30, 31, 32
C_OWN, C_Z, C_ZIN, C_X, C_XIN, C_CONF, C_COL, C_ALL = 0, 1, 4, 5, 8, 9, 15, 16


def dirs_where(axis, sign):
    return tuple(i for i in range(19) if velocities[i][axis] == sign)


def corner_dir(sx, sz):
    return next(i for i in range(19) if velocities[i][0] == sx and velocities[i][2] == sz)


def edge_dirs(axis, sign, other):
    return tuple(i for i in range(19) if velocities[i][axis] == sign and velocities[i][other] == 0)


def stress_of(conf):
    out = []
    for a, b in pairs:
        dot = conf[slot[a, 0]] * conf[slot[0, b]]
        for m in (1, 2):
            dot = dot + conf[slot[a, m]] * conf[slot[m, b]]
        out.append(conf[slot[a, b]] + 0.5 * dot)
    return out


def total(terms):
    result = None
    for sign, value in terms:
        if result is None:
            result = value if sign > 0 else -value
        else:
            result = result + value if sign > 0 else result - value
    return result


def moments(values):
    def weighted(sign_of):
        axial = total([(sign_of(velocities[i]), v) for i, v in values if 0 < i < 7 and sign_of(velocities[i])])
        edge = total([(sign_of(velocities[i]), v) for i, v in values if i >= 7 and sign_of(velocities[i])])
        if axial is None and edge is None:
            return None
        if axial is None:
            return edge * (1.0 / 36.0)
        if edge is None:
            return axial * (1.0 / 18.0)
        return axial * (1.0 / 18.0) + edge * (1.0 / 36.0)

    zeroth = weighted(lambda c: 1)
    rest = [v for i, v in values if i == 0]
    if rest:
        zeroth = zeroth + rest[0] * (1.0 / 3.0)
    first = [weighted(lambda c, a=a: c[a]) for a in range(3)]
    second = [weighted(lambda c, a=a, b=b: c[a] * c[b]) for a, b in pairs]
    return zeroth, first, second


def tensor_of(zeroth, second):
    out = []
    for k in range(6):
        value = None if second[k] is None else 9.0 * second[k]
        if k < 3:
            value = -3.0 * zeroth if value is None else value - 3.0 * zeroth
        out.append(value)
    return out


def apply(tensor, vector):
    out = []
    for a in range(3):
        value = None
        for b in range(3):
            if tensor[slot[a, b]] is not None:
                term = tensor[slot[a, b]] * vector[b]
                value = term if value is None else value + term
        out.append(value)
    return out


def plus(a, b):
    return a if b is None else b if a is None else a + b


def in_y(value, by):
    return value if by == 0 else pltpu.roll(value, (-by) % 128, 1)


def eights(n):
    return 8 * n if isinstance(n, int) else pl.multiple_of(8 * n, 8)


def rows_of(row):
    return jnp.broadcast_to(row, (8, 128))


def kernel(
    pop, col, conf, lab, cot, con,
    o_pop, o_col, o_conf,
    v_pop, v_col, v_conf, v_lab, v_cot, v_con,
    snd, rcv, csnd, crcv,
    x_cot, x_conf, x_col, x_str, x_h, x_up, x_down, z_cot, z_str, z_h, v_u, v_ri,
    in_sem, f_send, f_recv, c_send, c_recv, go_sem,
):
    fields = [(conf, v_conf), (col, v_col), (cot, v_cot), (pop, v_pop), (lab, v_lab), (con, v_con)]

    def load(group, begin, count):
        rows = pl.ds(begin, count)
        return [
            pltpu.make_async_copy(
                src.at[rows] if len(src.shape) == 2 else src.at[:, rows],
                dst.at[rows] if len(dst.shape) == 2 else dst.at[:, rows],
                in_sem.at[group, k],
            )
            for k, (src, dst) in enumerate(fields)
        ]

    outer = load(0, 0, 16) + load(1, 48, 16)
    middle = load(2, 16, 32)
    for copy in outer + middle:
        copy.start()
    nz, nx = lax.axis_size("gz"), lax.axis_size("xy")
    z, x = lax.axis_index("gz"), lax.axis_index("xy")
    z_of = {-1: lax.rem(z + nz - 1, nz), 0: z, 1: lax.rem(z + 1, nz)}
    x_of = {-1: lax.rem(x + nx - 1, nx), 0: x, 1: lax.rem(x + 1, nx)}
    faces = ((0, -1), (0, 1), (2, -1), (2, 1))
    face_device = [(z_of[0], x_of[-1]), (z_of[0], x_of[1]), (z_of[-1], x_of[0]), (z_of[1], x_of[0])]
    corners = ((-1, -1), (-1, 1), (1, -1), (1, 1))
    corner_device = [(z_of[cz], x_of[cx]) for cx, cz in corners]
    place = lax.rem(x, 8)
    upper = lax.rem(lax.div(x, 8), 2)
    edge_x = {-1: place == 0, 0: False, 1: place == 7}
    edge_z = {-1: z == 0, 0: False, 1: z == nz - 1}
    offsets = [((side, 0) if axis == 0 else (0, side)) for axis, side in faces] + list(corners)
    devices = face_device + corner_device
    flip = (1, 0, 3, 2, 7, 6, 5, 4)
    follows, leads, across_x = [], [], []
    for dx, dz in offsets:
        far_x, far_z = edge_x[dx], edge_z[dz]
        level = jnp.logical_and(jnp.minimum(z, z + dz) >= LEVEL[0], jnp.maximum(z, z + dz) <= LEVEL[1])
        far_x_led = jnp.logical_and(far_x, jnp.logical_not(level))
        far = jnp.logical_or(far_x_led, far_z)
        follow = jnp.logical_or(
            jnp.logical_and(far_x_led, upper == 0),
            jnp.logical_and(jnp.logical_and(far_z, jnp.logical_not(far_x)), z == 0),
        )
        follows.append(follow)
        across_x.append(far_x)
        leads.append(jnp.logical_and(far, jnp.logical_not(follow)))
    barrier = pltpu.get_barrier_semaphore()
    expected = jnp.int32(0)
    for device, follow, lead in zip(devices, follows, leads):
        expected = expected + jnp.where(follow, 0, 1)

        @pl.when(jnp.logical_not(lead))
        def _(device=device):
            pl.semaphore_signal(barrier, inc=1, device_id=device, device_id_type=MESH)


    lane = lax.broadcasted_iota(jnp.int32, (8, 128), 0)
    first, last = lane == 0, lane == 7

    def shift(value, by, low=None, high=None):
        if by == 0:
            return value
        rolled = pltpu.roll(value, 7 if by > 0 else 1, 0)
        fill = high if by > 0 else low
        fill = 0.0 if fill is None else fill
        return jnp.where(last if by > 0 else first, fill, rolled)

    def plane(ref, axis, at, k=None):
        rows = pl.ds(8 * at, 8) if axis == 0 else pl.ds(at, 8, stride=8)
        return ref[rows, :] if k is None else ref[k, rows, :]

    def flow_of(load):
        f = [load(i) for i in range(19)]
        rho = f[0]
        for i in range(1, 19):
            rho = rho + f[i]
        inverse = 1.0 / rho
        u = [total([(velocities[i][a], f[i]) for i in range(19) if velocities[i][a]]) * inverse for a in range(3)]
        return rho, inverse, u

    def make_face(index):
        axis, side = faces[index]
        across = 2 - axis
        edge = 7 if side > 0 else 0
        inner = edge - side
        p_edge = [plane(v_conf, axis, edge, k) for k in range(6)]
        p_inner = [plane(v_conf, axis, inner, k) for k in range(6)]
        s_edge, s_inner = stress_of(p_edge), stress_of(p_inner)
        c_edge, c_inner = plane(v_col, axis, edge), plane(v_col, axis, inner)
        _, inverse, u = flow_of(lambda i: plane(v_pop, axis, edge, i))
        ratio = 0.6875 * inverse
        fluid = jnp.where(plane(v_lab, axis, edge) == 0, 1.0, 0.0)
        out = snd.at[index]
        for k in range(6):
            out[F_CONF + k] = p_edge[k]
        out[F_COL] = c_edge
        for j, i in enumerate(dirs_where(axis, -side)):
            out[F_COT + j] = plane(v_cot, axis, edge, i)
        speed = u[axis] * u[axis] + smooth_square
        speed = speed * lax.rsqrt(speed)
        upwind = 0.25 * (speed - side * u[axis])
        for k in range(6):
            out[F_UPW + k] = upwind * plane(v_con, axis, edge, k)
        values = []
        for i in range(19):
            c = velocities[i]
            if c[axis] == side:
                continue
            got = plane(v_cot, axis, edge if c[axis] == 0 else inner, i)
            values.append((i, in_y(shift(got, c[across]), c[1])))
        zeroth, one, two = moments(values)
        tensor = tensor_of(zeroth, two)
        mobility = 1.0 - c_edge * c_edge
        force = []
        for a in range(3):
            k = slot[a, 1]
            value = 0.5 * (in_y(s_edge[k], 1) - in_y(s_edge[k], -1))
            k = slot[a, across]
            value = value + 0.5 * (shift(s_edge[k], 1) - shift(s_edge[k], -1))
            value = value - (0.5 * side) * s_inner[slot[a, axis]]
            if a == 1:
                slope = 0.5 * (in_y(c_edge, 1) - in_y(c_edge, -1))
            elif a == across:
                slope = 0.5 * (shift(c_edge, 1) - shift(c_edge, -1))
            else:
                slope = (-0.5 * side) * c_inner
            force.append(value + mobility * slope)
        for a in range(3):
            out[F_G + a] = one[a]
            out[F_W + a] = u[a] + ratio * force[a]
        for k in range(6):
            out[F_K + k] = tensor[k]
        out[F_R] = ratio
        out[F_CHI] = fluid

    def make_corner(index):
        cx, cz = corners[index]
        ex, ez = (7 if cx > 0 else 0), (7 if cz > 0 else 0)
        here = pl.ds(8 * ex + ez, 1)
        in_x, in_z = pl.ds(8 * (ex - cx) + ez, 1), pl.ds(8 * ex + ez - cz, 1)
        diagonal = corner_dir(-cx, -cz)

        def put(row, value):
            csnd[index, pl.ds(row, 1), :] = value

        put(C_OWN, v_cot[diagonal, here, :])
        for j, i in enumerate(edge_dirs(2, -cz, 0)):
            put(C_Z + j, v_cot[i, here, :])
        put(C_ZIN, v_cot[diagonal, in_x, :])
        for j, i in enumerate(edge_dirs(0, -cx, 2)):
            put(C_X + j, v_cot[i, here, :])
        put(C_XIN, v_cot[diagonal, in_z, :])
        for k in range(6):
            put(C_CONF + k, v_conf[k, here, :])
        put(C_COL, v_col[here, :])

    face_copies = [
        pltpu.make_async_remote_copy(
            src_ref=snd.at[k], dst_ref=rcv.at[k ^ 1], send_sem=f_send.at[k], recv_sem=f_recv.at[k ^ 1],
            device_id=face_device[k], device_id_type=MESH,
        )
        for k in range(4)
    ]
    corner_copies = [
        pltpu.make_async_remote_copy(
            src_ref=csnd.at[k], dst_ref=crcv.at[3 - k], send_sem=c_send.at[k], recv_sem=c_recv.at[3 - k],
            device_id=corner_device[k], device_id_type=MESH,
        )
        for k in range(4)
    ]
    copies = face_copies + corner_copies
    arrival = [copies[k] for k in flip]

    def send(ks):
        for k in ks:

            @pl.when(jnp.logical_not(follows[k]))
            def _(k=k):
                copies[k].start()

    def send_later(ks, over_x):
        for k in ks:

            @pl.when(jnp.logical_and(follows[k], jnp.equal(across_x[k], over_x)))
            def _(k=k):
                pl.semaphore_wait(go_sem.at[k], 1)
                copies[k].start()

    for copy in outer:
        copy.wait()
    for index in range(4):
        make_corner(index)
    make_face(0)
    make_face(1)
    pl.semaphore_wait(barrier, expected)
    for k in range(8):

        @pl.when(leads[k])
        def _(k=k):
            pl.semaphore_signal(go_sem.at[flip[k]], inc=1, device_id=devices[k], device_id_type=MESH)

    send((4, 5, 6, 7, 0, 1))
    for copy in middle:
        copy.wait()
    make_face(2)
    make_face(3)
    send((3, 2))

    def local(at, carry):
        rows, padded = pl.ds(pl.multiple_of(8 * at, 8), 8), pl.ds(pl.multiple_of(8 * at + 8, 8), 8)
        p = [v_conf[k, rows, :] for k in range(6)]
        s = stress_of(p)
        for k in range(6):
            x_conf[k, padded, :] = p[k]
            x_str[k, padded, :] = s[k]
        x_col[padded, :] = v_col[rows, :]
        for i in range(19):
            x_cot[i, padded, :] = v_cot[i, rows, :]
        _, inverse, u = flow_of(lambda i: v_pop[i, rows, :])
        for a in range(3):
            v_u[a, rows, :] = u[a]
        v_ri[rows, :] = inverse
        square = u[0] * u[0] + smooth_square
        speed = square * lax.rsqrt(square)
        up, down = 0.25 * (speed - u[0]), 0.25 * (speed + u[0])
        for k in range(6):
            q = v_con[k, rows, :]
            x_up[k, padded, :] = up * q
            x_down[k, padded, :] = down * q
        return carry

    lax.fori_loop(0, 8, local, 0)

    def z_halo():
        for n, (side, index) in enumerate(((-1, 2), (1, 3))):
            got = rcv.at[index]
            for j, i in enumerate(dirs_where(2, side)):
                z_cot[n, j, pl.ds(8, 8), :] = got[F_COT + j]
            s = stress_of([got[F_CONF + k] for k in range(6)])
            for a in range(3):
                z_str[n, a] = s[slot[a, 2]]

    def x_halo(side):
        index = 0 if side < 0 else 1
        rows = pl.ds(0 if side < 0 else 72, 8)
        got = rcv.at[index]
        p = [got[F_CONF + k] for k in range(6)]
        s = stress_of(p)
        for k in range(6):
            x_conf[k, rows, :] = p[k]
            x_str[k, rows, :] = s[k]
            (x_up if side < 0 else x_down)[k, rows, :] = got[F_UPW + k]
        x_col[rows, :] = got[F_COL]
        for j, i in enumerate(dirs_where(0, side)):
            x_cot[i, rows, :] = got[F_COT + j]
        for n, z_side in enumerate((-1, 1)):
            j = dirs_where(2, z_side).index(corner_dir(side, z_side))
            row = crcv[corners.index((side, z_side)), pl.ds(C_OWN, 1), :]
            z_cot[n, j, pl.ds(7 if side < 0 else 16, 1), :] = row

    def halo_force(index, given):
        axis, side = faces[index]
        across = 2 - axis
        edge = 0 if side < 0 else 7
        got = rcv.at[index]

        def corner_at(end):
            place = (side, end) if axis == 0 else (end, side)
            return corners.index(place)

        ends = {-1: first, 1: last}
        fills = {}
        for end in given:
            c = corner_at(end)
            p = [crcv[c, pl.ds(C_CONF + k, 1), :] for k in range(6)]
            s = stress_of(p)
            fills[end] = ([s[slot[a, across]] for a in range(3)], crcv[c, pl.ds(C_COL, 1), :])
        c_halo = got[F_COL]
        mobility = 1.0 - c_halo * c_halo

        def at_ends(pick):
            value = 0.0
            for end in given:
                value = jnp.where(ends[end], rows_of((0.5 * end) * pick(fills[end])), value)
            return value

        p = [plane(v_conf, axis, edge, k) for k in range(6)]
        s = stress_of(p)
        c_edge = plane(v_col, axis, edge)
        force = []
        for a in range(3):
            value = (-0.5 * side) * s[slot[a, axis]]
            if given:
                value = value + at_ends(lambda fill: fill[0][a])
            if a == axis:
                value = value + mobility * ((-0.5 * side) * c_edge)
            elif a == across and given:
                value = value + mobility * at_ends(lambda fill: fill[1])
            force.append(value)
        values = []
        for i in dirs_where(axis, -side):
            c = velocities[i]
            value = plane(v_cot, axis, edge, i)
            if c[across]:
                end = c[across]
                if axis == 0:
                    n = 0 if end < 0 else 1
                    j = dirs_where(2, end).index(i)
                    row = z_cot[n, j, pl.ds(8 + edge, 1), :]
                elif end in given:
                    row = x_cot[i, pl.ds((0 if end < 0 else 72) + edge, 1), :]
                else:
                    row = None
                fill = None if row is None else rows_of(row)
                value = shift(value, end, fill, fill)
            values.append((i, in_y(value, c[1])))
        for end in given:
            c = corner_at(end)
            base = C_Z if axis == 0 else C_X
            for j, i in enumerate(edge_dirs(across, end, axis)):
                row = crcv[c, pl.ds(base + j, 1), :]
                values.append((i, in_y(jnp.where(ends[end], rows_of(row), 0.0), velocities[i][1])))
            i = corner_dir(side, end) if axis == 0 else corner_dir(end, side)
            row = crcv[c, pl.ds(C_ZIN if axis == 0 else C_XIN, 1), :]
            values.append((i, jnp.where(ends[end], rows_of(row), 0.0)))
        zeroth, one, two = moments(values)
        tensor = tensor_of(zeroth, two)
        one = [plus(one[a], got[F_G + a]) for a in range(3)]
        tensor = [plus(tensor[k], got[F_K + k]) for k in range(6)]
        ratio = got[F_R]
        w = [got[F_W + a] + ratio * force[a] for a in range(3)]
        turned = apply(tensor, w)
        return [got[F_CHI] * (3.0 * one[a] + turned[a]) for a in range(3)]

    def put_halo_force(index, given):
        h = halo_force(index, given)
        for a in range(3):
            if index < 2:
                x_h[a, pl.ds(0 if index == 0 else 72, 8), :] = h[a]
            else:
                z_h[index - 2, a] = h[a]

    def main(at, carry):
        def rows(by=0):
            return pl.ds(eights(at + by), 8)

        def padded(by=0):
            return pl.ds(eights(at + by + 1), 8)

        def z_row(ref, n, k):
            return rows_of(ref[n, k, pl.ds(at, 1), :])

        def face_row(index, k):
            return rows_of(rcv[index, k, pl.ds(at, 1), :])

        label = v_lab[rows(), :]
        fluid = jnp.where(label == 0, 1.0, 0.0)
        solid = label == 1
        inverse = v_ri[rows(), :]
        u = [v_u[a, rows(), :] for a in range(3)]
        colour = x_col[padded(), :]
        mobility = 1.0 - colour * colour
        force = []
        for a in range(3):
            k = slot[a, 0]
            value = x_str[k, padded(1), :] - x_str[k, padded(-1), :]
            k = slot[a, 1]
            here = x_str[k, padded(), :]
            value = value + (in_y(here, 1) - in_y(here, -1))
            here = x_str[slot[a, 2], padded(), :]
            value = value + (shift(here, 1, None, z_row(z_str, 1, a)) - shift(here, -1, z_row(z_str, 0, a), None))
            if a == 0:
                slope = x_col[padded(1), :] - x_col[padded(-1), :]
            elif a == 1:
                slope = in_y(colour, 1) - in_y(colour, -1)
            else:
                slope = shift(colour, 1, None, face_row(3, F_COL)) - shift(colour, -1, face_row(2, F_COL), None)
            force.append(0.5 * (value + mobility * slope))
        values = []
        for i in range(19):
            c = velocities[i]
            value = x_cot[i, padded(c[0]), :]
            if c[2]:
                n = 0 if c[2] < 0 else 1
                row = rows_of(z_cot[n, dirs_where(2, c[2]).index(i), pl.ds(8 + at + c[0], 1), :])
                value = shift(value, c[2], row, row)
            values.append((i, in_y(value, c[1])))
        zeroth, one, two = moments(values)
        tensor = tensor_of(zeroth, two)
        v = [u[a] + 0.5 * inverse * force[a] for a in range(3)]
        turned = apply(tensor, v)
        lean = [3.0 * one[a] + turned[a] for a in range(3)]
        energy = zeroth
        for a in range(3):
            energy = energy + v[a] * (3.0 * one[a] + 0.5 * turned[a])
        other = apply(tensor, force)
        h = [fluid * (lean[a] + (0.1875 * inverse) * other[a]) for a in range(3)]
        pull = [fluid * (1.25 * lean[a] + (0.375 * inverse) * other[a]) for a in range(3)]
        for a in range(3):
            x_h[a, padded(), :] = h[a]
        rho_bar = (1.25 * fluid) * energy
        for a in range(3):
            rho_bar = rho_bar - (0.5 * inverse) * (pull[a] * force[a])
        inlet = (
            (1.0 - 1.5 * inlet_speed * inlet_speed) * zeroth
            + (3.0 * inlet_speed) * one[2]
            + (4.5 * inlet_speed * inlet_speed) * two[2]
        )
        rho_bar = rho_bar + jnp.where(label == 2, inlet, 0.0)
        q = [v_con[k, rows(), :] for k in range(6)]
        m_bar = []
        for a in range(3):
            along = bend = None
            for k in range(6):
                here = x_conf[k, padded(), :]
                if a == 0:
                    up, down = x_conf[k, padded(1), :], x_conf[k, padded(-1), :]
                elif a == 1:
                    up, down = in_y(here, 1), in_y(here, -1)
                else:
                    up = shift(here, 1, None, face_row(3, F_CONF + k))
                    down = shift(here, -1, face_row(2, F_CONF + k), None)
                d, c = q[k] * (up - down), q[k] * (up + down - 2.0 * here)
                along, bend = plus(along, d), plus(bend, c)
            square = u[a] * u[a] + smooth_square
            u_bar = (0.25 * u[a] * lax.rsqrt(square)) * bend - 0.25 * along
            m_bar.append(pull[a] + inverse * u_bar)
        for a in range(3):
            rho_bar = rho_bar - m_bar[a] * u[a]
        keep = -0.25 * fluid
        by_dir = dict(values)
        for i in range(19):
            c = velocities[i]
            value = rho_bar + jnp.where(solid, by_dir[opposite[i]], keep * by_dir[i])
            for a in range(3):
                if c[a]:
                    value = value + m_bar[a] if c[a] > 0 else value - m_bar[a]
            o_pop[i, rows(), :] = value
        return carry


    def finish(at, carry):
        def rows(by=0):
            return pl.ds(eights(at + by), 8)

        def padded(by=0):
            return pl.ds(eights(at + by + 1), 8)

        h = [x_h[a, padded(), :] for a in range(3)]
        u = [v_u[a, rows(), :] for a in range(3)]
        colour = x_col[padded(), :]
        mobility = 1.0 - colour * colour
        t = []
        colour_bar = None
        for a in range(3):
            row_down = rows_of(z_h[0, a, pl.ds(at, 1), :])
            row_up = rows_of(z_h[1, a, pl.ds(at, 1), :])
            t.append(
                [
                    x_h[a, padded(-1), :] - x_h[a, padded(1), :],
                    in_y(h[a], -1) - in_y(h[a], 1),
                    shift(h[a], -1, row_down, None) - shift(h[a], 1, None, row_up),
                ]
            )
        def flux(by):
            near = x_col[padded(by), :]
            return (1.0 - near * near) * x_h[0, padded(by), :]

        up_c, down_c = x_col[padded(1), :], x_col[padded(-1), :]
        z_up_c, z_down_c = rows_of(rcv[3, F_COL, pl.ds(at, 1), :]), rows_of(rcv[2, F_COL, pl.ds(at, 1), :])
        slopes = [
            up_c - down_c,
            in_y(colour, 1) - in_y(colour, -1),
            shift(colour, 1, None, z_up_c) - shift(colour, -1, z_down_c, None),
        ]
        colour_bar = h[0] * slopes[0] + h[1] * slopes[1] + h[2] * slopes[2]
        colour_bar = -colour * colour_bar
        in_z = mobility * h[2]
        z_up_f = (1.0 - z_up_c * z_up_c) * rows_of(z_h[1, 2, pl.ds(at, 1), :])
        z_down_f = (1.0 - z_down_c * z_down_c) * rows_of(z_h[0, 2, pl.ds(at, 1), :])
        flow_y = mobility * h[1]
        spread = (
            (flux(-1) - flux(1))
            + (in_y(flow_y, -1) - in_y(flow_y, 1))
            + (shift(in_z, -1, z_down_f, None) - shift(in_z, 1, None, z_up_f))
        )
        o_col[rows(), :] = colour_bar + 0.5 * spread
        w = []
        for a, b in pairs:
            w.append(0.5 * t[a][a] if a == b else 0.25 * (t[a][b] + t[b][a]))
        p = [x_conf[k, padded(), :] for k in range(6)]
        result = []
        for a, b in pairs:
            dot = None
            for m in range(3):
                if a == b:
                    dot = plus(dot, w[slot[a, m]] * p[slot[m, b]])
                else:
                    dot = plus(dot, w[slot[a, m]] * p[slot[m, b]] + p[slot[a, m]] * w[slot[m, b]])
            result.append(w[slot[a, b]] + dot if a == b else 2.0 * w[slot[a, b]] + dot)
        speeds = []
        for a in range(3):
            square = u[a] * u[a] + smooth_square
            speeds.append(square * lax.rsqrt(square))
        stay = 0.9 - 0.5 * (speeds[0] + speeds[1] + speeds[2])
        go_up = [0.25 * (speeds[a] - u[a]) for a in range(3)]
        go_down = [0.25 * (speeds[a] + u[a]) for a in range(3)]
        for k in range(6):
            q = v_con[k, rows(), :]
            value = result[k] + stay * q
            value = value + in_y(go_up[1] * q, -1) + in_y(go_down[1] * q, 1)
            value = value + shift(go_up[2] * q, -1, rows_of(rcv[2, F_UPW + k, pl.ds(at, 1), :]), None)
            value = value + shift(go_down[2] * q, 1, None, rows_of(rcv[3, F_UPW + k, pl.ds(at, 1), :]))
            value = value + x_up[k, padded(-1), :] + x_down[k, padded(1), :]
            o_conf[k, rows(), :] = value
        return carry

    send_later((4, 5, 6, 7, 2, 3), False)
    send_later((0, 1, 4, 5, 6, 7), True)
    for k in (2, 3):
        arrival[k].wait_recv()
    z_halo()
    put_halo_force(2, ())
    put_halo_force(3, ())
    lax.fori_loop(1, 7, main, 0)
    lax.fori_loop(2, 6, finish, 0)

    def visit(turn, carry):
        early = jnp.where(place == 0, 1, 0)
        now = jnp.where(turn == 0, early, 1 - early)
        for index, side in enumerate((-1, 1)):

            @pl.when(now == index)
            def _(index=index, side=side):
                for k in (index, 4 + corners.index((side, -1)), 4 + corners.index((side, 1))):
                    arrival[k].wait_recv()
                x_halo(side)
                put_halo_force(index, (-1, 1))
                put_halo_force(2, (side,))
                put_halo_force(3, (side,))
                edge = 0 if side < 0 else 7
                main(edge, 0)
                finish(edge, 0)
                finish(edge - side, 0)

        return carry

    lax.fori_loop(0, 2, visit, 0)
    for copy in copies:
        copy.wait_send()


def deliver(a, b, c, out_a, out_b, out_c, sem):
    copies = [
        pltpu.make_async_copy(src, dst, sem.at[k]) for k, (src, dst) in enumerate(((a, out_a), (b, out_b), (c, out_c)))
    ]
    for copy in copies:
        copy.start()
    for copy in copies:
        copy.wait()


def body(populations, colour, conformation, labels, pop_cotangent, conf_cotangent):
    anywhere = pl.BlockSpec(memory_space=pl.ANY)
    near = pl.BlockSpec(memory_space=pltpu.VMEM)
    args = [
        v.reshape(v.shape[:-3] + (64, 128))
        for v in (populations, colour, conformation, labels, pop_cotangent, conf_cotangent)
    ]
    shapes = [(19, 64, 128), (64, 128), (6, 64, 128)]
    scratch = [pltpu.VMEM(v.shape, v.dtype) for v in args]
    scratch += [pltpu.VMEM((4, F_ALL, 8, 128), F32)] * 2
    scratch += [pltpu.VMEM((4, C_ALL, 128), F32)] * 2
    padded = [(19, 80, 128), (6, 80, 128), (80, 128), (6, 80, 128), (3, 80, 128), (6, 80, 128), (6, 80, 128)]
    scratch += [pltpu.VMEM(s, F32) for s in padded]
    scratch += [pltpu.VMEM(s, F32) for s in [(2, 5, 24, 128), (2, 3, 8, 128), (2, 3, 8, 128), (3, 64, 128), (64, 128)]]
    scratch += [pltpu.SemaphoreType.DMA((3, 6))] + [pltpu.SemaphoreType.DMA((4,))] * 4
    scratch += [pltpu.SemaphoreType.REGULAR((8,))]
    parts = pl.pallas_call(
        kernel,
        out_shape=tuple(pltpu.VMEM(s, F32) for s in shapes),
        in_specs=[anywhere] * 6,
        out_specs=[near] * 3,
        scratch_shapes=scratch,
        compiler_params=pltpu.CompilerParams(
            collective_id=0, has_side_effects=True, vmem_limit_bytes=32 * 1024 * 1024
        ),
    )(*[pltpu.with_memory_space_constraint(v, pltpu.HBM) for v in args])
    parts = [pltpu.with_memory_space_constraint(v, pltpu.VMEM) for v in parts]
    out = pl.pallas_call(
        deliver,
        out_shape=tuple(jax.ShapeDtypeStruct(s, F32) for s in shapes),
        in_specs=[near] * 3,
        out_specs=[anywhere] * 3,
        scratch_shapes=[pltpu.SemaphoreType.DMA((3,))],
    )(*parts)
    return tuple(v.reshape(v.shape[:-2] + (8, 8, 128)) for v in out)


def solution(mesh):
    placed = (
        P(None, "xy", "gz", None),
        P("xy", "gz", None),
        P(None, "xy", "gz", None),
        P("xy", "gz", None),
        P(None, "xy", "gz", None),
        P(None, "xy", "gz", None),
    )
    return jax.shard_map(
        body,
        mesh=mesh,
        in_specs=placed,
        out_specs=(P(None, "xy", "gz", None), P("xy", "gz", None), P(None, "xy", "gz", None)),
        check_vma=False,
    )
```

```python
import functools

import jax
import jax.numpy as jnp
from jax import lax
from jax.experimental import pallas as pl
from jax.experimental.pallas import tpu as pltpu
from jax.sharding import PartitionSpec as P

MESH = pl.DeviceIdType.MESH
F32 = jnp.float32
LEVEL = (5, 6)
DIRECT = 19

velocities = (
    (0, 0, 0),
    (1, 0, 0),
    (-1, 0, 0),
    (0, 1, 0),
    (0, -1, 0),
    (0, 0, 1),
    (0, 0, -1),
    (1, 1, 0),
    (-1, -1, 0),
    (1, -1, 0),
    (-1, 1, 0),
    (1, 0, 1),
    (-1, 0, -1),
    (1, 0, -1),
    (-1, 0, 1),
    (0, 1, 1),
    (0, -1, -1),
    (0, 1, -1),
    (0, -1, 1),
)
opposite = (0, 2, 1, 4, 3, 6, 5, 8, 7, 10, 9, 12, 11, 14, 13, 16, 15, 18, 17)
slot = {(0, 0): 0, (1, 1): 1, (2, 2): 2, (0, 1): 3, (1, 0): 3, (0, 2): 4, (2, 0): 4, (1, 2): 5, (2, 1): 5}
pairs = ((0, 0), (1, 1), (2, 2), (0, 1), (0, 2), (1, 2))
inlet_speed = 0.05
smooth_square = 0.02 * 0.02
F_CONF, F_COL, F_COT, F_UPW, F_G, F_K, F_W, F_R, F_CHI, F_ALL = 0, 6, 7, 12, 18, 21, 27, 30, 31, 32
C_OWN, C_Z, C_ZIN, C_X, C_XIN, C_CONF, C_COL, C_ALL = 0, 1, 4, 5, 8, 9, 15, 16


def dirs_where(axis, sign):
    return tuple(i for i in range(19) if velocities[i][axis] == sign)


def corner_dir(sx, sz):
    return next(i for i in range(19) if velocities[i][0] == sx and velocities[i][2] == sz)


def edge_dirs(axis, sign, other):
    return tuple(i for i in range(19) if velocities[i][axis] == sign and velocities[i][other] == 0)


def stress_of(conf):
    out = []
    for a, b in pairs:
        dot = conf[slot[a, 0]] * conf[slot[0, b]]
        for m in (1, 2):
            dot = dot + conf[slot[a, m]] * conf[slot[m, b]]
        out.append(conf[slot[a, b]] + 0.5 * dot)
    return out


def total(terms):
    result = None
    for sign, value in terms:
        if result is None:
            result = value if sign > 0 else -value
        else:
            result = result + value if sign > 0 else result - value
    return result


def moments(values):
    def weighted(sign_of):
        axial = total([(sign_of(velocities[i]), v) for i, v in values if 0 < i < 7 and sign_of(velocities[i])])
        edge = total([(sign_of(velocities[i]), v) for i, v in values if i >= 7 and sign_of(velocities[i])])
        if axial is None and edge is None:
            return None
        if axial is None:
            return edge * (1.0 / 36.0)
        if edge is None:
            return axial * (1.0 / 18.0)
        return axial * (1.0 / 18.0) + edge * (1.0 / 36.0)

    zeroth = weighted(lambda c: 1)
    rest = [v for i, v in values if i == 0]
    if rest:
        zeroth = zeroth + rest[0] * (1.0 / 3.0)
    first = [weighted(lambda c, a=a: c[a]) for a in range(3)]
    second = [weighted(lambda c, a=a, b=b: c[a] * c[b]) for a, b in pairs]
    return zeroth, first, second


def tensor_of(zeroth, second):
    out = []
    for k in range(6):
        value = None if second[k] is None else 9.0 * second[k]
        if k < 3:
            value = -3.0 * zeroth if value is None else value - 3.0 * zeroth
        out.append(value)
    return out


def apply(tensor, vector):
    out = []
    for a in range(3):
        value = None
        for b in range(3):
            if tensor[slot[a, b]] is not None:
                term = tensor[slot[a, b]] * vector[b]
                value = term if value is None else value + term
        out.append(value)
    return out


def plus(a, b):
    return a if b is None else b if a is None else a + b


def in_y(value, by):
    return value if by == 0 else pltpu.roll(value, (-by) % 128, 1)


def eights(n):
    return 8 * n if isinstance(n, int) else pl.multiple_of(8 * n, 8)


def rows_of(row):
    return jnp.broadcast_to(row, (8, 128))


def kernel(
    pop, col, conf, lab, cot, con,
    o_pop, o_col, o_conf,
    v_pop, v_col, v_conf, v_lab, v_cot, v_con,
    snd, rcv, csnd, crcv,
    x_cot, x_conf, x_col, x_str, x_h, x_up, x_down, z_cot, z_str, z_h, v_u, v_ri,
    held, in_sem, f_send, f_recv, c_send, c_recv, go_sem, r_send, r_recv, h_send, h_recv, h_go,
):
    fields = [(conf, v_conf), (col, v_col), (cot, v_cot), (pop, v_pop), (lab, v_lab), (con, v_con)]

    def load(group, begin, count):
        rows = pl.ds(begin, count)
        return [
            pltpu.make_async_copy(
                src.at[rows] if len(src.shape) == 2 else src.at[:, rows],
                dst.at[rows] if len(dst.shape) == 2 else dst.at[:, rows],
                in_sem.at[group, k],
            )
            for k, (src, dst) in enumerate(fields)
        ]

    outer = load(0, 0, 16) + load(1, 48, 16)
    middle = load(2, 16, 32)
    for copy in outer + middle:
        copy.start()
    nz, nx = lax.axis_size("gz"), lax.axis_size("xy")
    z, x = lax.axis_index("gz"), lax.axis_index("xy")
    z_of = {-1: lax.rem(z + nz - 1, nz), 0: z, 1: lax.rem(z + 1, nz)}
    x_of = {-1: lax.rem(x + nx - 1, nx), 0: x, 1: lax.rem(x + 1, nx)}
    faces = ((0, -1), (0, 1), (2, -1), (2, 1))
    face_device = [(z_of[0], x_of[-1]), (z_of[0], x_of[1]), (z_of[-1], x_of[0]), (z_of[1], x_of[0])]
    corners = ((-1, -1), (-1, 1), (1, -1), (1, 1))
    corner_device = [(z_of[cz], x_of[cx]) for cx, cz in corners]
    place = lax.rem(x, 8)
    upper = lax.rem(lax.div(x, 8), 2)
    edge_x = {-1: place == 0, 0: False, 1: place == 7}
    edge_z = {-1: z == 0, 0: False, 1: z == nz - 1}
    offsets = [((side, 0) if axis == 0 else (0, side)) for axis, side in faces] + list(corners)
    devices = face_device + corner_device
    flip = (1, 0, 3, 2, 7, 6, 5, 4)
    follows, leads, across_x = [], [], []
    for dx, dz in offsets:
        far_x, far_z = edge_x[dx], edge_z[dz]
        level = jnp.logical_and(jnp.minimum(z, z + dz) >= LEVEL[0], jnp.maximum(z, z + dz) <= LEVEL[1])
        far_x_led = jnp.logical_and(far_x, jnp.logical_not(level))
        far = jnp.logical_or(far_x_led, far_z)
        follow = jnp.logical_or(
            jnp.logical_and(far_x_led, upper == 0),
            jnp.logical_and(jnp.logical_and(far_z, jnp.logical_not(far_x)), z == 0),
        )
        follows.append(follow)
        across_x.append(far_x)
        leads.append(jnp.logical_and(far, jnp.logical_not(follow)))
    barrier = pltpu.get_barrier_semaphore()
    expected = jnp.int32(0)
    for device, follow, lead in zip(devices, follows, leads):
        expected = expected + jnp.where(follow, 0, 1)

        @pl.when(jnp.logical_not(lead))
        def _(device=device):
            pl.semaphore_signal(barrier, inc=1, device_id=device, device_id_type=MESH)

    def along(by):
        return (z, lax.rem(x + by + nx, nx))

    def relay_of(k):
        return along(2 if k == 0 else -2)

    def far_relay_of(k):
        return along(-3 if k == 0 else 3)

    serves = {0: place == 2, 1: place == 5}
    owner = {0: along(-2), 1: along(2)}
    target = {0: along(-3), 1: along(3)}
    level_here = jnp.logical_and(z >= LEVEL[0], z <= LEVEL[1])
    owner_follows = jnp.logical_and(upper == 0, jnp.logical_not(level_here))
    owner_leads = jnp.logical_and(upper == 1, jnp.logical_not(level_here))
    is_relay = jnp.logical_or(serves[0], serves[1])
    expected = expected + jnp.where(jnp.logical_and(is_relay, jnp.logical_not(owner_follows)), 1, 0)
    for k in (0, 1):
        expected = expected + jnp.where(across_x[k], 1, 0) + jnp.where(leads[k], 1, 0)

        @pl.when(jnp.logical_and(across_x[k], jnp.logical_not(leads[k])))
        def _(k=k):
            pl.semaphore_signal(barrier, inc=1, device_id=far_relay_of(k), device_id_type=MESH)

        @pl.when(serves[k])
        def _(k=k):
            pl.semaphore_signal(barrier, inc=1, device_id=owner[k], device_id_type=MESH)

        @pl.when(jnp.logical_and(serves[k], owner_follows))
        def _(k=k):
            pl.semaphore_signal(barrier, inc=1, device_id=target[k], device_id_type=MESH)


    lane = lax.broadcasted_iota(jnp.int32, (8, 128), 0)
    first, last = lane == 0, lane == 7

    def shift(value, by, low=None, high=None):
        if by == 0:
            return value
        rolled = pltpu.roll(value, 7 if by > 0 else 1, 0)
        fill = high if by > 0 else low
        fill = 0.0 if fill is None else fill
        return jnp.where(last if by > 0 else first, fill, rolled)

    def plane(ref, axis, at, k=None):
        rows = pl.ds(8 * at, 8) if axis == 0 else pl.ds(at, 8, stride=8)
        return ref[rows, :] if k is None else ref[k, rows, :]

    def flow_of(load):
        f = [load(i) for i in range(19)]
        rho = f[0]
        for i in range(1, 19):
            rho = rho + f[i]
        inverse = 1.0 / rho
        u = [total([(velocities[i][a], f[i]) for i in range(19) if velocities[i][a]]) * inverse for a in range(3)]
        return rho, inverse, u

    def make_face(index):
        axis, side = faces[index]
        across = 2 - axis
        edge = 7 if side > 0 else 0
        inner = edge - side
        p_edge = [plane(v_conf, axis, edge, k) for k in range(6)]
        p_inner = [plane(v_conf, axis, inner, k) for k in range(6)]
        s_edge, s_inner = stress_of(p_edge), stress_of(p_inner)
        c_edge, c_inner = plane(v_col, axis, edge), plane(v_col, axis, inner)
        _, inverse, u = flow_of(lambda i: plane(v_pop, axis, edge, i))
        ratio = 0.6875 * inverse
        fluid = jnp.where(plane(v_lab, axis, edge) == 0, 1.0, 0.0)
        out = snd.at[index]
        for k in range(6):
            out[F_CONF + k] = p_edge[k]
        out[F_COL] = c_edge
        for j, i in enumerate(dirs_where(axis, -side)):
            out[F_COT + j] = plane(v_cot, axis, edge, i)
        speed = u[axis] * u[axis] + smooth_square
        speed = speed * lax.rsqrt(speed)
        upwind = 0.25 * (speed - side * u[axis])
        for k in range(6):
            out[F_UPW + k] = upwind * plane(v_con, axis, edge, k)
        values = []
        for i in range(19):
            c = velocities[i]
            if c[axis] == side:
                continue
            got = plane(v_cot, axis, edge if c[axis] == 0 else inner, i)
            values.append((i, in_y(shift(got, c[across]), c[1])))
        zeroth, one, two = moments(values)
        tensor = tensor_of(zeroth, two)
        mobility = 1.0 - c_edge * c_edge
        force = []
        for a in range(3):
            k = slot[a, 1]
            value = 0.5 * (in_y(s_edge[k], 1) - in_y(s_edge[k], -1))
            k = slot[a, across]
            value = value + 0.5 * (shift(s_edge[k], 1) - shift(s_edge[k], -1))
            value = value - (0.5 * side) * s_inner[slot[a, axis]]
            if a == 1:
                slope = 0.5 * (in_y(c_edge, 1) - in_y(c_edge, -1))
            elif a == across:
                slope = 0.5 * (shift(c_edge, 1) - shift(c_edge, -1))
            else:
                slope = (-0.5 * side) * c_inner
            force.append(value + mobility * slope)
        for a in range(3):
            out[F_G + a] = one[a]
            out[F_W + a] = u[a] + ratio * force[a]
        for k in range(6):
            out[F_K + k] = tensor[k]
        out[F_R] = ratio
        out[F_CHI] = fluid

    def make_corner(index):
        cx, cz = corners[index]
        ex, ez = (7 if cx > 0 else 0), (7 if cz > 0 else 0)
        here = pl.ds(8 * ex + ez, 1)
        in_x, in_z = pl.ds(8 * (ex - cx) + ez, 1), pl.ds(8 * ex + ez - cz, 1)
        diagonal = corner_dir(-cx, -cz)

        def put(row, value):
            csnd[index, pl.ds(row, 1), :] = value

        put(C_OWN, v_cot[diagonal, here, :])
        for j, i in enumerate(edge_dirs(2, -cz, 0)):
            put(C_Z + j, v_cot[i, here, :])
        put(C_ZIN, v_cot[diagonal, in_x, :])
        for j, i in enumerate(edge_dirs(0, -cx, 2)):
            put(C_X + j, v_cot[i, here, :])
        put(C_XIN, v_cot[diagonal, in_z, :])
        for k in range(6):
            put(C_CONF + k, v_conf[k, here, :])
        put(C_COL, v_col[here, :])

    face_copies = [
        pltpu.make_async_remote_copy(
            src_ref=snd.at[k], dst_ref=rcv.at[k ^ 1], send_sem=f_send.at[k], recv_sem=f_recv.at[k ^ 1],
            device_id=face_device[k], device_id_type=MESH,
        )
        for k in range(4)
    ]
    corner_copies = [
        pltpu.make_async_remote_copy(
            src_ref=csnd.at[k], dst_ref=crcv.at[3 - k], send_sem=c_send.at[k], recv_sem=c_recv.at[3 - k],
            device_id=corner_device[k], device_id_type=MESH,
        )
        for k in range(4)
    ]
    copies = face_copies + corner_copies
    rest = F_ALL - DIRECT
    direct = [
        pltpu.make_async_remote_copy(
            src_ref=snd.at[k, pl.ds(0, DIRECT)], dst_ref=rcv.at[k ^ 1, pl.ds(0, DIRECT)],
            send_sem=f_send.at[k], recv_sem=f_recv.at[k ^ 1], device_id=face_device[k], device_id_type=MESH,
        )
        for k in (0, 1)
    ]
    to_relay = [
        pltpu.make_async_remote_copy(
            src_ref=snd.at[k, pl.ds(DIRECT, rest)], dst_ref=held, send_sem=r_send, recv_sem=r_recv,
            device_id=relay_of(k), device_id_type=MESH,
        )
        for k in (0, 1)
    ]
    onwards = [
        pltpu.make_async_remote_copy(
            src_ref=held, dst_ref=rcv.at[k ^ 1, pl.ds(DIRECT, rest)], send_sem=h_send, recv_sem=h_recv,
            device_id=target[k], device_id_type=MESH,
        )
        for k in (0, 1)
    ]

    def start(k):
        if k > 1:
            copies[k].start()
            return

        @pl.when(across_x[k])
        def _():
            direct[k].start()

        @pl.when(jnp.logical_not(across_x[k]))
        def _():
            copies[k].start()

    def wait_arrival(k):
        if k > 1:
            arrival[k].wait_recv()
            return

        @pl.when(across_x[k])
        def _():
            direct[flip[k]].wait_recv()
            onwards[flip[k]].wait_recv()

        @pl.when(jnp.logical_not(across_x[k]))
        def _():
            arrival[k].wait_recv()

    def relay(when):
        for k in (0, 1):

            @pl.when(jnp.logical_and(serves[k], when))
            def _(k=k):
                to_relay[k].wait_recv()

        for k in (0, 1):

            @pl.when(jnp.logical_and(serves[k], when))
            def _(k=k):
                if when is owner_follows:
                    pl.semaphore_wait(h_go, 1)
                onwards[k].start()

    arrival = [copies[k] for k in flip]

    def send(ks):
        for k in ks:

            @pl.when(jnp.logical_not(follows[k]))
            def _(k=k):
                start(k)

    def send_later(ks, over_x):
        for k in ks:

            @pl.when(jnp.logical_and(follows[k], jnp.equal(across_x[k], over_x)))
            def _(k=k):
                pl.semaphore_wait(go_sem.at[k], 1)
                start(k)

    for copy in outer:
        copy.wait()
    for index in range(4):
        make_corner(index)
    make_face(0)
    make_face(1)
    pl.semaphore_wait(barrier, expected)
    for k in range(8):

        @pl.when(leads[k])
        def _(k=k):
            pl.semaphore_signal(go_sem.at[flip[k]], inc=1, device_id=devices[k], device_id_type=MESH)

    for k in (0, 1):

        @pl.when(leads[k])
        def _(k=k):
            pl.semaphore_signal(h_go, inc=1, device_id=far_relay_of(k), device_id_type=MESH)

        @pl.when(across_x[k])
        def _(k=k):
            to_relay[k].start()

    send((4, 5, 6, 7, 0, 1))
    relay(jnp.logical_not(owner_follows))
    for copy in middle:
        copy.wait()
    make_face(2)
    make_face(3)
    send((3, 2))

    def local(at, carry):
        rows, padded = pl.ds(pl.multiple_of(8 * at, 8), 8), pl.ds(pl.multiple_of(8 * at + 8, 8), 8)
        p = [v_conf[k, rows, :] for k in range(6)]
        s = stress_of(p)
        for k in range(6):
            x_conf[k, padded, :] = p[k]
            x_str[k, padded, :] = s[k]
        x_col[padded, :] = v_col[rows, :]
        for i in range(19):
            x_cot[i, padded, :] = v_cot[i, rows, :]
        _, inverse, u = flow_of(lambda i: v_pop[i, rows, :])
        for a in range(3):
            v_u[a, rows, :] = u[a]
        v_ri[rows, :] = inverse
        square = u[0] * u[0] + smooth_square
        speed = square * lax.rsqrt(square)
        up, down = 0.25 * (speed - u[0]), 0.25 * (speed + u[0])
        for k in range(6):
            q = v_con[k, rows, :]
            x_up[k, padded, :] = up * q
            x_down[k, padded, :] = down * q
        return carry

    lax.fori_loop(0, 8, local, 0)

    def z_halo():
        for n, (side, index) in enumerate(((-1, 2), (1, 3))):
            got = rcv.at[index]
            for j, i in enumerate(dirs_where(2, side)):
                z_cot[n, j, pl.ds(8, 8), :] = got[F_COT + j]
            s = stress_of([got[F_CONF + k] for k in range(6)])
            for a in range(3):
                z_str[n, a] = s[slot[a, 2]]

    def x_halo(side):
        index = 0 if side < 0 else 1
        rows = pl.ds(0 if side < 0 else 72, 8)
        got = rcv.at[index]
        p = [got[F_CONF + k] for k in range(6)]
        s = stress_of(p)
        for k in range(6):
            x_conf[k, rows, :] = p[k]
            x_str[k, rows, :] = s[k]
            (x_up if side < 0 else x_down)[k, rows, :] = got[F_UPW + k]
        x_col[rows, :] = got[F_COL]
        for j, i in enumerate(dirs_where(0, side)):
            x_cot[i, rows, :] = got[F_COT + j]
        for n, z_side in enumerate((-1, 1)):
            j = dirs_where(2, z_side).index(corner_dir(side, z_side))
            row = crcv[corners.index((side, z_side)), pl.ds(C_OWN, 1), :]
            z_cot[n, j, pl.ds(7 if side < 0 else 16, 1), :] = row

    def halo_force(index, given):
        axis, side = faces[index]
        across = 2 - axis
        edge = 0 if side < 0 else 7
        got = rcv.at[index]

        def corner_at(end):
            place = (side, end) if axis == 0 else (end, side)
            return corners.index(place)

        ends = {-1: first, 1: last}
        fills = {}
        for end in given:
            c = corner_at(end)
            p = [crcv[c, pl.ds(C_CONF + k, 1), :] for k in range(6)]
            s = stress_of(p)
            fills[end] = ([s[slot[a, across]] for a in range(3)], crcv[c, pl.ds(C_COL, 1), :])
        c_halo = got[F_COL]
        mobility = 1.0 - c_halo * c_halo

        def at_ends(pick):
            value = 0.0
            for end in given:
                value = jnp.where(ends[end], rows_of((0.5 * end) * pick(fills[end])), value)
            return value

        p = [plane(v_conf, axis, edge, k) for k in range(6)]
        s = stress_of(p)
        c_edge = plane(v_col, axis, edge)
        force = []
        for a in range(3):
            value = (-0.5 * side) * s[slot[a, axis]]
            if given:
                value = value + at_ends(lambda fill: fill[0][a])
            if a == axis:
                value = value + mobility * ((-0.5 * side) * c_edge)
            elif a == across and given:
                value = value + mobility * at_ends(lambda fill: fill[1])
            force.append(value)
        values = []
        for i in dirs_where(axis, -side):
            c = velocities[i]
            value = plane(v_cot, axis, edge, i)
            if c[across]:
                end = c[across]
                if axis == 0:
                    n = 0 if end < 0 else 1
                    j = dirs_where(2, end).index(i)
                    row = z_cot[n, j, pl.ds(8 + edge, 1), :]
                elif end in given:
                    row = x_cot[i, pl.ds((0 if end < 0 else 72) + edge, 1), :]
                else:
                    row = None
                fill = None if row is None else rows_of(row)
                value = shift(value, end, fill, fill)
            values.append((i, in_y(value, c[1])))
        for end in given:
            c = corner_at(end)
            base = C_Z if axis == 0 else C_X
            for j, i in enumerate(edge_dirs(across, end, axis)):
                row = crcv[c, pl.ds(base + j, 1), :]
                values.append((i, in_y(jnp.where(ends[end], rows_of(row), 0.0), velocities[i][1])))
            i = corner_dir(side, end) if axis == 0 else corner_dir(end, side)
            row = crcv[c, pl.ds(C_ZIN if axis == 0 else C_XIN, 1), :]
            values.append((i, jnp.where(ends[end], rows_of(row), 0.0)))
        zeroth, one, two = moments(values)
        tensor = tensor_of(zeroth, two)
        one = [plus(one[a], got[F_G + a]) for a in range(3)]
        tensor = [plus(tensor[k], got[F_K + k]) for k in range(6)]
        ratio = got[F_R]
        w = [got[F_W + a] + ratio * force[a] for a in range(3)]
        turned = apply(tensor, w)
        return [got[F_CHI] * (3.0 * one[a] + turned[a]) for a in range(3)]

    def put_halo_force(index, given):
        h = halo_force(index, given)
        for a in range(3):
            if index < 2:
                x_h[a, pl.ds(0 if index == 0 else 72, 8), :] = h[a]
            else:
                z_h[index - 2, a] = h[a]

    def main(at, carry):
        def rows(by=0):
            return pl.ds(eights(at + by), 8)

        def padded(by=0):
            return pl.ds(eights(at + by + 1), 8)

        def z_row(ref, n, k):
            return rows_of(ref[n, k, pl.ds(at, 1), :])

        def face_row(index, k):
            return rows_of(rcv[index, k, pl.ds(at, 1), :])

        label = v_lab[rows(), :]
        fluid = jnp.where(label == 0, 1.0, 0.0)
        solid = label == 1
        inverse = v_ri[rows(), :]
        u = [v_u[a, rows(), :] for a in range(3)]
        colour = x_col[padded(), :]
        mobility = 1.0 - colour * colour
        force = []
        for a in range(3):
            k = slot[a, 0]
            value = x_str[k, padded(1), :] - x_str[k, padded(-1), :]
            k = slot[a, 1]
            here = x_str[k, padded(), :]
            value = value + (in_y(here, 1) - in_y(here, -1))
            here = x_str[slot[a, 2], padded(), :]
            value = value + (shift(here, 1, None, z_row(z_str, 1, a)) - shift(here, -1, z_row(z_str, 0, a), None))
            if a == 0:
                slope = x_col[padded(1), :] - x_col[padded(-1), :]
            elif a == 1:
                slope = in_y(colour, 1) - in_y(colour, -1)
            else:
                slope = shift(colour, 1, None, face_row(3, F_COL)) - shift(colour, -1, face_row(2, F_COL), None)
            force.append(0.5 * (value + mobility * slope))
        values = []
        for i in range(19):
            c = velocities[i]
            value = x_cot[i, padded(c[0]), :]
            if c[2]:
                n = 0 if c[2] < 0 else 1
                row = rows_of(z_cot[n, dirs_where(2, c[2]).index(i), pl.ds(8 + at + c[0], 1), :])
                value = shift(value, c[2], row, row)
            values.append((i, in_y(value, c[1])))
        zeroth, one, two = moments(values)
        tensor = tensor_of(zeroth, two)
        v = [u[a] + 0.5 * inverse * force[a] for a in range(3)]
        turned = apply(tensor, v)
        lean = [3.0 * one[a] + turned[a] for a in range(3)]
        energy = zeroth
        for a in range(3):
            energy = energy + v[a] * (3.0 * one[a] + 0.5 * turned[a])
        other = apply(tensor, force)
        h = [fluid * (lean[a] + (0.1875 * inverse) * other[a]) for a in range(3)]
        pull = [fluid * (1.25 * lean[a] + (0.375 * inverse) * other[a]) for a in range(3)]
        for a in range(3):
            x_h[a, padded(), :] = h[a]
        rho_bar = (1.25 * fluid) * energy
        for a in range(3):
            rho_bar = rho_bar - (0.5 * inverse) * (pull[a] * force[a])
        inlet = (
            (1.0 - 1.5 * inlet_speed * inlet_speed) * zeroth
            + (3.0 * inlet_speed) * one[2]
            + (4.5 * inlet_speed * inlet_speed) * two[2]
        )
        rho_bar = rho_bar + jnp.where(label == 2, inlet, 0.0)
        q = [v_con[k, rows(), :] for k in range(6)]
        m_bar = []
        for a in range(3):
            along = bend = None
            for k in range(6):
                here = x_conf[k, padded(), :]
                if a == 0:
                    up, down = x_conf[k, padded(1), :], x_conf[k, padded(-1), :]
                elif a == 1:
                    up, down = in_y(here, 1), in_y(here, -1)
                else:
                    up = shift(here, 1, None, face_row(3, F_CONF + k))
                    down = shift(here, -1, face_row(2, F_CONF + k), None)
                d, c = q[k] * (up - down), q[k] * (up + down - 2.0 * here)
                along, bend = plus(along, d), plus(bend, c)
            square = u[a] * u[a] + smooth_square
            u_bar = (0.25 * u[a] * lax.rsqrt(square)) * bend - 0.25 * along
            m_bar.append(pull[a] + inverse * u_bar)
        for a in range(3):
            rho_bar = rho_bar - m_bar[a] * u[a]
        keep = -0.25 * fluid
        by_dir = dict(values)
        for i in range(19):
            c = velocities[i]
            value = rho_bar + jnp.where(solid, by_dir[opposite[i]], keep * by_dir[i])
            for a in range(3):
                if c[a]:
                    value = value + m_bar[a] if c[a] > 0 else value - m_bar[a]
            o_pop[i, rows(), :] = value
        return carry


    def finish(at, carry):
        def rows(by=0):
            return pl.ds(eights(at + by), 8)

        def padded(by=0):
            return pl.ds(eights(at + by + 1), 8)

        h = [x_h[a, padded(), :] for a in range(3)]
        u = [v_u[a, rows(), :] for a in range(3)]
        colour = x_col[padded(), :]
        mobility = 1.0 - colour * colour
        t = []
        colour_bar = None
        for a in range(3):
            row_down = rows_of(z_h[0, a, pl.ds(at, 1), :])
            row_up = rows_of(z_h[1, a, pl.ds(at, 1), :])
            t.append(
                [
                    x_h[a, padded(-1), :] - x_h[a, padded(1), :],
                    in_y(h[a], -1) - in_y(h[a], 1),
                    shift(h[a], -1, row_down, None) - shift(h[a], 1, None, row_up),
                ]
            )
        def flux(by):
            near = x_col[padded(by), :]
            return (1.0 - near * near) * x_h[0, padded(by), :]

        up_c, down_c = x_col[padded(1), :], x_col[padded(-1), :]
        z_up_c, z_down_c = rows_of(rcv[3, F_COL, pl.ds(at, 1), :]), rows_of(rcv[2, F_COL, pl.ds(at, 1), :])
        slopes = [
            up_c - down_c,
            in_y(colour, 1) - in_y(colour, -1),
            shift(colour, 1, None, z_up_c) - shift(colour, -1, z_down_c, None),
        ]
        colour_bar = h[0] * slopes[0] + h[1] * slopes[1] + h[2] * slopes[2]
        colour_bar = -colour * colour_bar
        in_z = mobility * h[2]
        z_up_f = (1.0 - z_up_c * z_up_c) * rows_of(z_h[1, 2, pl.ds(at, 1), :])
        z_down_f = (1.0 - z_down_c * z_down_c) * rows_of(z_h[0, 2, pl.ds(at, 1), :])
        flow_y = mobility * h[1]
        spread = (
            (flux(-1) - flux(1))
            + (in_y(flow_y, -1) - in_y(flow_y, 1))
            + (shift(in_z, -1, z_down_f, None) - shift(in_z, 1, None, z_up_f))
        )
        o_col[rows(), :] = colour_bar + 0.5 * spread
        w = []
        for a, b in pairs:
            w.append(0.5 * t[a][a] if a == b else 0.25 * (t[a][b] + t[b][a]))
        p = [x_conf[k, padded(), :] for k in range(6)]
        result = []
        for a, b in pairs:
            dot = None
            for m in range(3):
                if a == b:
                    dot = plus(dot, w[slot[a, m]] * p[slot[m, b]])
                else:
                    dot = plus(dot, w[slot[a, m]] * p[slot[m, b]] + p[slot[a, m]] * w[slot[m, b]])
            result.append(w[slot[a, b]] + dot if a == b else 2.0 * w[slot[a, b]] + dot)
        speeds = []
        for a in range(3):
            square = u[a] * u[a] + smooth_square
            speeds.append(square * lax.rsqrt(square))
        stay = 0.9 - 0.5 * (speeds[0] + speeds[1] + speeds[2])
        go_up = [0.25 * (speeds[a] - u[a]) for a in range(3)]
        go_down = [0.25 * (speeds[a] + u[a]) for a in range(3)]
        for k in range(6):
            q = v_con[k, rows(), :]
            value = result[k] + stay * q
            value = value + in_y(go_up[1] * q, -1) + in_y(go_down[1] * q, 1)
            value = value + shift(go_up[2] * q, -1, rows_of(rcv[2, F_UPW + k, pl.ds(at, 1), :]), None)
            value = value + shift(go_down[2] * q, 1, None, rows_of(rcv[3, F_UPW + k, pl.ds(at, 1), :]))
            value = value + x_up[k, padded(-1), :] + x_down[k, padded(1), :]
            o_conf[k, rows(), :] = value
        return carry

    send_later((4, 5, 6, 7, 2, 3), False)
    send_later((0, 1, 4, 5, 6, 7), True)
    relay(owner_follows)
    for k in (2, 3):
        wait_arrival(k)
    z_halo()
    put_halo_force(2, ())
    put_halo_force(3, ())
    lax.fori_loop(1, 7, main, 0)
    lax.fori_loop(2, 6, finish, 0)

    def visit(turn, carry):
        early = jnp.where(place == 0, 1, 0)
        now = jnp.where(turn == 0, early, 1 - early)
        for index, side in enumerate((-1, 1)):

            @pl.when(now == index)
            def _(index=index, side=side):
                for k in (index, 4 + corners.index((side, -1)), 4 + corners.index((side, 1))):
                    wait_arrival(k)
                x_halo(side)
                put_halo_force(index, (-1, 1))
                put_halo_force(2, (side,))
                put_halo_force(3, (side,))
                edge = 0 if side < 0 else 7
                main(edge, 0)
                finish(edge, 0)
                finish(edge - side, 0)

        return carry

    lax.fori_loop(0, 2, visit, 0)
    for copy in copies[2:]:
        copy.wait_send()
    for k in (0, 1):

        @pl.when(across_x[k])
        def _(k=k):
            direct[k].wait_send()
            to_relay[k].wait_send()

        @pl.when(jnp.logical_not(across_x[k]))
        def _(k=k):
            copies[k].wait_send()

        @pl.when(serves[k])
        def _(k=k):
            onwards[k].wait_send()


def deliver(a, b, c, out_a, out_b, out_c, sem):
    copies = [
        pltpu.make_async_copy(src, dst, sem.at[k]) for k, (src, dst) in enumerate(((a, out_a), (b, out_b), (c, out_c)))
    ]
    for copy in copies:
        copy.start()
    for copy in copies:
        copy.wait()


def body(populations, colour, conformation, labels, pop_cotangent, conf_cotangent):
    anywhere = pl.BlockSpec(memory_space=pl.ANY)
    near = pl.BlockSpec(memory_space=pltpu.VMEM)
    args = [
        v.reshape(v.shape[:-3] + (64, 128))
        for v in (populations, colour, conformation, labels, pop_cotangent, conf_cotangent)
    ]
    shapes = [(19, 64, 128), (64, 128), (6, 64, 128)]
    scratch = [pltpu.VMEM(v.shape, v.dtype) for v in args]
    scratch += [pltpu.VMEM((4, F_ALL, 8, 128), F32)] * 2
    scratch += [pltpu.VMEM((4, C_ALL, 128), F32)] * 2
    padded = [(19, 80, 128), (6, 80, 128), (80, 128), (6, 80, 128), (3, 80, 128), (6, 80, 128), (6, 80, 128)]
    scratch += [pltpu.VMEM(s, F32) for s in padded]
    scratch += [pltpu.VMEM(s, F32) for s in [(2, 5, 24, 128), (2, 3, 8, 128), (2, 3, 8, 128), (3, 64, 128), (64, 128)]]
    scratch += [pltpu.VMEM((F_ALL - DIRECT, 8, 128), F32)]
    scratch += [pltpu.SemaphoreType.DMA((3, 6))] + [pltpu.SemaphoreType.DMA((4,))] * 4
    scratch += [pltpu.SemaphoreType.REGULAR((8,))]
    scratch += [pltpu.SemaphoreType.DMA] * 4 + [pltpu.SemaphoreType.REGULAR]
    parts = pl.pallas_call(
        kernel,
        out_shape=tuple(pltpu.VMEM(s, F32) for s in shapes),
        in_specs=[anywhere] * 6,
        out_specs=[near] * 3,
        scratch_shapes=scratch,
        compiler_params=pltpu.CompilerParams(
            collective_id=0, has_side_effects=True, vmem_limit_bytes=32 * 1024 * 1024
        ),
    )(*[pltpu.with_memory_space_constraint(v, pltpu.HBM) for v in args])
    parts = [pltpu.with_memory_space_constraint(v, pltpu.VMEM) for v in parts]
    out = pl.pallas_call(
        deliver,
        out_shape=tuple(jax.ShapeDtypeStruct(s, F32) for s in shapes),
        in_specs=[near] * 3,
        out_specs=[anywhere] * 3,
        scratch_shapes=[pltpu.SemaphoreType.DMA((3,))],
    )(*parts)
    return tuple(v.reshape(v.shape[:-2] + (8, 8, 128)) for v in out)


def solution(mesh):
    placed = (
        P(None, "xy", "gz", None),
        P("xy", "gz", None),
        P(None, "xy", "gz", None),
        P("xy", "gz", None),
        P(None, "xy", "gz", None),
        P(None, "xy", "gz", None),
    )
    return jax.shard_map(
        body,
        mesh=mesh,
        in_specs=placed,
        out_specs=(P(None, "xy", "gz", None), P("xy", "gz", None), P(None, "xy", "gz", None)),
        check_vma=False,
    )
```

```python
import functools

import jax
import jax.numpy as jnp
from jax import lax
from jax.experimental import pallas as pl
from jax.experimental.pallas import tpu as pltpu
from jax.sharding import PartitionSpec as P

MESH = pl.DeviceIdType.MESH
F32 = jnp.float32
MID = (4, 6)
DIRECT = 21

velocities = (
    (0, 0, 0),
    (1, 0, 0),
    (-1, 0, 0),
    (0, 1, 0),
    (0, -1, 0),
    (0, 0, 1),
    (0, 0, -1),
    (1, 1, 0),
    (-1, -1, 0),
    (1, -1, 0),
    (-1, 1, 0),
    (1, 0, 1),
    (-1, 0, -1),
    (1, 0, -1),
    (-1, 0, 1),
    (0, 1, 1),
    (0, -1, -1),
    (0, 1, -1),
    (0, -1, 1),
)
opposite = (0, 2, 1, 4, 3, 6, 5, 8, 7, 10, 9, 12, 11, 14, 13, 16, 15, 18, 17)
slot = {(0, 0): 0, (1, 1): 1, (2, 2): 2, (0, 1): 3, (1, 0): 3, (0, 2): 4, (2, 0): 4, (1, 2): 5, (2, 1): 5}
pairs = ((0, 0), (1, 1), (2, 2), (0, 1), (0, 2), (1, 2))
inlet_speed = 0.05
smooth_square = 0.02 * 0.02
F_CONF, F_COL, F_COT, F_UPW, F_G, F_K, F_W, F_R, F_CHI, F_ALL = 0, 6, 7, 12, 18, 21, 27, 30, 31, 32
C_OWN, C_Z, C_ZIN, C_X, C_XIN, C_CONF, C_COL, C_ALL = 0, 1, 4, 5, 8, 9, 15, 16


def dirs_where(axis, sign):
    return tuple(i for i in range(19) if velocities[i][axis] == sign)


def corner_dir(sx, sz):
    return next(i for i in range(19) if velocities[i][0] == sx and velocities[i][2] == sz)


def edge_dirs(axis, sign, other):
    return tuple(i for i in range(19) if velocities[i][axis] == sign and velocities[i][other] == 0)


def stress_of(conf):
    out = []
    for a, b in pairs:
        dot = conf[slot[a, 0]] * conf[slot[0, b]]
        for m in (1, 2):
            dot = dot + conf[slot[a, m]] * conf[slot[m, b]]
        out.append(conf[slot[a, b]] + 0.5 * dot)
    return out


def total(terms):
    result = None
    for sign, value in terms:
        if result is None:
            result = value if sign > 0 else -value
        else:
            result = result + value if sign > 0 else result - value
    return result


def moments(values):
    def weighted(sign_of):
        axial = total([(sign_of(velocities[i]), v) for i, v in values if 0 < i < 7 and sign_of(velocities[i])])
        edge = total([(sign_of(velocities[i]), v) for i, v in values if i >= 7 and sign_of(velocities[i])])
        if axial is None and edge is None:
            return None
        if axial is None:
            return edge * (1.0 / 36.0)
        if edge is None:
            return axial * (1.0 / 18.0)
        return axial * (1.0 / 18.0) + edge * (1.0 / 36.0)

    zeroth = weighted(lambda c: 1)
    rest = [v for i, v in values if i == 0]
    if rest:
        zeroth = zeroth + rest[0] * (1.0 / 3.0)
    first = [weighted(lambda c, a=a: c[a]) for a in range(3)]
    second = [weighted(lambda c, a=a, b=b: c[a] * c[b]) for a, b in pairs]
    return zeroth, first, second


def tensor_of(zeroth, second):
    out = []
    for k in range(6):
        value = None if second[k] is None else 9.0 * second[k]
        if k < 3:
            value = -3.0 * zeroth if value is None else value - 3.0 * zeroth
        out.append(value)
    return out


def apply(tensor, vector):
    out = []
    for a in range(3):
        value = None
        for b in range(3):
            if tensor[slot[a, b]] is not None:
                term = tensor[slot[a, b]] * vector[b]
                value = term if value is None else value + term
        out.append(value)
    return out


def plus(a, b):
    return a if b is None else b if a is None else a + b


def in_y(value, by):
    return value if by == 0 else pltpu.roll(value, (-by) % 128, 1)


def eights(n):
    return 8 * n if isinstance(n, int) else pl.multiple_of(8 * n, 8)


def rows_of(row):
    return jnp.broadcast_to(row, (8, 128))


def kernel(
    pop, col, conf, lab, cot, con,
    o_pop, o_col, o_conf,
    v_pop, v_col, v_conf, v_lab, v_cot, v_con,
    snd, rcv, csnd, crcv,
    x_cot, x_conf, x_col, x_str, x_h, x_up, x_down, z_cot, z_str, z_h, v_u, v_ri,
    held, in_sem, f_send, f_recv, c_send, c_recv, go_sem, r_send, r_recv, h_send, h_recv, h_go,
):
    fields = [(conf, v_conf), (col, v_col), (cot, v_cot), (pop, v_pop), (lab, v_lab), (con, v_con)]

    def load(group, begin, count):
        rows = pl.ds(begin, count)
        return [
            pltpu.make_async_copy(
                src.at[rows] if len(src.shape) == 2 else src.at[:, rows],
                dst.at[rows] if len(dst.shape) == 2 else dst.at[:, rows],
                in_sem.at[group, k],
            )
            for k, (src, dst) in enumerate(fields)
        ]

    outer = load(0, 0, 16) + load(1, 48, 16)
    middle = load(2, 16, 32)
    for copy in outer + middle:
        copy.start()
    nz, nx = lax.axis_size("gz"), lax.axis_size("xy")
    z, x = lax.axis_index("gz"), lax.axis_index("xy")
    z_of = {-1: lax.rem(z + nz - 1, nz), 0: z, 1: lax.rem(z + 1, nz)}
    x_of = {-1: lax.rem(x + nx - 1, nx), 0: x, 1: lax.rem(x + 1, nx)}
    faces = ((0, -1), (0, 1), (2, -1), (2, 1))
    face_device = [(z_of[0], x_of[-1]), (z_of[0], x_of[1]), (z_of[-1], x_of[0]), (z_of[1], x_of[0])]
    corners = ((-1, -1), (-1, 1), (1, -1), (1, 1))
    corner_device = [(z_of[cz], x_of[cx]) for cx, cz in corners]
    place = lax.rem(x, 8)
    upper = lax.rem(lax.div(x, 8), 2)
    edge_x = {-1: place == 0, 0: False, 1: place == 7}
    edge_z = {-1: z == 0, 0: False, 1: z == nz - 1}
    offsets = [((side, 0) if axis == 0 else (0, side)) for axis, side in faces] + list(corners)
    devices = face_device + corner_device
    flip = (1, 0, 3, 2, 7, 6, 5, 4)
    follows, leads, across_x = [], [], []
    for dx, dz in offsets:
        far_x, far_z = edge_x[dx], edge_z[dz]
        far = jnp.logical_or(far_x, far_z)
        follow = jnp.logical_or(
            jnp.logical_and(far_x, upper == 0),
            jnp.logical_and(jnp.logical_and(far_z, jnp.logical_not(far_x)), z == 0),
        )
        follows.append(follow)
        across_x.append(far_x)
        leads.append(jnp.logical_and(far, jnp.logical_not(follow)))
    barrier = pltpu.get_barrier_semaphore()
    expected = jnp.int32(0)
    for device, follow, lead in zip(devices, follows, leads):
        expected = expected + jnp.where(follow, 0, 1)

        @pl.when(jnp.logical_not(lead))
        def _(device=device):
            pl.semaphore_signal(barrier, inc=1, device_id=device, device_id_type=MESH)

    def along(by):
        return (z, lax.rem(x + by + nx, nx))

    def relay_of(k):
        return along(2 if k == 0 else -2)

    def far_relay_of(k):
        return along(-3 if k == 0 else 3)

    serves = {0: place == 2, 1: place == 5}
    owner = {0: along(-2), 1: along(2)}
    target = {0: along(-3), 1: along(3)}
    owner_follows = upper == 0
    mid = jnp.logical_and(z >= MID[0], z <= MID[1])
    early_relay = jnp.logical_or(jnp.logical_not(owner_follows), mid)
    late_relay = jnp.logical_not(early_relay)
    heard = jnp.where(owner_follows, jnp.where(mid, 2, 0), 1)
    expected = expected + jnp.where(jnp.logical_or(serves[0], serves[1]), heard, 0)
    led_far = [jnp.logical_and(leads[k], jnp.logical_not(mid)) for k in (0, 1)]
    for k in (0, 1):
        expected = expected + jnp.where(across_x[k], 1, 0) + jnp.where(led_far[k], 1, 0)

        @pl.when(jnp.logical_and(across_x[k], jnp.logical_not(led_far[k])))
        def _(k=k):
            pl.semaphore_signal(barrier, inc=1, device_id=far_relay_of(k), device_id_type=MESH)

        @pl.when(jnp.logical_and(follows[k], mid))
        def _(k=k):
            pl.semaphore_signal(barrier, inc=1, device_id=relay_of(k), device_id_type=MESH)

        @pl.when(serves[k])
        def _(k=k):
            pl.semaphore_signal(barrier, inc=1, device_id=owner[k], device_id_type=MESH)

        @pl.when(jnp.logical_and(serves[k], late_relay))
        def _(k=k):
            pl.semaphore_signal(barrier, inc=1, device_id=target[k], device_id_type=MESH)

    lane = lax.broadcasted_iota(jnp.int32, (8, 128), 0)
    first, last = lane == 0, lane == 7

    def shift(value, by, low=None, high=None):
        if by == 0:
            return value
        rolled = pltpu.roll(value, 7 if by > 0 else 1, 0)
        fill = high if by > 0 else low
        fill = 0.0 if fill is None else fill
        return jnp.where(last if by > 0 else first, fill, rolled)

    def plane(ref, axis, at, k=None):
        rows = pl.ds(8 * at, 8) if axis == 0 else pl.ds(at, 8, stride=8)
        return ref[rows, :] if k is None else ref[k, rows, :]

    def flow_of(load):
        f = [load(i) for i in range(19)]
        rho = f[0]
        for i in range(1, 19):
            rho = rho + f[i]
        inverse = 1.0 / rho
        u = [total([(velocities[i][a], f[i]) for i in range(19) if velocities[i][a]]) * inverse for a in range(3)]
        return rho, inverse, u

    def make_face(index):
        axis, side = faces[index]
        across = 2 - axis
        edge = 7 if side > 0 else 0
        inner = edge - side
        p_edge = [plane(v_conf, axis, edge, k) for k in range(6)]
        p_inner = [plane(v_conf, axis, inner, k) for k in range(6)]
        s_edge, s_inner = stress_of(p_edge), stress_of(p_inner)
        c_edge, c_inner = plane(v_col, axis, edge), plane(v_col, axis, inner)
        _, inverse, u = flow_of(lambda i: plane(v_pop, axis, edge, i))
        ratio = 0.6875 * inverse
        fluid = jnp.where(plane(v_lab, axis, edge) == 0, 1.0, 0.0)
        out = snd.at[index]
        for k in range(6):
            out[F_CONF + k] = p_edge[k]
        out[F_COL] = c_edge
        for j, i in enumerate(dirs_where(axis, -side)):
            out[F_COT + j] = plane(v_cot, axis, edge, i)
        speed = u[axis] * u[axis] + smooth_square
        speed = speed * lax.rsqrt(speed)
        upwind = 0.25 * (speed - side * u[axis])
        for k in range(6):
            out[F_UPW + k] = upwind * plane(v_con, axis, edge, k)
        values = []
        for i in range(19):
            c = velocities[i]
            if c[axis] == side:
                continue
            got = plane(v_cot, axis, edge if c[axis] == 0 else inner, i)
            values.append((i, in_y(shift(got, c[across]), c[1])))
        zeroth, one, two = moments(values)
        tensor = tensor_of(zeroth, two)
        mobility = 1.0 - c_edge * c_edge
        force = []
        for a in range(3):
            k = slot[a, 1]
            value = 0.5 * (in_y(s_edge[k], 1) - in_y(s_edge[k], -1))
            k = slot[a, across]
            value = value + 0.5 * (shift(s_edge[k], 1) - shift(s_edge[k], -1))
            value = value - (0.5 * side) * s_inner[slot[a, axis]]
            if a == 1:
                slope = 0.5 * (in_y(c_edge, 1) - in_y(c_edge, -1))
            elif a == across:
                slope = 0.5 * (shift(c_edge, 1) - shift(c_edge, -1))
            else:
                slope = (-0.5 * side) * c_inner
            force.append(value + mobility * slope)
        for a in range(3):
            out[F_G + a] = one[a]
            out[F_W + a] = u[a] + ratio * force[a]
        for k in range(6):
            out[F_K + k] = tensor[k]
        out[F_R] = ratio
        out[F_CHI] = fluid

    def make_corner(index):
        cx, cz = corners[index]
        ex, ez = (7 if cx > 0 else 0), (7 if cz > 0 else 0)
        here = pl.ds(8 * ex + ez, 1)
        in_x, in_z = pl.ds(8 * (ex - cx) + ez, 1), pl.ds(8 * ex + ez - cz, 1)
        diagonal = corner_dir(-cx, -cz)

        def put(row, value):
            csnd[index, pl.ds(row, 1), :] = value

        put(C_OWN, v_cot[diagonal, here, :])
        for j, i in enumerate(edge_dirs(2, -cz, 0)):
            put(C_Z + j, v_cot[i, here, :])
        put(C_ZIN, v_cot[diagonal, in_x, :])
        for j, i in enumerate(edge_dirs(0, -cx, 2)):
            put(C_X + j, v_cot[i, here, :])
        put(C_XIN, v_cot[diagonal, in_z, :])
        for k in range(6):
            put(C_CONF + k, v_conf[k, here, :])
        put(C_COL, v_col[here, :])

    face_copies = [
        pltpu.make_async_remote_copy(
            src_ref=snd.at[k], dst_ref=rcv.at[k ^ 1], send_sem=f_send.at[k], recv_sem=f_recv.at[k ^ 1],
            device_id=face_device[k], device_id_type=MESH,
        )
        for k in range(4)
    ]
    corner_copies = [
        pltpu.make_async_remote_copy(
            src_ref=csnd.at[k], dst_ref=crcv.at[3 - k], send_sem=c_send.at[k], recv_sem=c_recv.at[3 - k],
            device_id=corner_device[k], device_id_type=MESH,
        )
        for k in range(4)
    ]
    copies = face_copies + corner_copies
    rest = F_ALL - DIRECT
    direct = [
        pltpu.make_async_remote_copy(
            src_ref=snd.at[k, pl.ds(0, DIRECT)], dst_ref=rcv.at[k ^ 1, pl.ds(0, DIRECT)],
            send_sem=f_send.at[k], recv_sem=f_recv.at[k ^ 1], device_id=face_device[k], device_id_type=MESH,
        )
        for k in (0, 1)
    ]
    to_relay = [
        pltpu.make_async_remote_copy(
            src_ref=snd.at[k, pl.ds(DIRECT, rest)], dst_ref=held, send_sem=r_send, recv_sem=r_recv,
            device_id=relay_of(k), device_id_type=MESH,
        )
        for k in (0, 1)
    ]
    onwards = [
        pltpu.make_async_remote_copy(
            src_ref=held, dst_ref=rcv.at[k ^ 1, pl.ds(DIRECT, rest)], send_sem=h_send, recv_sem=h_recv,
            device_id=target[k], device_id_type=MESH,
        )
        for k in (0, 1)
    ]

    def start(k):
        if k > 1:
            copies[k].start()
            return

        @pl.when(across_x[k])
        def _():
            direct[k].start()

        @pl.when(jnp.logical_not(across_x[k]))
        def _():
            copies[k].start()

    def wait_arrival(k):
        if k > 1:
            arrival[k].wait_recv()
            return

        @pl.when(across_x[k])
        def _():
            direct[flip[k]].wait_recv()
            onwards[flip[k]].wait_recv()

        @pl.when(jnp.logical_not(across_x[k]))
        def _():
            arrival[k].wait_recv()

    def relay(when):
        for k in (0, 1):

            @pl.when(jnp.logical_and(serves[k], when))
            def _(k=k):
                to_relay[k].wait_recv()

        for k in (0, 1):

            @pl.when(jnp.logical_and(serves[k], when))
            def _(k=k):
                if when is late_relay:
                    pl.semaphore_wait(h_go, 1)
                onwards[k].start()

    arrival = [copies[k] for k in flip]

    def send(ks):
        for k in ks:

            @pl.when(jnp.logical_not(follows[k]))
            def _(k=k):
                start(k)

    def send_later(ks, over_x):
        for k in ks:

            @pl.when(jnp.logical_and(follows[k], jnp.equal(across_x[k], over_x)))
            def _(k=k):
                pl.semaphore_wait(go_sem.at[k], 1)
                start(k)

    for copy in outer:
        copy.wait()
    for index in range(4):
        make_corner(index)
    make_face(0)
    make_face(1)
    pl.semaphore_wait(barrier, expected)
    for k in range(8):

        @pl.when(leads[k] if k > 1 else led_far[k])
        def _(k=k):
            pl.semaphore_signal(go_sem.at[flip[k]], inc=1, device_id=devices[k], device_id_type=MESH)

    for k in (0, 1):

        @pl.when(jnp.logical_and(serves[k], jnp.logical_and(owner_follows, mid)))
        def _(k=k):
            pl.semaphore_signal(go_sem.at[k], inc=1, device_id=owner[k], device_id_type=MESH)

        @pl.when(led_far[k])
        def _(k=k):
            pl.semaphore_signal(h_go, inc=1, device_id=far_relay_of(k), device_id_type=MESH)

        @pl.when(across_x[k])
        def _(k=k):
            to_relay[k].start()

    send((4, 5, 6, 7, 0, 1))
    relay(early_relay)
    for copy in middle:
        copy.wait()
    make_face(2)
    make_face(3)
    send((3, 2))

    def local(at, carry):
        rows, padded = pl.ds(pl.multiple_of(8 * at, 8), 8), pl.ds(pl.multiple_of(8 * at + 8, 8), 8)
        p = [v_conf[k, rows, :] for k in range(6)]
        s = stress_of(p)
        for k in range(6):
            x_conf[k, padded, :] = p[k]
            x_str[k, padded, :] = s[k]
        x_col[padded, :] = v_col[rows, :]
        for i in range(19):
            x_cot[i, padded, :] = v_cot[i, rows, :]
        _, inverse, u = flow_of(lambda i: v_pop[i, rows, :])
        for a in range(3):
            v_u[a, rows, :] = u[a]
        v_ri[rows, :] = inverse
        square = u[0] * u[0] + smooth_square
        speed = square * lax.rsqrt(square)
        up, down = 0.25 * (speed - u[0]), 0.25 * (speed + u[0])
        for k in range(6):
            q = v_con[k, rows, :]
            x_up[k, padded, :] = up * q
            x_down[k, padded, :] = down * q
        return carry

    lax.fori_loop(0, 8, local, 0)

    def z_halo():
        for n, (side, index) in enumerate(((-1, 2), (1, 3))):
            got = rcv.at[index]
            for j, i in enumerate(dirs_where(2, side)):
                z_cot[n, j, pl.ds(8, 8), :] = got[F_COT + j]
            s = stress_of([got[F_CONF + k] for k in range(6)])
            for a in range(3):
                z_str[n, a] = s[slot[a, 2]]

    def x_halo(side):
        index = 0 if side < 0 else 1
        rows = pl.ds(0 if side < 0 else 72, 8)
        got = rcv.at[index]
        p = [got[F_CONF + k] for k in range(6)]
        s = stress_of(p)
        for k in range(6):
            x_conf[k, rows, :] = p[k]
            x_str[k, rows, :] = s[k]
            (x_up if side < 0 else x_down)[k, rows, :] = got[F_UPW + k]
        x_col[rows, :] = got[F_COL]
        for j, i in enumerate(dirs_where(0, side)):
            x_cot[i, rows, :] = got[F_COT + j]
        for n, z_side in enumerate((-1, 1)):
            j = dirs_where(2, z_side).index(corner_dir(side, z_side))
            row = crcv[corners.index((side, z_side)), pl.ds(C_OWN, 1), :]
            z_cot[n, j, pl.ds(7 if side < 0 else 16, 1), :] = row

    def halo_force(index, given):
        axis, side = faces[index]
        across = 2 - axis
        edge = 0 if side < 0 else 7
        got = rcv.at[index]

        def corner_at(end):
            place = (side, end) if axis == 0 else (end, side)
            return corners.index(place)

        ends = {-1: first, 1: last}
        fills = {}
        for end in given:
            c = corner_at(end)
            p = [crcv[c, pl.ds(C_CONF + k, 1), :] for k in range(6)]
            s = stress_of(p)
            fills[end] = ([s[slot[a, across]] for a in range(3)], crcv[c, pl.ds(C_COL, 1), :])
        c_halo = got[F_COL]
        mobility = 1.0 - c_halo * c_halo

        def at_ends(pick):
            value = 0.0
            for end in given:
                value = jnp.where(ends[end], rows_of((0.5 * end) * pick(fills[end])), value)
            return value

        p = [plane(v_conf, axis, edge, k) for k in range(6)]
        s = stress_of(p)
        c_edge = plane(v_col, axis, edge)
        force = []
        for a in range(3):
            value = (-0.5 * side) * s[slot[a, axis]]
            if given:
                value = value + at_ends(lambda fill: fill[0][a])
            if a == axis:
                value = value + mobility * ((-0.5 * side) * c_edge)
            elif a == across and given:
                value = value + mobility * at_ends(lambda fill: fill[1])
            force.append(value)
        values = []
        for i in dirs_where(axis, -side):
            c = velocities[i]
            value = plane(v_cot, axis, edge, i)
            if c[across]:
                end = c[across]
                if axis == 0:
                    n = 0 if end < 0 else 1
                    j = dirs_where(2, end).index(i)
                    row = z_cot[n, j, pl.ds(8 + edge, 1), :]
                elif end in given:
                    row = x_cot[i, pl.ds((0 if end < 0 else 72) + edge, 1), :]
                else:
                    row = None
                fill = None if row is None else rows_of(row)
                value = shift(value, end, fill, fill)
            values.append((i, in_y(value, c[1])))
        for end in given:
            c = corner_at(end)
            base = C_Z if axis == 0 else C_X
            for j, i in enumerate(edge_dirs(across, end, axis)):
                row = crcv[c, pl.ds(base + j, 1), :]
                values.append((i, in_y(jnp.where(ends[end], rows_of(row), 0.0), velocities[i][1])))
            i = corner_dir(side, end) if axis == 0 else corner_dir(end, side)
            row = crcv[c, pl.ds(C_ZIN if axis == 0 else C_XIN, 1), :]
            values.append((i, jnp.where(ends[end], rows_of(row), 0.0)))
        zeroth, one, two = moments(values)
        tensor = tensor_of(zeroth, two)
        one = [plus(one[a], got[F_G + a]) for a in range(3)]
        tensor = [plus(tensor[k], got[F_K + k]) for k in range(6)]
        ratio = got[F_R]
        w = [got[F_W + a] + ratio * force[a] for a in range(3)]
        turned = apply(tensor, w)
        return [got[F_CHI] * (3.0 * one[a] + turned[a]) for a in range(3)]

    def put_halo_force(index, given):
        h = halo_force(index, given)
        for a in range(3):
            if index < 2:
                x_h[a, pl.ds(0 if index == 0 else 72, 8), :] = h[a]
            else:
                z_h[index - 2, a] = h[a]

    def main(at, carry):
        def rows(by=0):
            return pl.ds(eights(at + by), 8)

        def padded(by=0):
            return pl.ds(eights(at + by + 1), 8)

        def z_row(ref, n, k):
            return rows_of(ref[n, k, pl.ds(at, 1), :])

        def face_row(index, k):
            return rows_of(rcv[index, k, pl.ds(at, 1), :])

        label = v_lab[rows(), :]
        fluid = jnp.where(label == 0, 1.0, 0.0)
        solid = label == 1
        inverse = v_ri[rows(), :]
        u = [v_u[a, rows(), :] for a in range(3)]
        colour = x_col[padded(), :]
        mobility = 1.0 - colour * colour
        force = []
        for a in range(3):
            k = slot[a, 0]
            value = x_str[k, padded(1), :] - x_str[k, padded(-1), :]
            k = slot[a, 1]
            here = x_str[k, padded(), :]
            value = value + (in_y(here, 1) - in_y(here, -1))
            here = x_str[slot[a, 2], padded(), :]
            value = value + (shift(here, 1, None, z_row(z_str, 1, a)) - shift(here, -1, z_row(z_str, 0, a), None))
            if a == 0:
                slope = x_col[padded(1), :] - x_col[padded(-1), :]
            elif a == 1:
                slope = in_y(colour, 1) - in_y(colour, -1)
            else:
                slope = shift(colour, 1, None, face_row(3, F_COL)) - shift(colour, -1, face_row(2, F_COL), None)
            force.append(0.5 * (value + mobility * slope))
        values = []
        for i in range(19):
            c = velocities[i]
            value = x_cot[i, padded(c[0]), :]
            if c[2]:
                n = 0 if c[2] < 0 else 1
                row = rows_of(z_cot[n, dirs_where(2, c[2]).index(i), pl.ds(8 + at + c[0], 1), :])
                value = shift(value, c[2], row, row)
            values.append((i, in_y(value, c[1])))
        zeroth, one, two = moments(values)
        tensor = tensor_of(zeroth, two)
        v = [u[a] + 0.5 * inverse * force[a] for a in range(3)]
        turned = apply(tensor, v)
        lean = [3.0 * one[a] + turned[a] for a in range(3)]
        energy = zeroth
        for a in range(3):
            energy = energy + v[a] * (3.0 * one[a] + 0.5 * turned[a])
        other = apply(tensor, force)
        h = [fluid * (lean[a] + (0.1875 * inverse) * other[a]) for a in range(3)]
        pull = [fluid * (1.25 * lean[a] + (0.375 * inverse) * other[a]) for a in range(3)]
        for a in range(3):
            x_h[a, padded(), :] = h[a]
        rho_bar = (1.25 * fluid) * energy
        for a in range(3):
            rho_bar = rho_bar - (0.5 * inverse) * (pull[a] * force[a])
        inlet = (
            (1.0 - 1.5 * inlet_speed * inlet_speed) * zeroth
            + (3.0 * inlet_speed) * one[2]
            + (4.5 * inlet_speed * inlet_speed) * two[2]
        )
        rho_bar = rho_bar + jnp.where(label == 2, inlet, 0.0)
        q = [v_con[k, rows(), :] for k in range(6)]
        m_bar = []
        for a in range(3):
            along = bend = None
            for k in range(6):
                here = x_conf[k, padded(), :]
                if a == 0:
                    up, down = x_conf[k, padded(1), :], x_conf[k, padded(-1), :]
                elif a == 1:
                    up, down = in_y(here, 1), in_y(here, -1)
                else:
                    up = shift(here, 1, None, face_row(3, F_CONF + k))
                    down = shift(here, -1, face_row(2, F_CONF + k), None)
                d, c = q[k] * (up - down), q[k] * (up + down - 2.0 * here)
                along, bend = plus(along, d), plus(bend, c)
            square = u[a] * u[a] + smooth_square
            u_bar = (0.25 * u[a] * lax.rsqrt(square)) * bend - 0.25 * along
            m_bar.append(pull[a] + inverse * u_bar)
        for a in range(3):
            rho_bar = rho_bar - m_bar[a] * u[a]
        keep = -0.25 * fluid
        by_dir = dict(values)
        for i in range(19):
            c = velocities[i]
            value = rho_bar + jnp.where(solid, by_dir[opposite[i]], keep * by_dir[i])
            for a in range(3):
                if c[a]:
                    value = value + m_bar[a] if c[a] > 0 else value - m_bar[a]
            o_pop[i, rows(), :] = value
        return carry


    def finish(at, carry):
        def rows(by=0):
            return pl.ds(eights(at + by), 8)

        def padded(by=0):
            return pl.ds(eights(at + by + 1), 8)

        h = [x_h[a, padded(), :] for a in range(3)]
        u = [v_u[a, rows(), :] for a in range(3)]
        colour = x_col[padded(), :]
        mobility = 1.0 - colour * colour
        t = []
        colour_bar = None
        for a in range(3):
            row_down = rows_of(z_h[0, a, pl.ds(at, 1), :])
            row_up = rows_of(z_h[1, a, pl.ds(at, 1), :])
            t.append(
                [
                    x_h[a, padded(-1), :] - x_h[a, padded(1), :],
                    in_y(h[a], -1) - in_y(h[a], 1),
                    shift(h[a], -1, row_down, None) - shift(h[a], 1, None, row_up),
                ]
            )
        def flux(by):
            near = x_col[padded(by), :]
            return (1.0 - near * near) * x_h[0, padded(by), :]

        up_c, down_c = x_col[padded(1), :], x_col[padded(-1), :]
        z_up_c, z_down_c = rows_of(rcv[3, F_COL, pl.ds(at, 1), :]), rows_of(rcv[2, F_COL, pl.ds(at, 1), :])
        slopes = [
            up_c - down_c,
            in_y(colour, 1) - in_y(colour, -1),
            shift(colour, 1, None, z_up_c) - shift(colour, -1, z_down_c, None),
        ]
        colour_bar = h[0] * slopes[0] + h[1] * slopes[1] + h[2] * slopes[2]
        colour_bar = -colour * colour_bar
        in_z = mobility * h[2]
        z_up_f = (1.0 - z_up_c * z_up_c) * rows_of(z_h[1, 2, pl.ds(at, 1), :])
        z_down_f = (1.0 - z_down_c * z_down_c) * rows_of(z_h[0, 2, pl.ds(at, 1), :])
        flow_y = mobility * h[1]
        spread = (
            (flux(-1) - flux(1))
            + (in_y(flow_y, -1) - in_y(flow_y, 1))
            + (shift(in_z, -1, z_down_f, None) - shift(in_z, 1, None, z_up_f))
        )
        o_col[rows(), :] = colour_bar + 0.5 * spread
        w = []
        for a, b in pairs:
            w.append(0.5 * t[a][a] if a == b else 0.25 * (t[a][b] + t[b][a]))
        p = [x_conf[k, padded(), :] for k in range(6)]
        result = []
        for a, b in pairs:
            dot = None
            for m in range(3):
                if a == b:
                    dot = plus(dot, w[slot[a, m]] * p[slot[m, b]])
                else:
                    dot = plus(dot, w[slot[a, m]] * p[slot[m, b]] + p[slot[a, m]] * w[slot[m, b]])
            result.append(w[slot[a, b]] + dot if a == b else 2.0 * w[slot[a, b]] + dot)
        speeds = []
        for a in range(3):
            square = u[a] * u[a] + smooth_square
            speeds.append(square * lax.rsqrt(square))
        stay = 0.9 - 0.5 * (speeds[0] + speeds[1] + speeds[2])
        go_up = [0.25 * (speeds[a] - u[a]) for a in range(3)]
        go_down = [0.25 * (speeds[a] + u[a]) for a in range(3)]
        for k in range(6):
            q = v_con[k, rows(), :]
            value = result[k] + stay * q
            value = value + in_y(go_up[1] * q, -1) + in_y(go_down[1] * q, 1)
            value = value + shift(go_up[2] * q, -1, rows_of(rcv[2, F_UPW + k, pl.ds(at, 1), :]), None)
            value = value + shift(go_down[2] * q, 1, None, rows_of(rcv[3, F_UPW + k, pl.ds(at, 1), :]))
            value = value + x_up[k, padded(-1), :] + x_down[k, padded(1), :]
            o_conf[k, rows(), :] = value
        return carry

    send_later((4, 5, 6, 7, 2, 3), False)
    send_later((0, 1, 4, 5, 6, 7), True)
    relay(late_relay)
    for k in (2, 3):
        wait_arrival(k)
    z_halo()
    put_halo_force(2, ())
    put_halo_force(3, ())
    lax.fori_loop(1, 7, main, 0)
    lax.fori_loop(2, 6, finish, 0)

    def visit(turn, carry):
        early = jnp.where(place == 0, 1, 0)
        now = jnp.where(turn == 0, early, 1 - early)
        for index, side in enumerate((-1, 1)):

            @pl.when(now == index)
            def _(index=index, side=side):
                for k in (index, 4 + corners.index((side, -1)), 4 + corners.index((side, 1))):
                    wait_arrival(k)
                x_halo(side)
                put_halo_force(index, (-1, 1))
                put_halo_force(2, (side,))
                put_halo_force(3, (side,))
                edge = 0 if side < 0 else 7
                main(edge, 0)
                finish(edge, 0)
                finish(edge - side, 0)

        return carry

    lax.fori_loop(0, 2, visit, 0)
    for copy in copies[2:]:
        copy.wait_send()
    for k in (0, 1):

        @pl.when(across_x[k])
        def _(k=k):
            direct[k].wait_send()
            to_relay[k].wait_send()

        @pl.when(jnp.logical_not(across_x[k]))
        def _(k=k):
            copies[k].wait_send()

        @pl.when(serves[k])
        def _(k=k):
            onwards[k].wait_send()


def deliver(a, b, c, out_a, out_b, out_c, sem):
    copies = [
        pltpu.make_async_copy(src, dst, sem.at[k]) for k, (src, dst) in enumerate(((a, out_a), (b, out_b), (c, out_c)))
    ]
    for copy in copies:
        copy.start()
    for copy in copies:
        copy.wait()


def body(populations, colour, conformation, labels, pop_cotangent, conf_cotangent):
    anywhere = pl.BlockSpec(memory_space=pl.ANY)
    near = pl.BlockSpec(memory_space=pltpu.VMEM)
    args = [
        v.reshape(v.shape[:-3] + (64, 128))
        for v in (populations, colour, conformation, labels, pop_cotangent, conf_cotangent)
    ]
    shapes = [(19, 64, 128), (64, 128), (6, 64, 128)]
    scratch = [pltpu.VMEM(v.shape, v.dtype) for v in args]
    scratch += [pltpu.VMEM((4, F_ALL, 8, 128), F32)] * 2
    scratch += [pltpu.VMEM((4, C_ALL, 128), F32)] * 2
    padded = [(19, 80, 128), (6, 80, 128), (80, 128), (6, 80, 128), (3, 80, 128), (6, 80, 128), (6, 80, 128)]
    scratch += [pltpu.VMEM(s, F32) for s in padded]
    scratch += [pltpu.VMEM(s, F32) for s in [(2, 5, 24, 128), (2, 3, 8, 128), (2, 3, 8, 128), (3, 64, 128), (64, 128)]]
    scratch += [pltpu.VMEM((F_ALL - DIRECT, 8, 128), F32)]
    scratch += [pltpu.SemaphoreType.DMA((3, 6))] + [pltpu.SemaphoreType.DMA((4,))] * 4
    scratch += [pltpu.SemaphoreType.REGULAR((8,))]
    scratch += [pltpu.SemaphoreType.DMA] * 4 + [pltpu.SemaphoreType.REGULAR]
    parts = pl.pallas_call(
        kernel,
        out_shape=tuple(pltpu.VMEM(s, F32) for s in shapes),
        in_specs=[anywhere] * 6,
        out_specs=[near] * 3,
        scratch_shapes=scratch,
        compiler_params=pltpu.CompilerParams(
            collective_id=0, has_side_effects=True, vmem_limit_bytes=32 * 1024 * 1024
        ),
    )(*[pltpu.with_memory_space_constraint(v, pltpu.HBM) for v in args])
    parts = [pltpu.with_memory_space_constraint(v, pltpu.VMEM) for v in parts]
    out = pl.pallas_call(
        deliver,
        out_shape=tuple(jax.ShapeDtypeStruct(s, F32) for s in shapes),
        in_specs=[near] * 3,
        out_specs=[anywhere] * 3,
        scratch_shapes=[pltpu.SemaphoreType.DMA((3,))],
    )(*parts)
    return tuple(v.reshape(v.shape[:-2] + (8, 8, 128)) for v in out)


def solution(mesh):
    placed = (
        P(None, "xy", "gz", None),
        P("xy", "gz", None),
        P(None, "xy", "gz", None),
        P("xy", "gz", None),
        P(None, "xy", "gz", None),
        P(None, "xy", "gz", None),
    )
    return jax.shard_map(
        body,
        mesh=mesh,
        in_specs=placed,
        out_specs=(P(None, "xy", "gz", None), P("xy", "gz", None), P(None, "xy", "gz", None)),
        check_vma=False,
    )
```

```python
import functools

import jax
import jax.numpy as jnp
from jax import lax
from jax.experimental import pallas as pl
from jax.experimental.pallas import tpu as pltpu
from jax.sharding import PartitionSpec as P

MESH = pl.DeviceIdType.MESH
F32 = jnp.float32
MID = (4, 6)
DIRECT = 21

velocities = (
    (0, 0, 0),
    (1, 0, 0),
    (-1, 0, 0),
    (0, 1, 0),
    (0, -1, 0),
    (0, 0, 1),
    (0, 0, -1),
    (1, 1, 0),
    (-1, -1, 0),
    (1, -1, 0),
    (-1, 1, 0),
    (1, 0, 1),
    (-1, 0, -1),
    (1, 0, -1),
    (-1, 0, 1),
    (0, 1, 1),
    (0, -1, -1),
    (0, 1, -1),
    (0, -1, 1),
)
opposite = (0, 2, 1, 4, 3, 6, 5, 8, 7, 10, 9, 12, 11, 14, 13, 16, 15, 18, 17)
slot = {(0, 0): 0, (1, 1): 1, (2, 2): 2, (0, 1): 3, (1, 0): 3, (0, 2): 4, (2, 0): 4, (1, 2): 5, (2, 1): 5}
pairs = ((0, 0), (1, 1), (2, 2), (0, 1), (0, 2), (1, 2))
inlet_speed = 0.05
smooth_square = 0.02 * 0.02
F_CONF, F_COL, F_COT, F_UPW, F_G, F_K, F_W, F_R, F_CHI, F_ALL = 0, 6, 7, 12, 18, 21, 27, 30, 31, 32
C_OWN, C_Z, C_ZIN, C_X, C_XIN, C_CONF, C_COL, C_ALL = 0, 1, 4, 5, 8, 9, 15, 16


def dirs_where(axis, sign):
    return tuple(i for i in range(19) if velocities[i][axis] == sign)


def corner_dir(sx, sz):
    return next(i for i in range(19) if velocities[i][0] == sx and velocities[i][2] == sz)


def edge_dirs(axis, sign, other):
    return tuple(i for i in range(19) if velocities[i][axis] == sign and velocities[i][other] == 0)


def stress_of(conf):
    out = []
    for a, b in pairs:
        dot = conf[slot[a, 0]] * conf[slot[0, b]]
        for m in (1, 2):
            dot = dot + conf[slot[a, m]] * conf[slot[m, b]]
        out.append(conf[slot[a, b]] + 0.5 * dot)
    return out


def total(terms):
    result = None
    for sign, value in terms:
        if result is None:
            result = value if sign > 0 else -value
        else:
            result = result + value if sign > 0 else result - value
    return result


def moments(values):
    def weighted(sign_of):
        axial = total([(sign_of(velocities[i]), v) for i, v in values if 0 < i < 7 and sign_of(velocities[i])])
        edge = total([(sign_of(velocities[i]), v) for i, v in values if i >= 7 and sign_of(velocities[i])])
        if axial is None and edge is None:
            return None
        if axial is None:
            return edge * (1.0 / 36.0)
        if edge is None:
            return axial * (1.0 / 18.0)
        return axial * (1.0 / 18.0) + edge * (1.0 / 36.0)

    zeroth = weighted(lambda c: 1)
    rest = [v for i, v in values if i == 0]
    if rest:
        zeroth = zeroth + rest[0] * (1.0 / 3.0)
    first = [weighted(lambda c, a=a: c[a]) for a in range(3)]
    second = [weighted(lambda c, a=a, b=b: c[a] * c[b]) for a, b in pairs]
    return zeroth, first, second


def tensor_of(zeroth, second):
    out = []
    for k in range(6):
        value = None if second[k] is None else 9.0 * second[k]
        if k < 3:
            value = -3.0 * zeroth if value is None else value - 3.0 * zeroth
        out.append(value)
    return out


def apply(tensor, vector):
    out = []
    for a in range(3):
        value = None
        for b in range(3):
            if tensor[slot[a, b]] is not None:
                term = tensor[slot[a, b]] * vector[b]
                value = term if value is None else value + term
        out.append(value)
    return out


def plus(a, b):
    return a if b is None else b if a is None else a + b


def in_y(value, by):
    return value if by == 0 else pltpu.roll(value, (-by) % 128, 1)


def eights(n):
    return 8 * n if isinstance(n, int) else pl.multiple_of(8 * n, 8)


def rows_of(row):
    return jnp.broadcast_to(row, (8, 128))


def kernel(
    pop, col, conf, lab, cot, con,
    o_pop, o_col, o_conf,
    v_pop, v_col, v_conf, v_lab, v_cot, v_con,
    snd, rcv, csnd, crcv,
    x_cot, x_conf, x_col, x_str, x_h, x_up, x_down, z_cot, z_str, z_h, v_u, v_ri,
    held, in_sem, f_send, f_recv, c_send, c_recv, go_sem, r_send, r_recv, h_send, h_recv, h_go,
):
    fields = [(conf, v_conf), (col, v_col), (cot, v_cot), (pop, v_pop), (lab, v_lab), (con, v_con)]

    def load(group, begin, count):
        rows = pl.ds(begin, count)
        return [
            pltpu.make_async_copy(
                src.at[rows] if len(src.shape) == 2 else src.at[:, rows],
                dst.at[rows] if len(dst.shape) == 2 else dst.at[:, rows],
                in_sem.at[group, k],
            )
            for k, (src, dst) in enumerate(fields)
        ]

    outer = load(0, 0, 16) + load(1, 48, 16)
    middle = load(2, 16, 32)
    for copy in outer + middle:
        copy.start()
    nz, nx = lax.axis_size("gz"), lax.axis_size("xy")
    z, x = lax.axis_index("gz"), lax.axis_index("xy")
    z_of = {-1: lax.rem(z + nz - 1, nz), 0: z, 1: lax.rem(z + 1, nz)}
    x_of = {-1: lax.rem(x + nx - 1, nx), 0: x, 1: lax.rem(x + 1, nx)}
    faces = ((0, -1), (0, 1), (2, -1), (2, 1))
    face_device = [(z_of[0], x_of[-1]), (z_of[0], x_of[1]), (z_of[-1], x_of[0]), (z_of[1], x_of[0])]
    corners = ((-1, -1), (-1, 1), (1, -1), (1, 1))
    corner_device = [(z_of[cz], x_of[cx]) for cx, cz in corners]
    place = lax.rem(x, 8)
    upper = lax.rem(lax.div(x, 8), 2)
    edge_x = {-1: place == 0, 0: False, 1: place == 7}
    edge_z = {-1: z == 0, 0: False, 1: z == nz - 1}
    offsets = [((side, 0) if axis == 0 else (0, side)) for axis, side in faces] + list(corners)
    devices = face_device + corner_device
    flip = (1, 0, 3, 2, 7, 6, 5, 4)
    follows, leads, across_x = [], [], []
    for dx, dz in offsets:
        far_x, far_z = edge_x[dx], edge_z[dz]
        far = jnp.logical_or(far_x, far_z)
        follow = jnp.logical_or(
            jnp.logical_and(far_x, upper == 0),
            jnp.logical_and(jnp.logical_and(far_z, jnp.logical_not(far_x)), z == 0),
        )
        follows.append(follow)
        across_x.append(far_x)
        leads.append(jnp.logical_and(far, jnp.logical_not(follow)))
    barrier = pltpu.get_barrier_semaphore()
    expected = jnp.int32(0)
    for device, follow, lead in zip(devices, follows, leads):
        expected = expected + jnp.where(follow, 0, 1)

        @pl.when(jnp.logical_not(lead))
        def _(device=device):
            pl.semaphore_signal(barrier, inc=1, device_id=device, device_id_type=MESH)

    def along(by):
        return (z, lax.rem(x + by + nx, nx))

    def relay_of(k):
        return along(2 if k == 0 else -2)

    def far_relay_of(k):
        return along(-3 if k == 0 else 3)

    serves = {0: place == 2, 1: place == 5}
    owner = {0: along(-2), 1: along(2)}
    target = {0: along(-3), 1: along(3)}
    owner_follows = upper == 0
    mid = jnp.logical_and(z >= MID[0], z <= MID[1])
    early_relay = jnp.logical_or(jnp.logical_not(owner_follows), mid)
    late_relay = jnp.logical_not(early_relay)
    heard = jnp.where(owner_follows, jnp.where(mid, 2, 0), 1)
    expected = expected + jnp.where(jnp.logical_or(serves[0], serves[1]), heard, 0)
    led_far = [jnp.logical_and(leads[k], jnp.logical_not(mid)) for k in (0, 1)]
    for k in (0, 1):
        expected = expected + jnp.where(across_x[k], 1, 0) + jnp.where(led_far[k], 1, 0)

        @pl.when(jnp.logical_and(across_x[k], jnp.logical_not(led_far[k])))
        def _(k=k):
            pl.semaphore_signal(barrier, inc=1, device_id=far_relay_of(k), device_id_type=MESH)

        @pl.when(jnp.logical_and(follows[k], mid))
        def _(k=k):
            pl.semaphore_signal(barrier, inc=1, device_id=relay_of(k), device_id_type=MESH)

        @pl.when(serves[k])
        def _(k=k):
            pl.semaphore_signal(barrier, inc=1, device_id=owner[k], device_id_type=MESH)

        @pl.when(jnp.logical_and(serves[k], late_relay))
        def _(k=k):
            pl.semaphore_signal(barrier, inc=1, device_id=target[k], device_id_type=MESH)

    lane = lax.broadcasted_iota(jnp.int32, (8, 128), 0)
    first, last = lane == 0, lane == 7

    def shift(value, by, low=None, high=None):
        if by == 0:
            return value
        rolled = pltpu.roll(value, 7 if by > 0 else 1, 0)
        fill = high if by > 0 else low
        fill = 0.0 if fill is None else fill
        return jnp.where(last if by > 0 else first, fill, rolled)

    def plane(ref, axis, at, k=None):
        rows = pl.ds(8 * at, 8) if axis == 0 else pl.ds(at, 8, stride=8)
        return ref[rows, :] if k is None else ref[k, rows, :]

    def flow_of(load):
        f = [load(i) for i in range(19)]
        rho = f[0]
        for i in range(1, 19):
            rho = rho + f[i]
        inverse = 1.0 / rho
        u = [total([(velocities[i][a], f[i]) for i in range(19) if velocities[i][a]]) * inverse for a in range(3)]
        return rho, inverse, u

    def make_face(index):
        axis, side = faces[index]
        across = 2 - axis
        edge = 7 if side > 0 else 0
        inner = edge - side
        p_edge = [plane(v_conf, axis, edge, k) for k in range(6)]
        p_inner = [plane(v_conf, axis, inner, k) for k in range(6)]
        s_edge, s_inner = stress_of(p_edge), stress_of(p_inner)
        c_edge, c_inner = plane(v_col, axis, edge), plane(v_col, axis, inner)
        _, inverse, u = flow_of(lambda i: plane(v_pop, axis, edge, i))
        ratio = 0.6875 * inverse
        fluid = jnp.where(plane(v_lab, axis, edge) == 0, 1.0, 0.0)
        out = snd.at[index]
        for k in range(6):
            out[F_CONF + k] = p_edge[k]
        out[F_COL] = c_edge
        for j, i in enumerate(dirs_where(axis, -side)):
            out[F_COT + j] = plane(v_cot, axis, edge, i)
        speed = u[axis] * u[axis] + smooth_square
        speed = speed * lax.rsqrt(speed)
        upwind = 0.25 * (speed - side * u[axis])
        for k in range(6):
            out[F_UPW + k] = upwind * plane(v_con, axis, edge, k)
        values = []
        for i in range(19):
            c = velocities[i]
            if c[axis] == side:
                continue
            got = plane(v_cot, axis, edge if c[axis] == 0 else inner, i)
            values.append((i, in_y(shift(got, c[across]), c[1])))
        zeroth, one, two = moments(values)
        tensor = tensor_of(zeroth, two)
        mobility = 1.0 - c_edge * c_edge
        force = []
        for a in range(3):
            k = slot[a, 1]
            value = 0.5 * (in_y(s_edge[k], 1) - in_y(s_edge[k], -1))
            k = slot[a, across]
            value = value + 0.5 * (shift(s_edge[k], 1) - shift(s_edge[k], -1))
            value = value - (0.5 * side) * s_inner[slot[a, axis]]
            if a == 1:
                slope = 0.5 * (in_y(c_edge, 1) - in_y(c_edge, -1))
            elif a == across:
                slope = 0.5 * (shift(c_edge, 1) - shift(c_edge, -1))
            else:
                slope = (-0.5 * side) * c_inner
            force.append(value + mobility * slope)
        for a in range(3):
            out[F_G + a] = one[a]
            out[F_W + a] = u[a] + ratio * force[a]
        for k in range(6):
            out[F_K + k] = tensor[k]
        out[F_R] = ratio
        out[F_CHI] = fluid

    def make_corner(index):
        cx, cz = corners[index]
        ex, ez = (7 if cx > 0 else 0), (7 if cz > 0 else 0)
        here = pl.ds(8 * ex + ez, 1)
        in_x, in_z = pl.ds(8 * (ex - cx) + ez, 1), pl.ds(8 * ex + ez - cz, 1)
        diagonal = corner_dir(-cx, -cz)

        def put(row, value):
            csnd[index, pl.ds(row, 1), :] = value

        put(C_OWN, v_cot[diagonal, here, :])
        for j, i in enumerate(edge_dirs(2, -cz, 0)):
            put(C_Z + j, v_cot[i, here, :])
        put(C_ZIN, v_cot[diagonal, in_x, :])
        for j, i in enumerate(edge_dirs(0, -cx, 2)):
            put(C_X + j, v_cot[i, here, :])
        put(C_XIN, v_cot[diagonal, in_z, :])
        for k in range(6):
            put(C_CONF + k, v_conf[k, here, :])
        put(C_COL, v_col[here, :])

    face_copies = [
        pltpu.make_async_remote_copy(
            src_ref=snd.at[k], dst_ref=rcv.at[k ^ 1], send_sem=f_send.at[k], recv_sem=f_recv.at[k ^ 1],
            device_id=face_device[k], device_id_type=MESH,
        )
        for k in range(4)
    ]
    corner_copies = [
        pltpu.make_async_remote_copy(
            src_ref=csnd.at[k], dst_ref=crcv.at[3 - k], send_sem=c_send.at[k], recv_sem=c_recv.at[3 - k],
            device_id=corner_device[k], device_id_type=MESH,
        )
        for k in range(4)
    ]
    copies = face_copies + corner_copies
    rest = F_ALL - DIRECT
    direct = [
        pltpu.make_async_remote_copy(
            src_ref=snd.at[k, pl.ds(0, DIRECT)], dst_ref=rcv.at[k ^ 1, pl.ds(0, DIRECT)],
            send_sem=f_send.at[k], recv_sem=f_recv.at[k ^ 1], device_id=face_device[k], device_id_type=MESH,
        )
        for k in (0, 1)
    ]
    to_relay = [
        pltpu.make_async_remote_copy(
            src_ref=snd.at[k, pl.ds(DIRECT, rest)], dst_ref=held, send_sem=r_send, recv_sem=r_recv,
            device_id=relay_of(k), device_id_type=MESH,
        )
        for k in (0, 1)
    ]
    onwards = [
        pltpu.make_async_remote_copy(
            src_ref=held, dst_ref=rcv.at[k ^ 1, pl.ds(DIRECT, rest)], send_sem=h_send, recv_sem=h_recv,
            device_id=target[k], device_id_type=MESH,
        )
        for k in (0, 1)
    ]

    def start(k):
        if k > 1:
            copies[k].start()
            return

        @pl.when(across_x[k])
        def _():
            direct[k].start()

        @pl.when(jnp.logical_not(across_x[k]))
        def _():
            copies[k].start()

    def wait_arrival(k):
        if k > 1:
            arrival[k].wait_recv()
            return

        @pl.when(across_x[k])
        def _():
            direct[flip[k]].wait_recv()
            onwards[flip[k]].wait_recv()

        @pl.when(jnp.logical_not(across_x[k]))
        def _():
            arrival[k].wait_recv()

    def relay(when):
        for k in (0, 1):

            @pl.when(jnp.logical_and(serves[k], when))
            def _(k=k):
                to_relay[k].wait_recv()

        for k in (0, 1):

            @pl.when(jnp.logical_and(serves[k], when))
            def _(k=k):
                if when is late_relay:
                    pl.semaphore_wait(h_go, 1)
                onwards[k].start()

    arrival = [copies[k] for k in flip]

    def send(ks):
        for k in ks:

            @pl.when(jnp.logical_not(follows[k]))
            def _(k=k):
                start(k)

    def send_later(ks, over_x):
        for k in ks:

            @pl.when(jnp.logical_and(follows[k], jnp.equal(across_x[k], over_x)))
            def _(k=k):
                pl.semaphore_wait(go_sem.at[k], 1)
                start(k)

    for copy in outer:
        copy.wait()
    for index in range(4):
        make_corner(index)
    make_face(0)
    make_face(1)
    pl.semaphore_wait(barrier, expected)
    for k in range(8):

        @pl.when(leads[k] if k > 1 else led_far[k])
        def _(k=k):
            pl.semaphore_signal(go_sem.at[flip[k]], inc=1, device_id=devices[k], device_id_type=MESH)

    for k in (0, 1):

        @pl.when(jnp.logical_and(serves[k], jnp.logical_and(owner_follows, mid)))
        def _(k=k):
            pl.semaphore_signal(go_sem.at[k], inc=1, device_id=owner[k], device_id_type=MESH)

        @pl.when(led_far[k])
        def _(k=k):
            pl.semaphore_signal(h_go, inc=1, device_id=far_relay_of(k), device_id_type=MESH)

        @pl.when(across_x[k])
        def _(k=k):
            to_relay[k].start()

    send((4, 5, 6, 7, 0, 1))
    relay(early_relay)
    for copy in middle:
        copy.wait()
    make_face(2)
    make_face(3)
    send((3, 2))

    def local(at, carry):
        rows, padded = pl.ds(pl.multiple_of(8 * at, 8), 8), pl.ds(pl.multiple_of(8 * at + 8, 8), 8)
        p = [v_conf[k, rows, :] for k in range(6)]
        s = stress_of(p)
        for k in range(6):
            x_conf[k, padded, :] = p[k]
            x_str[k, padded, :] = s[k]
        x_col[padded, :] = v_col[rows, :]
        for i in range(19):
            x_cot[i, padded, :] = v_cot[i, rows, :]
        _, inverse, u = flow_of(lambda i: v_pop[i, rows, :])
        for a in range(3):
            v_u[a, rows, :] = u[a]
        v_ri[rows, :] = inverse
        square = u[0] * u[0] + smooth_square
        speed = square * lax.rsqrt(square)
        up, down = 0.25 * (speed - u[0]), 0.25 * (speed + u[0])
        for k in range(6):
            q = v_con[k, rows, :]
            x_up[k, padded, :] = up * q
            x_down[k, padded, :] = down * q
        return carry

    lax.fori_loop(0, 8, local, 0)

    def z_halo():
        for n, (side, index) in enumerate(((-1, 2), (1, 3))):
            got = rcv.at[index]
            for j, i in enumerate(dirs_where(2, side)):
                z_cot[n, j, pl.ds(8, 8), :] = got[F_COT + j]
            s = stress_of([got[F_CONF + k] for k in range(6)])
            for a in range(3):
                z_str[n, a] = s[slot[a, 2]]

    def x_halo(side):
        index = 0 if side < 0 else 1
        rows = pl.ds(0 if side < 0 else 72, 8)
        got = rcv.at[index]
        p = [got[F_CONF + k] for k in range(6)]
        s = stress_of(p)
        for k in range(6):
            x_conf[k, rows, :] = p[k]
            x_str[k, rows, :] = s[k]
            (x_up if side < 0 else x_down)[k, rows, :] = got[F_UPW + k]
        x_col[rows, :] = got[F_COL]
        for j, i in enumerate(dirs_where(0, side)):
            x_cot[i, rows, :] = got[F_COT + j]
        for n, z_side in enumerate((-1, 1)):
            j = dirs_where(2, z_side).index(corner_dir(side, z_side))
            row = crcv[corners.index((side, z_side)), pl.ds(C_OWN, 1), :]
            z_cot[n, j, pl.ds(7 if side < 0 else 16, 1), :] = row

    def halo_force(index, given):
        axis, side = faces[index]
        across = 2 - axis
        edge = 0 if side < 0 else 7
        got = rcv.at[index]

        def corner_at(end):
            place = (side, end) if axis == 0 else (end, side)
            return corners.index(place)

        ends = {-1: first, 1: last}
        fills = {}
        for end in given:
            c = corner_at(end)
            p = [crcv[c, pl.ds(C_CONF + k, 1), :] for k in range(6)]
            s = stress_of(p)
            fills[end] = ([s[slot[a, across]] for a in range(3)], crcv[c, pl.ds(C_COL, 1), :])
        c_halo = got[F_COL]
        mobility = 1.0 - c_halo * c_halo

        def at_ends(pick):
            value = 0.0
            for end in given:
                value = jnp.where(ends[end], rows_of((0.5 * end) * pick(fills[end])), value)
            return value

        p = [plane(v_conf, axis, edge, k) for k in range(6)]
        s = stress_of(p)
        c_edge = plane(v_col, axis, edge)
        force = []
        for a in range(3):
            value = (-0.5 * side) * s[slot[a, axis]]
            if given:
                value = value + at_ends(lambda fill: fill[0][a])
            if a == axis:
                value = value + mobility * ((-0.5 * side) * c_edge)
            elif a == across and given:
                value = value + mobility * at_ends(lambda fill: fill[1])
            force.append(value)
        values = []
        for i in dirs_where(axis, -side):
            c = velocities[i]
            value = plane(v_cot, axis, edge, i)
            if c[across]:
                end = c[across]
                if axis == 0:
                    n = 0 if end < 0 else 1
                    j = dirs_where(2, end).index(i)
                    row = z_cot[n, j, pl.ds(8 + edge, 1), :]
                elif end in given:
                    row = x_cot[i, pl.ds((0 if end < 0 else 72) + edge, 1), :]
                else:
                    row = None
                fill = None if row is None else rows_of(row)
                value = shift(value, end, fill, fill)
            values.append((i, in_y(value, c[1])))
        for end in given:
            c = corner_at(end)
            base = C_Z if axis == 0 else C_X
            for j, i in enumerate(edge_dirs(across, end, axis)):
                row = crcv[c, pl.ds(base + j, 1), :]
                values.append((i, in_y(jnp.where(ends[end], rows_of(row), 0.0), velocities[i][1])))
            i = corner_dir(side, end) if axis == 0 else corner_dir(end, side)
            row = crcv[c, pl.ds(C_ZIN if axis == 0 else C_XIN, 1), :]
            values.append((i, jnp.where(ends[end], rows_of(row), 0.0)))
        zeroth, one, two = moments(values)
        tensor = tensor_of(zeroth, two)
        one = [plus(one[a], got[F_G + a]) for a in range(3)]
        tensor = [plus(tensor[k], got[F_K + k]) for k in range(6)]
        ratio = got[F_R]
        w = [got[F_W + a] + ratio * force[a] for a in range(3)]
        turned = apply(tensor, w)
        return [got[F_CHI] * (3.0 * one[a] + turned[a]) for a in range(3)]

    def put_halo_force(index, given):
        h = halo_force(index, given)
        for a in range(3):
            if index < 2:
                x_h[a, pl.ds(0 if index == 0 else 72, 8), :] = h[a]
            else:
                z_h[index - 2, a] = h[a]

    def main(at, carry):
        def rows(by=0):
            return pl.ds(eights(at + by), 8)

        def padded(by=0):
            return pl.ds(eights(at + by + 1), 8)

        def z_row(ref, n, k):
            return rows_of(ref[n, k, pl.ds(at, 1), :])

        def face_row(index, k):
            return rows_of(rcv[index, k, pl.ds(at, 1), :])

        label = v_lab[rows(), :]
        fluid = jnp.where(label == 0, 1.0, 0.0)
        solid = label == 1
        inverse = v_ri[rows(), :]
        u = [v_u[a, rows(), :] for a in range(3)]
        colour = x_col[padded(), :]
        mobility = 1.0 - colour * colour
        force = []
        for a in range(3):
            k = slot[a, 0]
            value = x_str[k, padded(1), :] - x_str[k, padded(-1), :]
            k = slot[a, 1]
            here = x_str[k, padded(), :]
            value = value + (in_y(here, 1) - in_y(here, -1))
            here = x_str[slot[a, 2], padded(), :]
            value = value + (shift(here, 1, None, z_row(z_str, 1, a)) - shift(here, -1, z_row(z_str, 0, a), None))
            if a == 0:
                slope = x_col[padded(1), :] - x_col[padded(-1), :]
            elif a == 1:
                slope = in_y(colour, 1) - in_y(colour, -1)
            else:
                slope = shift(colour, 1, None, face_row(3, F_COL)) - shift(colour, -1, face_row(2, F_COL), None)
            force.append(0.5 * (value + mobility * slope))
        values = []
        for i in range(19):
            c = velocities[i]
            value = x_cot[i, padded(c[0]), :]
            if c[2]:
                n = 0 if c[2] < 0 else 1
                row = rows_of(z_cot[n, dirs_where(2, c[2]).index(i), pl.ds(8 + at + c[0], 1), :])
                value = shift(value, c[2], row, row)
            values.append((i, in_y(value, c[1])))
        zeroth, one, two = moments(values)
        tensor = tensor_of(zeroth, two)
        v = [u[a] + 0.5 * inverse * force[a] for a in range(3)]
        turned = apply(tensor, v)
        lean = [3.0 * one[a] + turned[a] for a in range(3)]
        energy = zeroth
        for a in range(3):
            energy = energy + v[a] * (3.0 * one[a] + 0.5 * turned[a])
        other = apply(tensor, force)
        h = [fluid * (lean[a] + (0.1875 * inverse) * other[a]) for a in range(3)]
        pull = [fluid * (1.25 * lean[a] + (0.375 * inverse) * other[a]) for a in range(3)]
        for a in range(3):
            x_h[a, padded(), :] = h[a]
        rho_bar = (1.25 * fluid) * energy
        for a in range(3):
            rho_bar = rho_bar - (0.5 * inverse) * (pull[a] * force[a])
        inlet = (
            (1.0 - 1.5 * inlet_speed * inlet_speed) * zeroth
            + (3.0 * inlet_speed) * one[2]
            + (4.5 * inlet_speed * inlet_speed) * two[2]
        )
        rho_bar = rho_bar + jnp.where(label == 2, inlet, 0.0)
        q = [v_con[k, rows(), :] for k in range(6)]
        m_bar = []
        for a in range(3):
            along = bend = None
            for k in range(6):
                here = x_conf[k, padded(), :]
                if a == 0:
                    up, down = x_conf[k, padded(1), :], x_conf[k, padded(-1), :]
                elif a == 1:
                    up, down = in_y(here, 1), in_y(here, -1)
                else:
                    up = shift(here, 1, None, face_row(3, F_CONF + k))
                    down = shift(here, -1, face_row(2, F_CONF + k), None)
                d, c = q[k] * (up - down), q[k] * (up + down - 2.0 * here)
                along, bend = plus(along, d), plus(bend, c)
            square = u[a] * u[a] + smooth_square
            u_bar = (0.25 * u[a] * lax.rsqrt(square)) * bend - 0.25 * along
            m_bar.append(pull[a] + inverse * u_bar)
        for a in range(3):
            rho_bar = rho_bar - m_bar[a] * u[a]
        keep = -0.25 * fluid
        by_dir = dict(values)
        for i in range(19):
            c = velocities[i]
            value = rho_bar + jnp.where(solid, by_dir[opposite[i]], keep * by_dir[i])
            for a in range(3):
                if c[a]:
                    value = value + m_bar[a] if c[a] > 0 else value - m_bar[a]
            o_pop[i, rows(), :] = value
        return carry


    def finish(at, carry):
        def rows(by=0):
            return pl.ds(eights(at + by), 8)

        def padded(by=0):
            return pl.ds(eights(at + by + 1), 8)

        h = [x_h[a, padded(), :] for a in range(3)]
        u = [v_u[a, rows(), :] for a in range(3)]
        colour = x_col[padded(), :]
        mobility = 1.0 - colour * colour
        t = []
        colour_bar = None
        for a in range(3):
            row_down = rows_of(z_h[0, a, pl.ds(at, 1), :])
            row_up = rows_of(z_h[1, a, pl.ds(at, 1), :])
            t.append(
                [
                    x_h[a, padded(-1), :] - x_h[a, padded(1), :],
                    in_y(h[a], -1) - in_y(h[a], 1),
                    shift(h[a], -1, row_down, None) - shift(h[a], 1, None, row_up),
                ]
            )
        def flux(by):
            near = x_col[padded(by), :]
            return (1.0 - near * near) * x_h[0, padded(by), :]

        up_c, down_c = x_col[padded(1), :], x_col[padded(-1), :]
        z_up_c, z_down_c = rows_of(rcv[3, F_COL, pl.ds(at, 1), :]), rows_of(rcv[2, F_COL, pl.ds(at, 1), :])
        slopes = [
            up_c - down_c,
            in_y(colour, 1) - in_y(colour, -1),
            shift(colour, 1, None, z_up_c) - shift(colour, -1, z_down_c, None),
        ]
        colour_bar = h[0] * slopes[0] + h[1] * slopes[1] + h[2] * slopes[2]
        colour_bar = -colour * colour_bar
        in_z = mobility * h[2]
        z_up_f = (1.0 - z_up_c * z_up_c) * rows_of(z_h[1, 2, pl.ds(at, 1), :])
        z_down_f = (1.0 - z_down_c * z_down_c) * rows_of(z_h[0, 2, pl.ds(at, 1), :])
        flow_y = mobility * h[1]
        spread = (
            (flux(-1) - flux(1))
            + (in_y(flow_y, -1) - in_y(flow_y, 1))
            + (shift(in_z, -1, z_down_f, None) - shift(in_z, 1, None, z_up_f))
        )
        o_col[rows(), :] = colour_bar + 0.5 * spread
        w = []
        for a, b in pairs:
            w.append(0.5 * t[a][a] if a == b else 0.25 * (t[a][b] + t[b][a]))
        p = [x_conf[k, padded(), :] for k in range(6)]
        result = []
        for a, b in pairs:
            dot = None
            for m in range(3):
                if a == b:
                    dot = plus(dot, w[slot[a, m]] * p[slot[m, b]])
                else:
                    dot = plus(dot, w[slot[a, m]] * p[slot[m, b]] + p[slot[a, m]] * w[slot[m, b]])
            result.append(w[slot[a, b]] + dot if a == b else 2.0 * w[slot[a, b]] + dot)
        speeds = []
        for a in range(3):
            square = u[a] * u[a] + smooth_square
            speeds.append(square * lax.rsqrt(square))
        stay = 0.9 - 0.5 * (speeds[0] + speeds[1] + speeds[2])
        go_up = [0.25 * (speeds[a] - u[a]) for a in range(3)]
        go_down = [0.25 * (speeds[a] + u[a]) for a in range(3)]
        for k in range(6):
            q = v_con[k, rows(), :]
            value = result[k] + stay * q
            value = value + in_y(go_up[1] * q, -1) + in_y(go_down[1] * q, 1)
            value = value + shift(go_up[2] * q, -1, rows_of(rcv[2, F_UPW + k, pl.ds(at, 1), :]), None)
            value = value + shift(go_down[2] * q, 1, None, rows_of(rcv[3, F_UPW + k, pl.ds(at, 1), :]))
            value = value + x_up[k, padded(-1), :] + x_down[k, padded(1), :]
            o_conf[k, rows(), :] = value
        return carry

    send_later((4, 5, 6, 7, 2, 3), False)
    send_later((0, 1, 4, 5, 6, 7), True)
    relay(late_relay)
    for k in (2, 3):
        wait_arrival(k)
    z_halo()
    put_halo_force(2, ())
    put_halo_force(3, ())
    lax.fori_loop(1, 7, main, 0)
    lax.fori_loop(2, 6, finish, 0)

    def visit(turn, carry):
        early = jnp.where(place == 0, 1, 0)
        now = jnp.where(turn == 0, early, 1 - early)
        for index, side in enumerate((-1, 1)):

            @pl.when(now == index)
            def _(index=index, side=side):
                for k in (index, 4 + corners.index((side, -1)), 4 + corners.index((side, 1))):
                    wait_arrival(k)
                x_halo(side)
                put_halo_force(index, (-1, 1))
                put_halo_force(2, (side,))
                put_halo_force(3, (side,))
                edge = 0 if side < 0 else 7
                main(edge, 0)
                finish(edge, 0)
                finish(edge - side, 0)

        return carry

    lax.fori_loop(0, 2, visit, 0)
    for copy in copies[2:]:
        copy.wait_send()
    for k in (0, 1):

        @pl.when(across_x[k])
        def _(k=k):
            direct[k].wait_send()
            to_relay[k].wait_send()

        @pl.when(jnp.logical_not(across_x[k]))
        def _(k=k):
            copies[k].wait_send()

        @pl.when(serves[k])
        def _(k=k):
            onwards[k].wait_send()


def deliver(a, b, c, out_a, out_b, out_c, sem):
    copies = [
        pltpu.make_async_copy(src, dst, sem.at[k]) for k, (src, dst) in enumerate(((a, out_a), (b, out_b), (c, out_c)))
    ]
    for copy in copies:
        copy.start()
    for copy in copies:
        copy.wait()


def body(populations, colour, conformation, labels, pop_cotangent, conf_cotangent):
    anywhere = pl.BlockSpec(memory_space=pl.ANY)
    near = pl.BlockSpec(memory_space=pltpu.VMEM)
    args = [
        v.reshape(v.shape[:-3] + (64, 128))
        for v in (populations, colour, conformation, labels, pop_cotangent, conf_cotangent)
    ]
    shapes = [(19, 64, 128), (64, 128), (6, 64, 128)]
    scratch = [pltpu.VMEM(v.shape[:-2] + (72, 128), v.dtype) for v in args]
    scratch += [pltpu.VMEM((4, F_ALL, 8, 128), F32)] * 2
    scratch += [pltpu.VMEM((4, C_ALL, 128), F32)] * 2
    padded = [(19, 80, 128), (6, 80, 128), (80, 128), (6, 80, 128), (3, 80, 128), (6, 80, 128), (6, 80, 128)]
    scratch += [pltpu.VMEM(s, F32) for s in padded]
    scratch += [pltpu.VMEM(s, F32) for s in [(2, 5, 24, 128), (2, 3, 8, 128), (2, 3, 8, 128), (3, 64, 128), (64, 128)]]
    scratch += [pltpu.VMEM((F_ALL - DIRECT, 8, 128), F32)]
    scratch += [pltpu.SemaphoreType.DMA((3, 6))] + [pltpu.SemaphoreType.DMA((4,))] * 4
    scratch += [pltpu.SemaphoreType.REGULAR((8,))]
    scratch += [pltpu.SemaphoreType.DMA] * 4 + [pltpu.SemaphoreType.REGULAR]
    parts = pl.pallas_call(
        kernel,
        out_shape=tuple(pltpu.VMEM(s, F32) for s in shapes),
        in_specs=[anywhere] * 6,
        out_specs=[near] * 3,
        scratch_shapes=scratch,
        compiler_params=pltpu.CompilerParams(
            collective_id=0, has_side_effects=True, vmem_limit_bytes=32 * 1024 * 1024
        ),
    )(*[pltpu.with_memory_space_constraint(v, pltpu.HBM) for v in args])
    parts = [pltpu.with_memory_space_constraint(v, pltpu.VMEM) for v in parts]
    out = pl.pallas_call(
        deliver,
        out_shape=tuple(jax.ShapeDtypeStruct(s, F32) for s in shapes),
        in_specs=[near] * 3,
        out_specs=[anywhere] * 3,
        scratch_shapes=[pltpu.SemaphoreType.DMA((3,))],
    )(*parts)
    return tuple(v.reshape(v.shape[:-2] + (8, 8, 128)) for v in out)


def solution(mesh):
    placed = (
        P(None, "xy", "gz", None),
        P("xy", "gz", None),
        P(None, "xy", "gz", None),
        P("xy", "gz", None),
        P(None, "xy", "gz", None),
        P(None, "xy", "gz", None),
    )
    return jax.shard_map(
        body,
        mesh=mesh,
        in_specs=placed,
        out_specs=(P(None, "xy", "gz", None), P("xy", "gz", None), P(None, "xy", "gz", None)),
        check_vma=False,
    )
```
